1024 devices in a mesh: grp: 16 (over y, core), dom: 64 (over z, x).
Axes of the slice: x: 4, y: 8, z: 16, core: 2. Of those that a mesh axis runs over, the one named last changes fastest.
Arguments:
- x_edges: float32 [2, 1572864], P(None, ('grp', 'dom')), may hold values from -6 to 6
- x_inner: float32 [2, 1048576], P(None, ('grp', 'dom')), may hold values from -6 to 6
- b_edges: float32 [2, 1572864], P(None, ('grp', 'dom')), may hold values from -6 to 6
- b_inner: float32 [2, 1048576], P(None, ('grp', 'dom')), may hold values from -6 to 6
- w_edges: float32 [2, 1572864], P(None, ('grp', 'dom')), may hold values from 0.05 to 0.3
- w_inner: float32 [2, 1048576], P(None, ('grp', 'dom')), may hold values from 0.05 to 0.3
- elem_edges: int32 [3, 1048576], P(None, ('grp', 'dom')), may hold values from 0 to 3199
- element_live: int32 [1048576], P(('grp', 'dom')), may hold values 0 or 1
- elem_matrix: float32 [8, 8, 1048576], P(None, None, ('grp', 'dom')), may hold values from -3.36 to 6, as said below
- projection: float32 [8, 6, 1048576], P(None, None, ('grp', 'dom')), may hold values from -2.5 to 2.5
- owner_counts: int32 [1024, 64], P(('grp', 'dom')), may hold values from 1 to 96, 3072 in all within a row
- aux_node: int32 [6291456], P(('grp', 'dom')), may hold values from 0 to 255
- aux_inverse: float32 [4096, 128, 128], P(('grp', 'dom')), may hold values from -0.22627416997969518 to 3, as said below
Outputs:
- x1_edges: float32 [2, 1572864], P(None, ('grp', 'dom'))
- x1_inner: float32 [2, 1048576], P(None, ('grp', 'dom'))
- r1_edges: float32 [2, 1572864], P(None, ('grp', 'dom'))
- r1_inner: float32 [2, 1048576], P(None, ('grp', 'dom'))
The draws below stay inside these ranges and needn't reach their ends.
Inputs may be any that keep to these rules, and one draw needn't show every extreme that they name: `owner_counts`: every row sums to 3072. `elem_matrix`: symmetric in the first two dimensions. `aux_inverse`: symmetric in the last two dimensions.
All inputs are finite; a program needn't handle non-finite values. No bound on the sum of `element_live` on one device may be relied on, other than what follows from the above.
Results may differ from the reference program's by a relative error of at most 0.0003.
Values sent between devices are 32-bit elements; how exact they have to be, the bound alone decides.
No kernel may reach another device: no remote copies, remote signals or barrier semaphores. Data moves between devices by JAX's collectives and lax.ppermute only.
A program may use at most 32 MiB of HBM per device.

```python
import math
import jax
import jax.numpy as jnp
import numpy as np
from jax import lax

E_DEV = 1024
AGG = 64
NE_DEV = 1536
RIM = 32
AUX_DEV = 256
NAGG = 4
CAP = 96
SLOTS = 6144
E_ALL = 1048576
NE_ALL = 1572864
N_GRP = 16
N_DOM = 64
DEVICES = 1024


def build_block(diag, off, size):
    eye = jnp.eye(size, dtype=jnp.float32)
    return diag * eye + off * (1.0 - eye)


def draw_elem_matrix(key, part):
    key = jax.random.fold_in(key, 11)
    key_diag, key_off, key_scale = jax.random.split(key, 3)
    diag = jnp.exp(jax.random.uniform(key_diag, (8, 1, E_ALL), jnp.float32, 0.0, math.log(3.0)))
    raw = jnp.clip(jax.random.normal(key_off, (8, 8, E_ALL), jnp.float32), -4.0, 4.0)
    off = (raw + jnp.transpose(raw, (1, 0, 2))) * 0.21
    scale = jnp.exp(jax.random.uniform(key_scale, (1, 1, E_ALL), jnp.float32, math.log(0.5), math.log(2.0)))
    eye = jnp.eye(8, dtype=jnp.float32)[:, :, None]
    return scale * (diag * eye + off * (1.0 - eye))


def draw_aux_inverse(key, part):
    key = jax.random.fold_in(key, 23)
    key_diag, key_off = jax.random.split(key)
    size = 2 * AGG
    count = DEVICES * NAGG
    diag = jnp.exp(jax.random.uniform(key_diag, (count, size, 1), jnp.float32, math.log(1.2), math.log(3.0)))
    raw = jnp.clip(jax.random.normal(key_off, (count, size, size), jnp.float32), -4.0, 4.0)
    off = (raw + jnp.transpose(raw, (0, 2, 1))) * (0.32 / math.sqrt(size))
    return build_block(diag, off, size)


def with_ends(result, stream_key, low, largest):
    dims = result.shape
    place = [jax.random.randint(jax.random.fold_in(stream_key, axis), (), 0, dims[axis]) for axis in range(len(dims))]
    result = result.at[tuple(place)].set(low)
    longest = dims.index(max(dims))
    place[longest] = (place[longest] + 1) % dims[longest]
    return result.at[tuple(place)].set(largest)


def shard_levels(key, extent, pieces, smallest, largest):
    factor_of = 1.0
    for axis_at, shards_of in pieces:
        draws = jax.random.uniform(jax.random.fold_in(jax.random.fold_in(key, 6), axis_at), (shards_of,), jnp.float32, smallest / len(pieces), largest / len(pieces))
        factor_of = factor_of * jnp.repeat(jnp.exp(draws), extent[axis_at] // shards_of).reshape((-1,) + (1,) * (len(extent) - 1 - axis_at))
    return factor_of


def split_up(number_of, total, most, skew):
    weights = [(1 << 20) // math.isqrt(standing ** skew) + 1 for standing in range(2, number_of + 1)]
    rest, counts = total - most - (number_of - 1), [1] * (number_of - 1)
    while rest > 0:
        movable = [i for i in range(number_of - 1) if counts[i] < most]
        whole, left = sum([weights[i] for i in movable]), rest
        for i in movable:
            more = min(most - counts[i], max(1, left * weights[i] // whole), rest)
            counts[i] = counts[i] + more
            rest = rest - more
    return np.array([most] + counts)


def uneven_parts(own_key, amount, total, most, skew):
    if amount == 2:
        one = jax.random.randint(own_key, (), max(1, total - most), min(most, total - 1) + 1)
        return jnp.stack([one, total - one])
    lengths = jnp.asarray(split_up(amount, total, most, skew), jnp.int32)
    couples = (amount - 1) // 2
    donor, taker = lengths[1:1 + 2 * couples:2], lengths[2:2 + 2 * couples:2]
    room = jnp.minimum(donor - 1, most - taker)
    moved = jax.random.randint(jax.random.fold_in(own_key, 1), (couples,), 0, 1 << 20) % (room + 1)
    lengths = lengths.at[1:1 + 2 * couples:2].set(donor - moved).at[2:2 + 2 * couples:2].set(taker + moved)
    return lengths[jax.random.permutation(jax.random.fold_in(own_key, 2), amount)]


def scatter_about(key, extent, width, most, shards=(), held_as=jnp.bfloat16):
    entries = jax.random.normal(key, extent, jnp.float32) * width
    if len(shards) > 0:
        entries = shard_levels(key, extent, shards, -0.22, 0.18) * entries
    return jnp.clip(entries, min=-most, max=most).astype(held_as)


def setup_inputs(seed: int = 0) -> dict:
    splits = jax.random.split(jax.random.key(seed), 14)
    x_edges = scatter_about(splits[0], (2, NE_ALL), 1.0, 6.0, ((1, 1024),), jnp.float32)
    x_inner = scatter_about(splits[1], (2, E_ALL), 1.0, 6.0, ((1, 1024),), jnp.float32)
    b_edges = scatter_about(splits[2], (2, NE_ALL), 1.0, 6.0, ((1, 1024),), jnp.float32)
    b_inner = scatter_about(splits[3], (2, E_ALL), 1.0, 6.0, ((1, 1024),), jnp.float32)
    w_edges = jnp.clip(jnp.exp(math.log(0.3) - 1.7917595 * jax.random.uniform(splits[4], (2, NE_ALL), jnp.float32) ** shard_levels(splits[4], (2, NE_ALL), ((1, 1024),), -0.2, 0.2)), 0.05, 0.3)
    w_inner = jnp.clip(jnp.exp(math.log(0.3) - 1.7917595 * jax.random.uniform(splits[5], (2, E_ALL), jnp.float32) ** shard_levels(splits[5], (2, E_ALL), ((1, 1024),), -0.2, 0.2)), 0.05, 0.3)
    elem_edges = with_ends(jax.random.randint(splits[6], (3, E_ALL), 0, 2 * (NE_DEV + 2 * RIM)), jax.random.fold_in(splits[6], 1), 0, (2 * (NE_DEV + 2 * RIM)) - 1).astype(jnp.int32)
    element_live = with_ends((jax.random.randint(splits[7], (E_ALL,), 0, 8) < 7).astype(jnp.int32), jax.random.fold_in(splits[7], 1), 0, 1)
    elem_matrix = draw_elem_matrix(jax.random.fold_in(splits[13], 71), 0)
    projection = scatter_about(splits[9], (8, 6, E_ALL), 6 ** -0.5, 2.5, ((2, 1024),), jnp.float32)
    owner_counts = jax.vmap(lambda own: uneven_parts(own, N_DOM, 3 * E_DEV, CAP, 2))(jax.random.split(splits[10], DEVICES)).reshape((DEVICES, N_DOM)).astype(jnp.int32)
    aux_node = with_ends(jax.random.randint(splits[11], (DEVICES * SLOTS,), 0, AUX_DEV), jax.random.fold_in(splits[11], 1), 0, AUX_DEV - 1).astype(jnp.int32)
    aux_inverse = draw_aux_inverse(jax.random.fold_in(splits[13], 71), 0)
    return dict(x_edges=x_edges, x_inner=x_inner, b_edges=b_edges, b_inner=b_inner, w_edges=w_edges, w_inner=w_inner, elem_edges=elem_edges, element_live=element_live, elem_matrix=elem_matrix, projection=projection, owner_counts=owner_counts, aux_node=aux_node, aux_inverse=aux_inverse)


def edge_map(elem_edges):
    elem_dev = (jnp.arange(E_ALL, dtype=jnp.int32) // E_DEV)[None, :]
    glob = elem_dev * NE_DEV + elem_edges // 2 - RIM
    valid = (glob >= 0) & (glob < NE_ALL)
    index = jnp.clip(glob, 0, NE_ALL - 1).astype(jnp.int32)
    flip = (1 - 2 * (elem_edges % 2)).astype(jnp.float32)
    first = jnp.where(valid, flip, jnp.zeros_like(flip))
    second = jnp.where(valid, jnp.ones_like(flip), jnp.zeros_like(flip))
    return index, jnp.stack([first, second], 1)


def to_elements(edges, inner, index, signs):
    picked = jnp.transpose(edges[:, index], (1, 0, 2)) * signs
    return jnp.concatenate([picked.reshape(6, -1), inner], 0)


def to_edges(values, index, signs):
    parts = values[:6].reshape(3, 2, -1) * signs
    total = jnp.zeros((2, NE_ALL), jnp.float32)
    return total.at[:, index].add(jnp.transpose(parts, (1, 0, 2))), values[6:8]


def apply_matrix(elem_matrix, live, edges, inner, index, signs):
    u = to_elements(edges, inner, index, signs)
    y = live * jnp.sum(elem_matrix * u[None, :, :], axis=1)
    return to_edges(y, index, signs)


def reference(x_edges, x_inner, b_edges, b_inner, w_edges, w_inner, elem_edges, element_live, elem_matrix, projection, owner_counts, aux_node, aux_inverse):
    index, signs = edge_map(elem_edges)
    live = element_live.astype(jnp.float32)[None, :]
    y_edges, y_inner = apply_matrix(elem_matrix, live, x_edges, x_inner, index, signs)
    r_edges = b_edges - y_edges
    r_inner = b_inner - y_inner
    s_edges = w_edges * r_edges
    s_inner = w_inner * r_inner
    u = to_elements(r_edges, r_inner, index, signs)
    a = live * jnp.sum(projection * u[:, None, :], axis=0)
    vals = jnp.transpose(a.reshape(3, 2, DEVICES, E_DEV), (2, 1, 0, 3)).reshape(DEVICES, 2, 3 * E_DEV)
    ends = jnp.cumsum(owner_counts, axis=1).astype(jnp.int32)
    starts = (ends - owner_counts).astype(jnp.int32)
    slot = jnp.arange(CAP, dtype=jnp.int32)
    jidx = starts[:, :, None] + slot[None, None, :]
    filled = slot[None, None, :] < owner_counts[:, :, None]
    jidx = jnp.clip(jidx, 0, 3 * E_DEV - 1).reshape(DEVICES, 1, SLOTS)
    packed = jnp.take_along_axis(vals, jidx, axis=2)
    packed = jnp.where(filled.reshape(DEVICES, 1, SLOTS), packed, jnp.zeros_like(packed))
    moved = jnp.transpose(packed.reshape(N_GRP, N_DOM, 2, N_DOM, CAP), (0, 3, 2, 1, 4)).reshape(DEVICES, 2, SLOTS)
    nodes = aux_node.reshape(DEVICES, SLOTS)

    def gather_node(arrived, node):
        return jnp.zeros((2, AUX_DEV), jnp.float32).at[:, node].add(arrived)

    g = jax.vmap(gather_node)(moved, nodes)
    gb = jnp.transpose(g.reshape(DEVICES, 2, NAGG, AGG), (0, 2, 1, 3)).reshape(DEVICES * NAGG, 2 * AGG)
    h = jnp.einsum("bij,bj->bi", aux_inverse, gb, precision=lax.Precision.HIGHEST)
    h = jnp.transpose(h.reshape(DEVICES, NAGG, 2, AGG), (0, 2, 1, 3)).reshape(DEVICES, 2, AUX_DEV)
    outgoing = jnp.take_along_axis(h, nodes[:, None, :], axis=2)
    back = jnp.transpose(outgoing.reshape(N_GRP, N_DOM, 2, N_DOM, CAP), (0, 3, 2, 1, 4)).reshape(DEVICES, 2, SLOTS)
    entry = jnp.arange(3 * E_DEV, dtype=jnp.int32)
    owner = jax.vmap(lambda e: jnp.searchsorted(e, entry, side="right"))(ends).astype(jnp.int32)
    first_of = jnp.take_along_axis(starts, owner, axis=1)
    flat = (owner * CAP + entry[None, :] - first_of).astype(jnp.int32)
    vals_back = jnp.take_along_axis(back, flat[:, None, :], axis=2)
    h_e = jnp.transpose(vals_back.reshape(DEVICES, 2, 3, E_DEV), (2, 1, 0, 3)).reshape(6, E_ALL)
    p_e = live * jnp.sum(projection * h_e[None, :, :], axis=1)
    p_edges, p_inner = to_edges(p_e, index, signs)
    z_edges = s_edges + p_edges
    z_inner = s_inner + p_inner
    az_edges, az_inner = apply_matrix(elem_matrix, live, z_edges, z_inner, index, signs)
    return x_edges + z_edges, x_inner + z_inner, r_edges - az_edges, r_inner - az_inner
```

```python
import functools

import jax
import jax.numpy as jnp
from jax import lax
from jax.experimental import pallas as pl
from jax.experimental.pallas import tpu as pltpu
from jax.sharding import PartitionSpec as P

LANES = 128
VMEM_LIMIT = 24 * 2**20


def iota(shape, dim):
    return lax.broadcasted_iota(jnp.int32, shape, dim)


def edge_places(edges_ref, rim, width):
    places = []
    for k in range(3):
        coded = edges_ref[k : k + 1, :]
        flip = (1 - 2 * (coded & 1)).astype(jnp.float32)
        place = (coded >> 1) - rim
        place = jnp.where(place < 0, place + width, place)
        places.append((place >> 7, place & (LANES - 1), flip))
    return places


def gather_moments(table, inner, places):
    count = inner.shape[1]
    row = iota((8, LANES), 0)
    wide = iota((8, count), 0)
    total = jnp.concatenate([jnp.zeros((6, count), jnp.float32), inner], 0)
    for k, (high, low, flip) in enumerate(places):
        columns = []
        for at in range(0, count, LANES):
            low_b = jnp.broadcast_to(low[:, at : at + LANES], (8, LANES))
            high_b = jnp.broadcast_to(high[:, at : at + LANES], (8, LANES))
            found = jnp.zeros((8, LANES), jnp.float32)
            for g in range(table.shape[0] // 8):
                picked = jnp.take_along_axis(table[8 * g : 8 * g + 8], low_b, axis=1)
                found = found + jnp.where(high_b == 4 * g + (row >> 1), picked, 0.0)
            found = found + pltpu.roll(found, 4, 0)
            columns.append(found + pltpu.roll(found, 2, 0))
        found = jnp.concatenate(columns, 1)
        found = found * jnp.where(wide == 2 * k, flip, 1.0)
        total = jnp.where((wide >> 1) == k, found, total)
    return total


def scatter_moments(values, places, rows):
    count = values.shape[1]
    wide = iota((8, count), 0)
    tall = iota((LANES, count), 0)
    total = jnp.zeros((2 * rows, LANES), jnp.float32)
    for k, (high, low, flip) in enumerate(places):
        part = jnp.where((wide >> 1) == k, values, 0.0)
        part = part * jnp.where(wide == 2 * k, flip, 1.0)
        part = part + pltpu.roll(part, 4, 0)
        part = part + pltpu.roll(part, 2, 0)
        coarse = part.astype(jnp.bfloat16).astype(jnp.float32)
        spread = []
        for piece in (coarse, part - coarse):
            for g in range(rows // 8):
                spread.append(jnp.where(high == 4 * g + (wide >> 1), piece, 0.0))
        spread = jnp.concatenate(spread, 0).astype(jnp.bfloat16)
        hot = jnp.where(tall == low, 1.0, 0.0).astype(jnp.bfloat16)
        total = total + lax.dot_general(
            spread, hot, (((1,), (1,)), ((), ())), preferred_element_type=jnp.float32
        )
    return total[:rows] + total[rows:]


def apply_matrix(matrix_ref, live, u):
    y = matrix_ref[0] * u[0:1]
    for j in range(1, 8):
        y = y + matrix_ref[j] * u[j : j + 1]
    return y * live


def rim_row(from_left, from_right, rim):
    lane = iota(from_left.shape, 1)
    low = jnp.where(lane < rim, from_right, 0.0)
    return jnp.where((lane >= rim) & (lane < 2 * rim), pltpu.roll(from_left, 64, 1), low)


def settle(partial, last, from_left, from_right, rim):
    lane = iota((2, LANES), 1)
    head = partial[0:2] + jnp.where(lane < rim, from_left[2:4], 0.0)
    tail = partial[last : last + 2] + jnp.where(
        lane >= LANES - rim, pltpu.roll(from_right[2:4], 64, 1), 0.0
    )
    ends = partial[last + 2 : last + 4] + rim_row(from_left[0:2], from_right[0:2], rim)
    return head, tail, ends


def load_table(table_ref, edges, ends):
    blocks = edges.shape[1] // LANES
    for h in range(blocks):
        table_ref[2 * h : 2 * h + 2, :] = edges[:, h * LANES : (h + 1) * LANES]
    table_ref[2 * blocks : 2 * blocks + 2, :] = ends
    rest = table_ref.shape[0] - 2 * blocks - 2
    table_ref[2 * blocks + 2 :, :] = jnp.zeros((rest, LANES), jnp.float32)


def residual_kernel(
    rim, x_ref, inner_ref, left_ref, right_ref, edges_ref, live_ref, matrix_ref,
    y_ref, y_inner_ref, to_left_ref, to_right_ref, table_ref,
):
    rows = table_ref.shape[0]
    edge_count = x_ref.shape[1]
    last = 2 * (edge_count // LANES) - 2
    load_table(table_ref, x_ref[...], rim_row(left_ref[0:2], right_ref[0:2], rim))
    places = edge_places(edges_ref, rim, edge_count + 2 * rim)
    live = live_ref[...].astype(jnp.float32)
    u = gather_moments(table_ref[...], inner_ref[...], places)
    y = apply_matrix(matrix_ref, live, u)
    y_inner_ref[...] = y[6:8]
    y_ref[...] = scatter_moments(y, places, rows)
    to_right_ref[...] = y_ref[last : last + 4, :]
    to_left_ref[0:2, :] = y_ref[0:2, :]
    to_left_ref[2:4, :] = y_ref[last + 2 : last + 4, :]


def restrict_kernel(
    rim, y_ref, y_inner_ref, b_ref, b_inner_ref, left_ref, right_ref, from_left_ref,
    from_right_ref, edges_ref, live_ref, projection_ref, counts_ref,
    r_ref, r_inner_ref, packed_ref, vals_ref,
):
    edge_count = b_ref.shape[1]
    count = b_inner_ref.shape[1]
    last = 2 * (edge_count // LANES) - 2
    head, tail, ends = settle(y_ref, last, from_left_ref[...], from_right_ref[...], rim)
    exists = rim_row(left_ref[6:8], right_ref[6:8], rim)
    load_table(r_ref, b_ref[...], rim_row(left_ref[2:4], right_ref[2:4], rim))
    r_ref[0:2, :] = r_ref[0:2, :] - head
    r_ref[2:last, :] = r_ref[2:last, :] - y_ref[2:last, :]
    r_ref[last : last + 2, :] = r_ref[last : last + 2, :] - tail
    r_ref[last + 2 : last + 4, :] = exists * (r_ref[last + 2 : last + 4, :] - ends)
    r_inner = b_inner_ref[...] - y_inner_ref[...]
    r_inner_ref[...] = r_inner
    places = edge_places(edges_ref, rim, edge_count + 2 * rim)
    live = live_ref[...].astype(jnp.float32)
    u = gather_moments(r_ref[...], r_inner, places)
    a = projection_ref[0] * u[0:1]
    for m in range(1, 8):
        a = a + projection_ref[m] * u[m : m + 1]
    a = a * live
    for k in range(3):
        vals_ref[:, k * count : (k + 1) * count] = a[2 * k : 2 * k + 2]
    vals_ref[:, 3 * count :] = jnp.zeros((2, LANES), jnp.float32)
    lane = iota((2, LANES), 1)
    start = jnp.int32(0)
    for q in range(packed_ref.shape[0]):
        amount = counts_ref[0, q]
        shift = start & (LANES - 1)
        base = pl.multiple_of(start - shift, LANES)
        back = (LANES - shift) & (LANES - 1)
        first = pltpu.roll(vals_ref[:, pl.ds(base, LANES)], back, 1)
        second = pltpu.roll(vals_ref[:, pl.ds(base + LANES, LANES)], back, 1)
        chosen = jnp.where(lane < LANES - shift, first, second)
        packed_ref[q] = jnp.where(lane < amount, chosen, 0.0)
        start = start + amount


def solve_kernel(arrived_ref, nodes_ref, inverse_ref, out_ref):
    peers = arrived_ref.shape[0]
    groups = inverse_ref.shape[0]
    agg = inverse_ref.shape[1] // 2
    row = iota((8, LANES), 0)
    tall = iota((agg, LANES), 0)
    nodes = nodes_ref[...]
    block, place = nodes >> 6, nodes & (agg - 1)
    total = jnp.zeros((16, agg), jnp.float32)
    span = 16
    for first in range(0, peers, span):
        coarse_parts, fine_parts, hots = [], [], []
        for d in range(first, first + span):
            value = jnp.where(
                row < 4,
                jnp.broadcast_to(arrived_ref[d, 0:1, :], (8, LANES)),
                jnp.broadcast_to(arrived_ref[d, 1:2, :], (8, LANES)),
            )
            value = jnp.where((row & 3) == block[d : d + 1], value, 0.0)
            coarse = value.astype(jnp.bfloat16).astype(jnp.float32)
            coarse_parts.append(coarse)
            fine_parts.append(value - coarse)
            hots.append(jnp.where(tall == place[d : d + 1], 1.0, 0.0))
        spread = jnp.concatenate(
            [jnp.concatenate(coarse_parts, 1), jnp.concatenate(fine_parts, 1)], 0
        ).astype(jnp.bfloat16)
        hot = jnp.concatenate(hots, 1).astype(jnp.bfloat16)
        total = total + lax.dot_general(
            spread, hot, (((1,), (1,)), ((), ())), preferred_element_type=jnp.float32
        )
    g = total[:8] + total[8:]
    vectors = jnp.concatenate([g, pltpu.roll(g, 4, 0)], 1)
    table = jnp.zeros((8, LANES), jnp.float32)
    for b in range(groups):
        h = lax.dot_general(
            vectors, inverse_ref[b], (((1,), (0,)), ((), ())),
            precision=lax.Precision.HIGHEST, preferred_element_type=jnp.float32,
        )[b : b + 1]
        h = jnp.broadcast_to(h, (8, LANES))
        table = jnp.where(row == 2 * b, h, table)
        table = jnp.where(row == 2 * b + 1, pltpu.roll(h, agg, 1), table)
    for d in range(peers):
        low = jnp.broadcast_to(place[d : d + 1], (8, LANES))
        found = jnp.take_along_axis(table, low, axis=1)
        found = jnp.where((row >> 1) == block[d : d + 1], found, 0.0)
        found = found + pltpu.roll(found, 4, 0)
        found = found + pltpu.roll(found, 2, 0)
        out_ref[d] = found[0:2]


def prolong_kernel(
    rim, edge_count, returned_ref, edges_ref, live_ref, projection_ref, counts_ref,
    p_ref, p_inner_ref, to_left_ref, to_right_ref, vals_ref,
):
    rows = p_ref.shape[0]
    count = live_ref.shape[1]
    last = 2 * (edge_count // LANES) - 2
    lane = iota((2, LANES), 1)
    start = jnp.int32(0)
    for q in range(returned_ref.shape[0]):
        shift = start & (LANES - 1)
        base = pl.multiple_of(start - shift, LANES)
        moved = pltpu.roll(returned_ref[q], shift, 1)
        here = pl.ds(base, LANES)
        vals_ref[:, here] = jnp.where(lane >= shift, moved, vals_ref[:, here])
        vals_ref[:, pl.ds(base + LANES, LANES)] = moved
        start = start + counts_ref[0, q]
    nodal = jnp.concatenate([vals_ref[:, k * count : (k + 1) * count] for k in range(3)], 0)
    live = live_ref[...].astype(jnp.float32)
    p = [jnp.sum(projection_ref[m] * nodal, axis=0, keepdims=True) for m in range(8)]
    p = jnp.concatenate(p, 0) * live
    places = edge_places(edges_ref, rim, edge_count + 2 * rim)
    p_inner_ref[...] = p[6:8]
    p_ref[...] = scatter_moments(p, places, rows)
    to_right_ref[...] = p_ref[last : last + 4, :]
    to_left_ref[0:2, :] = p_ref[0:2, :]
    to_left_ref[2:4, :] = p_ref[last + 2 : last + 4, :]


def update_kernel(
    rim, p_ref, p_inner_ref, r_ref, r_inner_ref, x_ref, inner_ref, w_ref, w_inner_ref,
    left_ref, right_ref, from_left_ref, from_right_ref, edges_ref, live_ref, matrix_ref,
    x1_ref, x1_inner_ref, r1_ref, r1_inner_ref, ends_ref, table_ref,
):
    rows = table_ref.shape[0]
    edge_count = x_ref.shape[1]
    blocks = edge_count // LANES
    last = 2 * blocks - 2
    head, tail, ends = settle(p_ref, last, from_left_ref[...], from_right_ref[...], rim)
    exists = rim_row(left_ref[6:8], right_ref[6:8], rim)
    load_table(table_ref, w_ref[...], rim_row(left_ref[4:6], right_ref[4:6], rim))
    table_ref[...] = table_ref[...] * r_ref[...]
    table_ref[0:2, :] = table_ref[0:2, :] + head
    table_ref[2:last, :] = table_ref[2:last, :] + p_ref[2:last, :]
    table_ref[last : last + 2, :] = table_ref[last : last + 2, :] + tail
    table_ref[last + 2 : last + 4, :] = exists * (table_ref[last + 2 : last + 4, :] + ends)
    z_inner = w_inner_ref[...] * r_inner_ref[...] + p_inner_ref[...]
    for h in range(blocks):
        here = slice(h * LANES, (h + 1) * LANES)
        x1_ref[:, here] = x_ref[:, here] + table_ref[2 * h : 2 * h + 2, :]
    x1_inner_ref[...] = inner_ref[...] + z_inner
    places = edge_places(edges_ref, rim, edge_count + 2 * rim)
    live = live_ref[...].astype(jnp.float32)
    u = gather_moments(table_ref[...], z_inner, places)
    y = apply_matrix(matrix_ref, live, u)
    r1_inner_ref[...] = r_inner_ref[...] - y[6:8]
    table_ref[...] = scatter_moments(y, places, rows)
    for h in range(blocks):
        r1_ref[:, h * LANES : (h + 1) * LANES] = (
            r_ref[2 * h : 2 * h + 2, :] - table_ref[2 * h : 2 * h + 2, :]
        )
    ends_ref[...] = table_ref[last + 2 : last + 4, :]


def finish_kernel(rim, partial_ref, from_left_ref, from_right_ref, r1_ref):
    edge_count = partial_ref.shape[1]
    lane = iota((2, LANES), 1)
    r1_ref[...] = partial_ref[...]
    r1_ref[:, :LANES] = partial_ref[:, :LANES] - jnp.where(lane < rim, from_left_ref[...], 0.0)
    r1_ref[:, edge_count - LANES :] = partial_ref[:, edge_count - LANES :] - jnp.where(
        lane >= LANES - rim, pltpu.roll(from_right_ref[...], 64, 1), 0.0
    )


def local_call(kernel, outs, in_smem=(), scratch=(), name=None):
    def call(*args):
        specs = [
            pl.BlockSpec(memory_space=pltpu.SMEM if i in in_smem else pltpu.VMEM)
            for i in range(len(args))
        ]
        shapes = [jax.ShapeDtypeStruct(s, jnp.float32) for s in outs]
        return pl.pallas_call(
            kernel,
            out_shape=shapes,
            in_specs=specs,
            out_specs=[pl.BlockSpec(memory_space=pltpu.VMEM)] * len(outs),
            scratch_shapes=[pltpu.VMEM(s, jnp.float32) for s in scratch],
            compiler_params=pltpu.CompilerParams(vmem_limit_bytes=VMEM_LIMIT),
            name=name,
        )(*args)

    return call


def neighbours(to_left, to_right):
    axis = ("grp", "dom")
    ends = lax.axis_size(axis) - 1
    from_left = lax.ppermute(to_right, axis, [(i, i + 1) for i in range(ends)])
    from_right = lax.ppermute(to_left, axis, [(i + 1, i) for i in range(ends)])
    return from_left, from_right


def shards(
    x_edges,
    x_inner,
    b_edges,
    b_inner,
    w_edges,
    w_inner,
    elem_edges,
    element_live,
    elem_matrix,
    projection,
    owner_counts,
    aux_node,
    aux_inverse,
):
    edge_count = x_edges.shape[1]
    elem_count = x_inner.shape[1]
    rim = elem_count // 32
    peers = owner_counts.shape[1]
    cap = aux_node.shape[0] // peers
    rows = -(-2 * (edge_count // LANES + 1) // 8) * 8
    live = element_live.reshape(1, elem_count)
    ones = jnp.ones((2, LANES), jnp.float32)
    fields = (x_edges, b_edges, w_edges)
    heads = jnp.concatenate([f[:, :LANES] for f in fields] + [ones], 0)
    tails = jnp.concatenate([f[:, edge_count - LANES :] for f in fields] + [ones], 0)
    left, right = neighbours(heads, tails)
    nodes = jnp.pad(aux_node.reshape(peers, cap), ((0, 0), (0, LANES - cap)))
    table = (rows, LANES)
    inner = (2, elem_count)
    message = (4, LANES)
    slots = (peers, 2, LANES)

    y, y_inner, to_left, to_right = local_call(
        functools.partial(residual_kernel, rim), [table, inner, message, message],
        scratch=[table], name="residual",
    )(x_edges, x_inner, left, right, elem_edges, live, elem_matrix)
    from_left, from_right = neighbours(to_left, to_right)
    r, r_inner, packed = local_call(
        functools.partial(restrict_kernel, rim), [table, inner, slots], in_smem=(11,),
        scratch=[(2, 3 * elem_count + LANES)], name="restrict",
    )(
        y, y_inner, b_edges, b_inner, left, right, from_left, from_right, elem_edges, live,
        projection, owner_counts,
    )
    arrived = lax.all_to_all(packed, "dom", split_axis=0, concat_axis=0, tiled=True)
    (outgoing,) = local_call(solve_kernel, [slots], name="solve")(arrived, nodes, aux_inverse)
    returned = lax.all_to_all(outgoing, "dom", split_axis=0, concat_axis=0, tiled=True)
    p, p_inner, to_left, to_right = local_call(
        functools.partial(prolong_kernel, rim, edge_count), [table, inner, message, message],
        in_smem=(4,), scratch=[(2, 3 * elem_count + LANES)], name="prolong",
    )(returned, elem_edges, live, projection, owner_counts)
    from_left, from_right = neighbours(to_left, to_right)
    x1_edges, x1_inner, r1_part, r1_inner, ends = local_call(
        functools.partial(update_kernel, rim),
        [x_edges.shape, inner, x_edges.shape, inner, (2, LANES)],
        scratch=[table], name="update",
    )(
        p, p_inner, r, r_inner, x_edges, x_inner, w_edges, w_inner, left, right, from_left,
        from_right, elem_edges, live, elem_matrix,
    )
    from_left, from_right = neighbours(ends, ends)
    (r1_edges,) = local_call(
        functools.partial(finish_kernel, rim), [x_edges.shape], name="finish"
    )(r1_part, from_left, from_right)
    return x1_edges, x1_inner, r1_edges, r1_inner


def solution(mesh):
    edges = P(None, ("grp", "dom"))
    in_specs = (edges,) * 7 + (
        P(("grp", "dom")),
        P(None, None, ("grp", "dom")),
        P(None, None, ("grp", "dom")),
        P(("grp", "dom"), None),
        P(("grp", "dom")),
        P(("grp", "dom"), None, None),
    )
    return jax.shard_map(
        shards, mesh=mesh, in_specs=in_specs, out_specs=(edges,) * 4, check_vma=False
    )
```

```python
import functools

import jax
import jax.numpy as jnp
from jax import lax
from jax.experimental import pallas as pl
from jax.experimental.pallas import tpu as pltpu
from jax.sharding import PartitionSpec as P

LANES = 128
VMEM_LIMIT = 24 * 2**20


def iota(shape, dim):
    return lax.broadcasted_iota(jnp.int32, shape, dim)


def edge_places(edges_ref, rim, width):
    places = []
    for k in range(3):
        coded = edges_ref[k : k + 1, :]
        flip = (1 - 2 * (coded & 1)).astype(jnp.float32)
        place = (coded >> 1) - rim
        place = jnp.where(place < 0, place + width, place)
        places.append((place >> 7, place & (LANES - 1), flip))
    return places


def row_highs(blocks):
    row = iota((8, LANES), 0)
    return [4 * g + (row >> 1) for g in range(-(-(blocks + 1) // 4))]


def end_highs(blocks):
    row = iota((8, LANES), 0)
    rims = jnp.where(row < 6, blocks, -1)
    return [jnp.where(row < 2, 0, jnp.where(row < 4, blocks - 1, rims))]


def widen(mask_rows, count):
    return jnp.concatenate([mask_rows] * (count // LANES), 1)


def gather_moments(groups, highs, inner, places):
    count = inner.shape[1]
    wide = iota((8, count), 0)
    total = jnp.concatenate([jnp.zeros((6, count), jnp.float32), inner], 0)
    for k, (high, low, flip) in enumerate(places):
        columns = []
        for at in range(0, count, LANES):
            low_b = jnp.broadcast_to(low[:, at : at + LANES], (8, LANES))
            high_b = jnp.broadcast_to(high[:, at : at + LANES], (8, LANES))
            found = jnp.zeros((8, LANES), jnp.float32)
            for group, at_high in zip(groups, highs):
                picked = jnp.take_along_axis(group, low_b, axis=1)
                found = found + jnp.where(high_b == at_high, picked, 0.0)
            found = found + pltpu.roll(found, 4, 0)
            columns.append(found + pltpu.roll(found, 2, 0))
        found = jnp.concatenate(columns, 1)
        found = found * jnp.where(wide == 2 * k, flip, 1.0)
        total = jnp.where((wide >> 1) == k, found, total)
    return total


def scatter_moments(values, places, hot_ref, highs):
    count = values.shape[1]
    rows = 8 * len(highs)
    wide = iota((8, count), 0)
    total = jnp.zeros((2 * rows, LANES), jnp.float32)
    for k, (high, low, flip) in enumerate(places):
        part = jnp.where((wide >> 1) == k, values, 0.0)
        part = part * jnp.where(wide == 2 * k, flip, 1.0)
        part = part + pltpu.roll(part, 4, 0)
        part = part + pltpu.roll(part, 2, 0)
        coarse = part.astype(jnp.bfloat16).astype(jnp.float32)
        spread = []
        for piece in (coarse, part - coarse):
            for at_high in highs:
                spread.append(jnp.where(high == widen(at_high, count), piece, 0.0))
        spread = jnp.concatenate(spread, 0).astype(jnp.bfloat16)
        total = total + lax.dot_general(
            spread, hot_ref[:, k * count : (k + 1) * count], (((1,), (1,)), ((), ())),
            preferred_element_type=jnp.float32,
        )
    return total[:rows] + total[rows:]


def apply_matrix(matrix_ref, live_ref, u):
    y = matrix_ref[0] * u[0:1]
    for j in range(1, 8):
        y = y + matrix_ref[j] * u[j : j + 1]
    return y * live_ref[...].astype(jnp.float32)


def restrict(projection_ref, live_ref, u):
    a = [jnp.sum(projection_ref[n] * u, axis=0, keepdims=True) for n in range(6)]
    return jnp.concatenate(a, 0) * live_ref[...].astype(jnp.float32)


def rim_row(from_left, from_right, rim):
    lane = iota(from_left.shape, 1)
    low = jnp.where(lane < rim, from_right, 0.0)
    return jnp.where((lane >= rim) & (lane < 2 * rim), pltpu.roll(from_left, 64, 1), low)


def arrivals(left, right, rim):
    lane = iota((2, LANES), 1)
    head = jnp.where(lane < rim, left, 0.0)
    return head, jnp.where(lane >= LANES - rim, pltpu.roll(right, 64, 1), 0.0)


def by_side(even_ref, via_odd, via_even):
    even = even_ref[0 : via_odd.shape[0], :] > 0.5
    return jnp.where(even, via_odd, via_even), jnp.where(even, via_even, via_odd)


def load_table(table_ref, edges_ref):
    blocks = edges_ref.shape[1] // LANES
    for h in range(blocks):
        table_ref[2 * h : 2 * h + 2, :] = edges_ref[:, h * LANES : (h + 1) * LANES]
    rest = table_ref.shape[0] - 2 * blocks
    table_ref[2 * blocks :, :] = jnp.zeros((rest, LANES), jnp.float32)


def table_groups(table_ref):
    return [table_ref[8 * g : 8 * g + 8, :] for g in range(table_ref.shape[0] // 8)]


def own_kernel(
    rim, x_ref, inner_ref, edges_ref, live_ref, matrix_ref, y_ref, hot_ref, table_ref
):
    edge_count = x_ref.shape[1]
    count = inner_ref.shape[1]
    load_table(table_ref, x_ref)
    places = edge_places(edges_ref, rim, edge_count + 2 * rim)
    tall = iota((LANES, count), 0)
    for k, (_, low, _) in enumerate(places):
        hot = jnp.where(tall == low, 1.0, 0.0).astype(jnp.bfloat16)
        hot_ref[:, k * count : (k + 1) * count] = hot
    highs = row_highs(edge_count // LANES)
    u = gather_moments(table_groups(table_ref), highs, inner_ref[...], places)
    y_ref[...] = apply_matrix(matrix_ref, live_ref, u)


def residual_kernel(
    rim, even_ref, via_odd_ref, via_even_ref, own_ref, b_ref, w_ref, edges_ref, live_ref,
    matrix_ref, hot_ref, y_ref, ends_ref, exists_ref, odd_ref, even_out_ref,
):
    edge_count = b_ref.shape[1]
    blocks = edge_count // LANES
    count = own_ref.shape[1]
    left, right = by_side(even_ref, via_odd_ref[...], via_even_ref[...])
    exists_ref[...] = rim_row(left[2:4], right[2:4], rim)
    none = jnp.zeros((2, LANES), jnp.float32)
    change = jnp.concatenate([none, none, rim_row(left[0:2], right[0:2], rim), none], 0)
    places = edge_places(edges_ref, rim, edge_count + 2 * rim)
    highs = end_highs(blocks)
    u = gather_moments([change], highs, jnp.zeros((2, count), jnp.float32), places)
    y = own_ref[...] + apply_matrix(matrix_ref, live_ref, u)
    y_ref[...] = y
    ends = scatter_moments(y, places, hot_ref, highs)
    ends_ref[...] = ends
    tail = slice(edge_count - LANES, edge_count)
    to_left = jnp.concatenate([ends[0:2], ends[4:6], b_ref[:, :LANES], w_ref[:, :LANES]], 0)
    to_right = jnp.concatenate([ends[2:4], ends[4:6], b_ref[:, tail], w_ref[:, tail]], 0)
    odd_ref[...], even_out_ref[...] = by_side(even_ref, to_left, to_right)


def partial_kernel(
    rim, y_ref, b_ref, b_inner_ref, edges_ref, live_ref, projection_ref, hot_ref,
    r_ref, r_inner_ref, a_ref,
):
    edge_count = b_ref.shape[1]
    blocks = edge_count // LANES
    places = edge_places(edges_ref, rim, edge_count + 2 * rim)
    highs = row_highs(blocks)
    load_table(r_ref, b_ref)
    total = scatter_moments(y_ref[...], places, hot_ref, highs)
    row = iota(total.shape, 0)
    r_ref[...] = r_ref[...] - jnp.where(row < 2 * blocks, total, 0.0)
    r_inner = b_inner_ref[...] - y_ref[6:8, :]
    r_inner_ref[...] = r_inner
    u = gather_moments(table_groups(r_ref), highs, r_inner, places)
    a_ref[...] = restrict(projection_ref, live_ref, u)


def restrict_kernel(
    rim, edge_count, even_ref, via_odd_ref, via_even_ref, ends_ref, exists_ref, part_ref, a_ref,
    edges_ref, live_ref, projection_ref, counts_ref, r_ref, s_rim_ref, packed_ref, vals_ref,
):
    blocks = edge_count // LANES
    count = a_ref.shape[1]
    left, right = by_side(even_ref, via_odd_ref[...], via_even_ref[...])
    head, tail = arrivals(left[2:4], right[2:4], rim)
    exists = exists_ref[...]
    settled = ends_ref[4:6, :] + rim_row(left[0:2], right[0:2], rim)
    r_rim = exists * (rim_row(left[4:6], right[4:6], rim) - settled)
    change = jnp.concatenate([-head, -tail, r_rim, jnp.zeros((2, LANES), jnp.float32)], 0)
    s_rim_ref[...] = rim_row(left[6:8], right[6:8], rim) * r_rim
    places = edge_places(edges_ref, rim, edge_count + 2 * rim)
    u = gather_moments(
        [change], end_highs(blocks), jnp.zeros((2, count), jnp.float32), places
    )
    a = a_ref[...] + restrict(projection_ref, live_ref, u)
    for k in range(3):
        vals_ref[:, k * count : (k + 1) * count] = a[2 * k : 2 * k + 2]
    vals_ref[:, 3 * count :] = jnp.zeros((2, LANES), jnp.float32)
    lane = iota((2, LANES), 1)
    start = jnp.int32(0)
    for q in range(packed_ref.shape[0]):
        amount = counts_ref[0, q]
        shift = start & (LANES - 1)
        base = pl.multiple_of(start - shift, LANES)
        back = (LANES - shift) & (LANES - 1)
        first = pltpu.roll(vals_ref[:, pl.ds(base, LANES)], back, 1)
        second = pltpu.roll(vals_ref[:, pl.ds(base + LANES, LANES)], back, 1)
        chosen = jnp.where(lane < LANES - shift, first, second)
        packed_ref[q] = jnp.where(lane < amount, chosen, 0.0)
        start = start + amount
    r_ref[...] = part_ref[...]
    last = 2 * blocks - 2
    r_ref[0:2, :] = r_ref[0:2, :] - head
    r_ref[last : last + 2, :] = r_ref[last : last + 2, :] - tail


def slots_kernel(nodes_ref, hot_ref):
    agg = hot_ref.shape[0]
    place = nodes_ref[...] & (agg - 1)
    tall = iota((agg, LANES), 0)
    for d in range(nodes_ref.shape[0]):
        hot = jnp.where(tall == place[d : d + 1], 1.0, 0.0).astype(jnp.bfloat16)
        hot_ref[:, d * LANES : (d + 1) * LANES] = hot


def solve_kernel(arrived_ref, nodes_ref, hot_ref, inverse_ref, out_ref):
    peers = arrived_ref.shape[0]
    groups = inverse_ref.shape[0]
    agg = inverse_ref.shape[1] // 2
    row = iota((8, LANES), 0)
    nodes = nodes_ref[...]
    block, place = nodes >> 6, nodes & (agg - 1)
    total = jnp.zeros((16, agg), jnp.float32)
    span = 16
    for first in range(0, peers, span):
        coarse_parts, fine_parts = [], []
        for d in range(first, first + span):
            value = jnp.where(
                row < 4,
                jnp.broadcast_to(arrived_ref[d, 0:1, :], (8, LANES)),
                jnp.broadcast_to(arrived_ref[d, 1:2, :], (8, LANES)),
            )
            value = jnp.where((row & 3) == block[d : d + 1], value, 0.0)
            coarse = value.astype(jnp.bfloat16).astype(jnp.float32)
            coarse_parts.append(coarse)
            fine_parts.append(value - coarse)
        spread = jnp.concatenate(
            [jnp.concatenate(coarse_parts, 1), jnp.concatenate(fine_parts, 1)], 0
        ).astype(jnp.bfloat16)
        hot = hot_ref[:, first * LANES : (first + span) * LANES]
        total = total + lax.dot_general(
            spread, hot, (((1,), (1,)), ((), ())), preferred_element_type=jnp.float32
        )
    g = total[:8] + total[8:]
    vectors = jnp.concatenate([g, pltpu.roll(g, 4, 0)], 1)
    table = jnp.zeros((8, LANES), jnp.float32)
    for b in range(groups):
        h = lax.dot_general(
            vectors, inverse_ref[b], (((1,), (0,)), ((), ())),
            precision=lax.Precision.HIGHEST, preferred_element_type=jnp.float32,
        )[b : b + 1]
        h = jnp.broadcast_to(h, (8, LANES))
        table = jnp.where(row == 2 * b, h, table)
        table = jnp.where(row == 2 * b + 1, pltpu.roll(h, agg, 1), table)
    for d in range(peers):
        low = jnp.broadcast_to(place[d : d + 1], (8, LANES))
        found = jnp.take_along_axis(table, low, axis=1)
        found = jnp.where((row >> 1) == block[d : d + 1], found, 0.0)
        found = found + pltpu.roll(found, 4, 0)
        found = found + pltpu.roll(found, 2, 0)
        out_ref[d] = found[0:2]


def prolong_kernel(
    rim, edge_count, even_ref, returned_ref, edges_ref, live_ref, projection_ref, counts_ref,
    hot_ref, p_ref, ends_ref, odd_ref, even_out_ref, vals_ref,
):
    count = live_ref.shape[1]
    lane = iota((2, LANES), 1)
    start = jnp.int32(0)
    for q in range(returned_ref.shape[0]):
        shift = start & (LANES - 1)
        base = pl.multiple_of(start - shift, LANES)
        moved = pltpu.roll(returned_ref[q], shift, 1)
        here = pl.ds(base, LANES)
        vals_ref[:, here] = jnp.where(lane >= shift, moved, vals_ref[:, here])
        vals_ref[:, pl.ds(base + LANES, LANES)] = moved
        start = start + counts_ref[0, q]
    nodal = jnp.concatenate([vals_ref[:, k * count : (k + 1) * count] for k in range(3)], 0)
    p = projection_ref[0] * nodal[0:1]
    for n in range(1, 6):
        p = p + projection_ref[n] * nodal[n : n + 1]
    p = p * live_ref[...].astype(jnp.float32)
    p_ref[...] = p
    places = edge_places(edges_ref, rim, edge_count + 2 * rim)
    ends = scatter_moments(p, places, hot_ref, end_highs(edge_count // LANES))
    ends_ref[...] = ends
    to_left = jnp.concatenate([ends[0:2], ends[4:6]], 0)
    to_right = jnp.concatenate([ends[2:4], ends[4:6]], 0)
    odd_ref[...], even_out_ref[...] = by_side(even_ref, to_left, to_right)


def smooth_kernel(
    rim, p_ref, r_ref, r_inner_ref, inner_ref, w_ref, w_inner_ref, edges_ref, live_ref,
    matrix_ref, hot_ref, z_ref, x1_inner_ref, y_ref,
):
    edge_count = w_ref.shape[1]
    blocks = edge_count // LANES
    places = edge_places(edges_ref, rim, edge_count + 2 * rim)
    highs = row_highs(blocks)
    total = scatter_moments(p_ref[...], places, hot_ref, highs)
    row = iota(total.shape, 0)
    load_table(z_ref, w_ref)
    z_ref[...] = z_ref[...] * r_ref[...] + jnp.where(row < 2 * blocks, total, 0.0)
    z_inner = w_inner_ref[...] * r_inner_ref[...] + p_ref[6:8, :]
    x1_inner_ref[...] = inner_ref[...] + z_inner
    u = gather_moments(table_groups(z_ref), highs, z_inner, places)
    y_ref[...] = apply_matrix(matrix_ref, live_ref, u)


def update_kernel(
    rim, edge_count, even_ref, via_odd_ref, via_even_ref, ends_ref, exists_ref, s_rim_ref,
    part_ref, edges_ref, live_ref, matrix_ref, hot_ref, y_ref, change_ref, rims_ref,
):
    count = part_ref.shape[1]
    left, right = by_side(even_ref, via_odd_ref[...], via_even_ref[...])
    head, tail = arrivals(left[2:4], right[2:4], rim)
    settled = ends_ref[4:6, :] + rim_row(left[0:2], right[0:2], rim)
    z_rim = s_rim_ref[...] + exists_ref[...] * settled
    change = jnp.concatenate([head, tail, z_rim, jnp.zeros((2, LANES), jnp.float32)], 0)
    change_ref[...] = change
    places = edge_places(edges_ref, rim, edge_count + 2 * rim)
    highs = end_highs(edge_count // LANES)
    u = gather_moments([change], highs, jnp.zeros((2, count), jnp.float32), places)
    y = part_ref[...] + apply_matrix(matrix_ref, live_ref, u)
    y_ref[...] = y
    rims_ref[...] = scatter_moments(y, places, hot_ref, highs)[4:6]


def output_kernel(
    rim, y_ref, change_ref, z_ref, r_ref, r_inner_ref, x_ref, edges_ref, hot_ref,
    x1_ref, r1_ref, r1_inner_ref,
):
    edge_count = x_ref.shape[1]
    blocks = edge_count // LANES
    places = edge_places(edges_ref, rim, edge_count + 2 * rim)
    total = scatter_moments(y_ref[...], places, hot_ref, row_highs(blocks))
    r1_inner_ref[...] = r_inner_ref[...] - y_ref[6:8, :]
    for h in range(blocks):
        here = slice(h * LANES, (h + 1) * LANES)
        rows = slice(2 * h, 2 * h + 2)
        z = z_ref[rows, :]
        if h == 0:
            z = z + change_ref[0:2, :]
        if h == blocks - 1:
            z = z + change_ref[2:4, :]
        x1_ref[:, here] = x_ref[:, here] + z
        r1_ref[:, here] = r_ref[rows, :] - total[rows]


def finish_kernel(rim, even_ref, part_ref, via_odd_ref, via_even_ref, r1_ref):
    edge_count = part_ref.shape[1]
    left, right = by_side(even_ref, via_odd_ref[...], via_even_ref[...])
    head, tail = arrivals(left, right, rim)
    last = slice(edge_count - LANES, edge_count)
    r1_ref[...] = part_ref[...]
    r1_ref[:, :LANES] = part_ref[:, :LANES] - head
    r1_ref[:, last] = part_ref[:, last] - tail


def local_call(kernel, outs, in_smem=(), scratch=(), name=None):
    def call(*args):
        specs = [
            pl.BlockSpec(memory_space=pltpu.SMEM if i in in_smem else pltpu.VMEM)
            for i in range(len(args))
        ]
        shapes = [jax.ShapeDtypeStruct(*(s if s[-1] == jnp.bfloat16 else (s, jnp.float32)))
                  for s in outs]
        return pl.pallas_call(
            kernel,
            out_shape=shapes,
            in_specs=specs,
            out_specs=[pl.BlockSpec(memory_space=pltpu.VMEM)] * len(outs),
            scratch_shapes=[pltpu.VMEM(s, jnp.float32) for s in scratch],
            compiler_params=pltpu.CompilerParams(vmem_limit_bytes=VMEM_LIMIT),
            cost_estimate=pl.CostEstimate(
                flops=10**8, bytes_accessed=2 * 10**6, transcendentals=0
            ),
            name=name,
        )(*args)

    return call


def swap(odd, even):
    axis = ("grp", "dom")
    count = lax.axis_size(axis)

    def pairs(first):
        lows = range(first, count - 1, 2)
        return [(i, i + 1) for i in lows] + [(i + 1, i) for i in lows]

    return lax.ppermute(odd, axis, pairs(1)), lax.ppermute(even, axis, pairs(0))


def shards(
    x_edges,
    x_inner,
    b_edges,
    b_inner,
    w_edges,
    w_inner,
    elem_edges,
    element_live,
    elem_matrix,
    projection,
    owner_counts,
    aux_node,
    aux_inverse,
):
    edge_count = x_edges.shape[1]
    elem_count = x_inner.shape[1]
    rim = elem_count // 32
    peers = owner_counts.shape[1]
    cap = aux_node.shape[0] // peers
    agg = aux_inverse.shape[1] // 2
    rows = -(-2 * (edge_count // LANES + 1) // 8) * 8
    live = element_live.reshape(1, elem_count)
    projection = jnp.transpose(projection, (1, 0, 2))
    is_even = lax.axis_index(("grp", "dom")) % 2 == 0
    even = jnp.where(is_even, jnp.ones((8, LANES), jnp.float32), 0.0)
    ones = jnp.ones((2, LANES), jnp.float32)
    x_head, x_tail = x_edges[:, :LANES], x_edges[:, edge_count - LANES :]
    via_odd, via_even = swap(
        jnp.concatenate([jnp.where(is_even, x_head, x_tail), ones], 0),
        jnp.concatenate([jnp.where(is_even, x_tail, x_head), ones], 0),
    )
    nodes = jnp.pad(aux_node.reshape(peers, cap), ((0, 0), (0, LANES - cap)))
    table = (rows, LANES)
    group = (8, LANES)
    inner = (2, elem_count)
    moments = (8, elem_count)
    slots = (peers, 2, LANES)
    hots = ((LANES, 3 * elem_count), jnp.bfloat16)
    lists = (2, 3 * elem_count + LANES)

    own, hot = local_call(
        functools.partial(own_kernel, rim), [moments, hots], scratch=[table], name="own"
    )(x_edges, x_inner, elem_edges, live, elem_matrix)
    y, ends, exists, odd_out, even_out = local_call(
        functools.partial(residual_kernel, rim), [moments, group, (2, LANES), group, group],
        name="residual",
    )(
        even, via_odd, via_even, own, b_edges, w_edges, elem_edges, live, elem_matrix, hot
    )
    via_odd, via_even = swap(odd_out, even_out)
    r, r_inner, a = local_call(
        functools.partial(partial_kernel, rim), [table, inner, (6, elem_count)], name="partial"
    )(y, b_edges, b_inner, elem_edges, live, projection, hot)
    r, s_rim, packed = local_call(
        functools.partial(restrict_kernel, rim, edge_count), [table, (2, LANES), slots],
        in_smem=(10,), scratch=[lists], name="restrict",
    )(
        even, via_odd, via_even, ends, exists, r, a, elem_edges, live, projection, owner_counts
    )
    arrived = lax.all_to_all(packed, "dom", split_axis=0, concat_axis=0, tiled=True)
    (slots_hot,) = local_call(
        slots_kernel, [((agg, peers * LANES), jnp.bfloat16)], name="slots"
    )(nodes)
    (outgoing,) = local_call(solve_kernel, [slots], name="solve")(
        arrived, nodes, slots_hot, aux_inverse
    )
    returned = lax.all_to_all(outgoing, "dom", split_axis=0, concat_axis=0, tiled=True)
    p, ends, odd_out, even_out = local_call(
        functools.partial(prolong_kernel, rim, edge_count),
        [moments, group, (4, LANES), (4, LANES)], in_smem=(5,), scratch=[lists], name="prolong",
    )(even, returned, elem_edges, live, projection, owner_counts, hot)
    via_odd, via_even = swap(odd_out, even_out)
    z, x1_inner, az = local_call(
        functools.partial(smooth_kernel, rim), [table, inner, moments], name="smooth"
    )(p, r, r_inner, x_inner, w_edges, w_inner, elem_edges, live, elem_matrix, hot)
    az, change, rims = local_call(
        functools.partial(update_kernel, rim, edge_count), [moments, group, (2, LANES)],
        name="update",
    )(
        even, via_odd, via_even, ends, exists, s_rim, az, elem_edges, live, elem_matrix, hot
    )
    via_odd, via_even = swap(rims, rims)
    x1_edges, r1_part, r1_inner = local_call(
        functools.partial(output_kernel, rim), [x_edges.shape, x_edges.shape, inner],
        name="output",
    )(az, change, z, r, r_inner, x_edges, elem_edges, hot)
    (r1_edges,) = local_call(
        functools.partial(finish_kernel, rim), [x_edges.shape], name="finish"
    )(even, r1_part, via_odd, via_even)
    return x1_edges, x1_inner, r1_edges, r1_inner


def solution(mesh):
    edges = P(None, ("grp", "dom"))
    in_specs = (edges,) * 7 + (
        P(("grp", "dom")),
        P(None, None, ("grp", "dom")),
        P(None, None, ("grp", "dom")),
        P(("grp", "dom"), None),
        P(("grp", "dom")),
        P(("grp", "dom"), None, None),
    )
    return jax.shard_map(
        shards, mesh=mesh, in_specs=in_specs, out_specs=(edges,) * 4, check_vma=False
    )
```

```python
import functools

import jax
import jax.numpy as jnp
from jax import lax
from jax.experimental import pallas as pl
from jax.experimental.pallas import tpu as pltpu
from jax.sharding import PartitionSpec as P

LANES = 128
VMEM_LIMIT = 24 * 2**20


def iota(shape, dim):
    return lax.broadcasted_iota(jnp.int32, shape, dim)


def edge_places(edges_ref, rim, width):
    places = []
    for k in range(3):
        coded = edges_ref[k : k + 1, :]
        flip = (1 - 2 * (coded & 1)).astype(jnp.float32)
        place = (coded >> 1) - rim
        place = jnp.where(place < 0, place + width, place)
        places.append((place >> 7, place & (LANES - 1), flip))
    return places


def row_highs(blocks):
    row = iota((8, LANES), 0)
    return [4 * g + (row >> 1) for g in range(-(-(blocks + 1) // 4))]


def end_highs(blocks):
    row = iota((8, LANES), 0)
    rims = jnp.where(row < 6, blocks, -1)
    return [jnp.where(row < 2, 0, jnp.where(row < 4, blocks - 1, rims))]


def widen(mask_rows, count):
    return jnp.concatenate([mask_rows] * (count // LANES), 1)


def gather_moments(groups, highs, inner, places):
    count = inner.shape[1]
    wide = iota((8, count), 0)
    total = jnp.concatenate([jnp.zeros((6, count), jnp.float32), inner], 0)
    for k, (high, low, flip) in enumerate(places):
        columns = []
        for at in range(0, count, LANES):
            low_b = jnp.broadcast_to(low[:, at : at + LANES], (8, LANES))
            high_b = jnp.broadcast_to(high[:, at : at + LANES], (8, LANES))
            found = jnp.zeros((8, LANES), jnp.float32)
            for group, at_high in zip(groups, highs):
                picked = jnp.take_along_axis(group, low_b, axis=1)
                found = found + jnp.where(high_b == at_high, picked, 0.0)
            found = found + pltpu.roll(found, 4, 0)
            columns.append(found + pltpu.roll(found, 2, 0))
        found = jnp.concatenate(columns, 1)
        found = found * jnp.where(wide == 2 * k, flip, 1.0)
        total = jnp.where((wide >> 1) == k, found, total)
    return total


def scatter_moments(values, places, hot_ref, highs):
    count = values.shape[1]
    rows = 8 * len(highs)
    wide = iota((8, count), 0)
    total = jnp.zeros((2 * rows, LANES), jnp.float32)
    for k, (high, low, flip) in enumerate(places):
        part = jnp.where((wide >> 1) == k, values, 0.0)
        part = part * jnp.where(wide == 2 * k, flip, 1.0)
        part = part + pltpu.roll(part, 4, 0)
        part = part + pltpu.roll(part, 2, 0)
        coarse = part.astype(jnp.bfloat16).astype(jnp.float32)
        spread = []
        for piece in (coarse, part - coarse):
            for at_high in highs:
                spread.append(jnp.where(high == widen(at_high, count), piece, 0.0))
        spread = jnp.concatenate(spread, 0).astype(jnp.bfloat16)
        total = total + lax.dot_general(
            spread, hot_ref[k * count : (k + 1) * count, :], (((1,), (0,)), ((), ())),
            preferred_element_type=jnp.float32,
        )
    return total[:rows] + total[rows:]


def apply_matrix(matrix_ref, live_ref, u):
    y = matrix_ref[0] * u[0:1]
    for j in range(1, 8):
        y = y + matrix_ref[j] * u[j : j + 1]
    return y * live_ref[...].astype(jnp.float32)


def restrict(projection_ref, live_ref, u):
    columns = []
    for at in range(0, u.shape[1], LANES):
        first = at // 2
        a = projection_ref[first : first + 8, :] * u[0:1, at : at + LANES]
        for m in range(1, 8):
            rows = slice(first + 8 * m, first + 8 * m + 8)
            a = a + projection_ref[rows, :] * u[m : m + 1, at : at + LANES]
        columns.append(a)
    a = jnp.concatenate(columns, 1)
    return a * live_ref[...].astype(jnp.float32)


def rim_row(from_left, from_right, rim):
    lane = iota(from_left.shape, 1)
    low = jnp.where(lane < rim, from_right, 0.0)
    return jnp.where((lane >= rim) & (lane < 2 * rim), pltpu.roll(from_left, 64, 1), low)


def arrivals(left, right, rim):
    lane = iota((2, LANES), 1)
    head = jnp.where(lane < rim, left, 0.0)
    return head, jnp.where(lane >= LANES - rim, pltpu.roll(right, 64, 1), 0.0)


def by_side(even_ref, via_odd, via_even):
    even = even_ref[0 : via_odd.shape[0], :] > 0.5
    return jnp.where(even, via_odd, via_even), jnp.where(even, via_even, via_odd)


def load_table(table_ref, edges_ref):
    blocks = edges_ref.shape[1] // LANES
    for h in range(blocks):
        table_ref[2 * h : 2 * h + 2, :] = edges_ref[:, h * LANES : (h + 1) * LANES]
    rest = table_ref.shape[0] - 2 * blocks
    table_ref[2 * blocks :, :] = jnp.zeros((rest, LANES), jnp.float32)


def table_groups(table_ref):
    return [table_ref[8 * g : 8 * g + 8, :] for g in range(table_ref.shape[0] // 8)]


def stage_kernel(rim, count_in, *refs):
    sources, (staged, rest) = refs[:count_in], (refs[count_in : 2 * count_in], refs[2 * count_in :])
    by_moment_ref, y_ref, hot_ref, table_ref, sems = rest
    x_ref, inner_ref, edges_ref, live_ref, matrix_ref, projection_ref = staged[:6]
    copies = [
        pltpu.make_async_copy(source, target, sems.at[i])
        for i, (source, target) in enumerate(zip(sources, staged))
    ]
    for copy in copies:
        copy.start()
    for copy in copies[:4]:
        copy.wait()
    edge_count = x_ref.shape[1]
    count = inner_ref.shape[1]
    load_table(table_ref, x_ref)
    places = edge_places(edges_ref, rim, edge_count + 2 * rim)
    tall = iota((LANES, count), 0)
    for k, (_, low, _) in enumerate(places):
        hot = jnp.transpose(jnp.where(tall == low, 1.0, 0.0))
        hot_ref[k * count : (k + 1) * count, :] = hot.astype(jnp.bfloat16)
    highs = row_highs(edge_count // LANES)
    u = gather_moments(table_groups(table_ref), highs, inner_ref[...], places)
    for copy in copies[4:]:
        copy.wait()
    y_ref[...] = apply_matrix(matrix_ref, live_ref, u)
    by_moment_ref[...] = jnp.zeros(by_moment_ref.shape, jnp.float32)
    for n in range(projection_ref.shape[0]):
        for at in range(0, count, LANES):
            rows = pl.ds(at // 2 + n, 8, stride=8)
            by_moment_ref[rows, :] = projection_ref[n, :, at : at + LANES]


def residual_kernel(
    rim, even_ref, via_odd_ref, via_even_ref, own_ref, b_ref, w_ref, edges_ref, live_ref,
    matrix_ref, hot_ref, y_ref, ends_ref, odd_ref, even_out_ref,
):
    edge_count = b_ref.shape[1]
    blocks = edge_count // LANES
    count = own_ref.shape[1]
    tail = slice(edge_count - LANES, edge_count)
    left, right = by_side(even_ref, via_odd_ref[...], via_even_ref[...])
    none = jnp.zeros((2, LANES), jnp.float32)
    change = jnp.concatenate([none, none, rim_row(left[0:2], right[0:2], rim), none], 0)
    places = edge_places(edges_ref, rim, edge_count + 2 * rim)
    highs = end_highs(blocks)
    u = gather_moments([change], highs, jnp.zeros((2, count), jnp.float32), places)
    y = own_ref[...] + apply_matrix(matrix_ref, live_ref, u)
    y_ref[...] = y
    ends = scatter_moments(y, places, hot_ref, highs)
    ends_ref[...] = ends
    to_left = jnp.concatenate([ends[0:2], ends[4:6], b_ref[:, :LANES], w_ref[:, :LANES]], 0)
    to_right = jnp.concatenate([ends[2:4], ends[4:6], b_ref[:, tail], w_ref[:, tail]], 0)
    odd_ref[...], even_out_ref[...] = by_side(even_ref, to_left, to_right)


def partial_kernel(
    rim, y_ref, b_ref, b_inner_ref, edges_ref, live_ref, projection_ref, hot_ref, nodes_ref,
    inverse_ref, counts_ref, r_ref, r_inner_ref, a_ref, slots_ref, parts_ref,
):
    edge_count = b_ref.shape[1]
    blocks = edge_count // LANES
    places = edge_places(edges_ref, rim, edge_count + 2 * rim)
    highs = row_highs(blocks)
    load_table(r_ref, b_ref)
    total = scatter_moments(y_ref[...], places, hot_ref, highs)
    row = iota(total.shape, 0)
    r_ref[...] = r_ref[...] - jnp.where(row < 2 * blocks, total, 0.0)
    r_inner = b_inner_ref[...] - y_ref[6:8, :]
    r_inner_ref[...] = r_inner
    u = gather_moments(table_groups(r_ref), highs, r_inner, places)
    a_ref[...] = restrict(projection_ref, live_ref, u)
    agg = slots_ref.shape[1]
    place = nodes_ref[...] & (agg - 1)
    tall = iota((agg, LANES), 0)
    for d in range(nodes_ref.shape[0]):
        hot = jnp.transpose(jnp.where(tall == place[d : d + 1], 1.0, 0.0))
        slots_ref[d * LANES : (d + 1) * LANES, :] = hot.astype(jnp.bfloat16)
    size = inverse_ref.shape[1]
    for b in range(inverse_ref.shape[0]):
        coarse = inverse_ref[b].astype(jnp.bfloat16)
        fine = (inverse_ref[b] - coarse.astype(jnp.float32)).astype(jnp.bfloat16)
        parts_ref[:size, b * size : (b + 1) * size] = coarse
        parts_ref[size:, b * size : (b + 1) * size] = fine


def restrict_kernel(
    rim, edge_count, even_ref, via_odd_ref, via_even_ref, ends_ref, exists_ref, part_ref, a_ref,
    edges_ref, live_ref, projection_ref, counts_ref, r_ref, s_rim_ref, packed_ref, vals_ref,
):
    blocks = edge_count // LANES
    count = a_ref.shape[1]
    left, right = by_side(even_ref, via_odd_ref[...], via_even_ref[...])
    head, tail = arrivals(left[2:4], right[2:4], rim)
    exists = exists_ref[...]
    settled = ends_ref[4:6, :] + rim_row(left[0:2], right[0:2], rim)
    r_rim = exists * (rim_row(left[4:6], right[4:6], rim) - settled)
    change = jnp.concatenate([-head, -tail, r_rim, jnp.zeros((2, LANES), jnp.float32)], 0)
    s_rim_ref[...] = rim_row(left[6:8], right[6:8], rim) * r_rim
    places = edge_places(edges_ref, rim, edge_count + 2 * rim)
    u = gather_moments(
        [change], end_highs(blocks), jnp.zeros((2, count), jnp.float32), places
    )
    a = a_ref[...] + restrict(projection_ref, live_ref, u)
    for k in range(3):
        vals_ref[:, k * count : (k + 1) * count] = a[2 * k : 2 * k + 2]
    vals_ref[:, 3 * count :] = jnp.zeros((2, LANES), jnp.float32)
    lane = iota((2, LANES), 1)
    start = jnp.int32(0)
    for q in range(packed_ref.shape[0]):
        amount = counts_ref[0, q]
        shift = start & (LANES - 1)
        base = pl.multiple_of(start - shift, LANES)
        back = (LANES - shift) & (LANES - 1)
        first = pltpu.roll(vals_ref[:, pl.ds(base, LANES)], back, 1)
        second = pltpu.roll(vals_ref[:, pl.ds(base + LANES, LANES)], back, 1)
        chosen = jnp.where(lane < LANES - shift, first, second)
        packed_ref[q] = jnp.where(lane < amount, chosen, 0.0)
        start = start + amount
    r_ref[...] = part_ref[...]
    last = 2 * blocks - 2
    r_ref[0:2, :] = r_ref[0:2, :] - head
    r_ref[last : last + 2, :] = r_ref[last : last + 2, :] - tail


def solve_kernel(arrived_ref, nodes_ref, slots_ref, parts_ref, out_ref):
    peers, agg = nodes_ref.shape[0], slots_ref.shape[1]
    groups = parts_ref.shape[1] // (2 * agg)
    row = iota((8, LANES), 0)
    block = nodes_ref[...] >> 6
    total = jnp.zeros((16, agg), jnp.float32)
    span = 16
    for first in range(0, peers, span):
        coarse_parts, fine_parts = [], []
        for d in range(first, first + span):
            value = jnp.where(
                row < 4,
                jnp.broadcast_to(arrived_ref[2 * d : 2 * d + 1, :], (8, LANES)),
                jnp.broadcast_to(arrived_ref[2 * d + 1 : 2 * d + 2, :], (8, LANES)),
            )
            value = jnp.where((row & 3) == block[d : d + 1], value, 0.0)
            coarse = value.astype(jnp.bfloat16).astype(jnp.float32)
            coarse_parts.append(coarse)
            fine_parts.append(value - coarse)
        spread = jnp.concatenate(
            [jnp.concatenate(coarse_parts, 1), jnp.concatenate(fine_parts, 1)], 0
        ).astype(jnp.bfloat16)
        total = total + lax.dot_general(
            spread, slots_ref[first * LANES : (first + span) * LANES, :],
            (((1,), (0,)), ((), ())), preferred_element_type=jnp.float32,
        )
    g = total[:8] + total[8:]
    vectors = jnp.concatenate([g, pltpu.roll(g, 4, 0)], 1)
    coarse = vectors.astype(jnp.bfloat16).astype(jnp.float32)
    fine = vectors - coarse
    sides = jnp.concatenate(
        [jnp.concatenate([coarse, coarse], 1), jnp.concatenate([fine, jnp.zeros_like(fine)], 1)], 0
    ).astype(jnp.bfloat16)
    solved = lax.dot_general(
        sides, parts_ref[...], (((1,), (0,)), ((), ())), preferred_element_type=jnp.float32
    )
    solved = solved[:8] + solved[8:]
    tables = [
        jnp.broadcast_to(solved[b : b + 1, b * LANES : (b + 1) * LANES], (8, LANES))
        for b in range(groups)
    ]
    for first in range(0, peers, 8):
        here = nodes_ref[first : first + 8, :]
        owner, place = here >> 6, here & (agg - 1)
        for c in range(2):
            found = jnp.zeros((8, LANES), jnp.float32)
            for b in range(groups):
                picked = jnp.take_along_axis(tables[b], place + c * agg, axis=1)
                found = jnp.where(owner == b, picked, found)
            out_ref[pl.ds(2 * first + c, 8, stride=2), :] = found


def prolong_kernel(
    rim, edge_count, even_ref, returned_ref, edges_ref, live_ref, projection_ref, counts_ref,
    hot_ref, p_ref, ends_ref, odd_ref, even_out_ref, vals_ref,
):
    count = live_ref.shape[1]
    lane = iota((2, LANES), 1)
    start = jnp.int32(0)
    for q in range(returned_ref.shape[0]):
        shift = start & (LANES - 1)
        base = pl.multiple_of(start - shift, LANES)
        moved = pltpu.roll(returned_ref[q], shift, 1)
        here = pl.ds(base, LANES)
        pltpu.store(vals_ref.at[:, here], moved, mask=lane >= shift)
        vals_ref[:, pl.ds(base + LANES, LANES)] = moved
        start = start + counts_ref[0, q]
    nodal = jnp.concatenate([vals_ref[:, k * count : (k + 1) * count] for k in range(3)], 0)
    p = projection_ref[0] * nodal[0:1]
    for n in range(1, 6):
        p = p + projection_ref[n] * nodal[n : n + 1]
    p = p * live_ref[...].astype(jnp.float32)
    p_ref[...] = p
    places = edge_places(edges_ref, rim, edge_count + 2 * rim)
    ends = scatter_moments(p, places, hot_ref, end_highs(edge_count // LANES))
    ends_ref[...] = ends
    to_left = jnp.concatenate([ends[0:2], ends[4:6]], 0)
    to_right = jnp.concatenate([ends[2:4], ends[4:6]], 0)
    odd_ref[...], even_out_ref[...] = by_side(even_ref, to_left, to_right)


def smooth_kernel(
    rim, p_ref, r_ref, r_inner_ref, inner_ref, w_ref, w_inner_ref, edges_ref, live_ref,
    matrix_ref, hot_ref, z_ref, x1_inner_ref, y_ref,
):
    edge_count = w_ref.shape[1]
    blocks = edge_count // LANES
    places = edge_places(edges_ref, rim, edge_count + 2 * rim)
    highs = row_highs(blocks)
    total = scatter_moments(p_ref[...], places, hot_ref, highs)
    row = iota(total.shape, 0)
    load_table(z_ref, w_ref)
    z_ref[...] = z_ref[...] * r_ref[...] + jnp.where(row < 2 * blocks, total, 0.0)
    z_inner = w_inner_ref[...] * r_inner_ref[...] + p_ref[6:8, :]
    x1_inner_ref[...] = inner_ref[...] + z_inner
    u = gather_moments(table_groups(z_ref), highs, z_inner, places)
    y_ref[...] = apply_matrix(matrix_ref, live_ref, u)


def update_kernel(
    rim, edge_count, even_ref, via_odd_ref, via_even_ref, ends_ref, exists_ref, s_rim_ref,
    part_ref, edges_ref, live_ref, matrix_ref, hot_ref, y_ref, change_ref, odd_ref, even_out_ref,
):
    count = part_ref.shape[1]
    left, right = by_side(even_ref, via_odd_ref[...], via_even_ref[...])
    head, tail = arrivals(left[2:4], right[2:4], rim)
    settled = ends_ref[4:6, :] + rim_row(left[0:2], right[0:2], rim)
    z_rim = s_rim_ref[...] + exists_ref[...] * settled
    change = jnp.concatenate([head, tail, z_rim, jnp.zeros((2, LANES), jnp.float32)], 0)
    change_ref[...] = change
    places = edge_places(edges_ref, rim, edge_count + 2 * rim)
    highs = end_highs(edge_count // LANES)
    u = gather_moments([change], highs, jnp.zeros((2, count), jnp.float32), places)
    y = part_ref[...] + apply_matrix(matrix_ref, live_ref, u)
    y_ref[...] = y
    rims = scatter_moments(y, places, hot_ref, highs)[4:6]
    odd_ref[...] = rims
    even_out_ref[...] = rims


def output_kernel(
    rim, y_ref, change_ref, z_ref, r_ref, r_inner_ref, x_ref, edges_ref, hot_ref,
    x1_ref, r1_ref, r1_inner_ref,
):
    edge_count = x_ref.shape[1]
    blocks = edge_count // LANES
    places = edge_places(edges_ref, rim, edge_count + 2 * rim)
    total = scatter_moments(y_ref[...], places, hot_ref, row_highs(blocks))
    r1_inner_ref[...] = r_inner_ref[...] - y_ref[6:8, :]
    for h in range(blocks):
        here = slice(h * LANES, (h + 1) * LANES)
        rows = slice(2 * h, 2 * h + 2)
        z = z_ref[rows, :]
        if h == 0:
            z = z + change_ref[0:2, :]
        if h == blocks - 1:
            z = z + change_ref[2:4, :]
        x1_ref[:, here] = x_ref[:, here] + z
        r1_ref[:, here] = r_ref[rows, :] - total[rows]


def finish_kernel(rim, even_ref, part_ref, via_odd_ref, via_even_ref, r1_ref):
    edge_count = part_ref.shape[1]
    left, right = by_side(even_ref, via_odd_ref[...], via_even_ref[...])
    head, tail = arrivals(left, right, rim)
    last = slice(edge_count - LANES, edge_count)
    r1_ref[...] = part_ref[...]
    r1_ref[:, :LANES] = part_ref[:, :LANES] - head
    r1_ref[:, last] = part_ref[:, last] - tail


def local_call(kernel, outs, in_smem=(), in_place=False, scratch=(), sems=0, name=None):
    def call(*args):
        spaces = [pltpu.SMEM if i in in_smem else pltpu.VMEM for i in range(len(args))]
        if in_place:
            spaces = [pltpu.HBM] * len(args)
        shapes = [
            jax.ShapeDtypeStruct(*(o if isinstance(o[0], tuple) else (o, jnp.float32)))
            for o in outs
        ]
        extra = [pltpu.SemaphoreType.DMA((sems,))] if sems else []
        return pl.pallas_call(
            kernel,
            out_shape=shapes,
            in_specs=[pl.BlockSpec(memory_space=space) for space in spaces],
            out_specs=[pl.BlockSpec(memory_space=pltpu.VMEM)] * len(outs),
            scratch_shapes=[pltpu.VMEM(s, jnp.float32) for s in scratch] + extra,
            compiler_params=pltpu.CompilerParams(vmem_limit_bytes=VMEM_LIMIT),
            cost_estimate=pl.CostEstimate(
                flops=10**8, bytes_accessed=2 * 10**6, transcendentals=0
            ),
            name=name,
        )(*args)

    return call


def swap(odd, even):
    axis = ("grp", "dom")
    count = lax.axis_size(axis)

    def pairs(first):
        lows = range(first, count - 1, 2)
        return [(i, i + 1) for i in lows] + [(i + 1, i) for i in lows]

    return lax.ppermute(odd, axis, pairs(1)), lax.ppermute(even, axis, pairs(0))


def shards(
    x_edges,
    x_inner,
    b_edges,
    b_inner,
    w_edges,
    w_inner,
    elem_edges,
    element_live,
    elem_matrix,
    projection,
    owner_counts,
    aux_node,
    aux_inverse,
):
    edge_count = x_edges.shape[1]
    elem_count = x_inner.shape[1]
    rim = elem_count // 32
    peers = owner_counts.shape[1]
    cap = aux_node.shape[0] // peers
    agg = aux_inverse.shape[1] // 2
    rows = -(-2 * (edge_count // LANES + 1) // 8) * 8
    live = element_live.reshape(1, elem_count)
    strip = lax.axis_index(("grp", "dom"))
    even = jnp.where(strip % 2 == 0, jnp.ones((8, LANES), jnp.float32), 0.0)
    lane = iota((2, LANES), 1)
    is_last = strip == lax.axis_size(("grp", "dom")) - 1
    exists = jnp.where(lane < rim, jnp.where(is_last, 0.0, 1.0), jnp.where(strip == 0, 0.0, 1.0))
    exists = jnp.where(lane < 2 * rim, exists, 0.0)
    x_head, x_tail = x_edges[:, :LANES], x_edges[:, edge_count - LANES :]
    ones = jnp.ones((2, LANES), jnp.float32)
    via_odd, via_even = swap(
        jnp.concatenate([jnp.where(strip % 2 == 0, x_head, x_tail), ones], 0),
        jnp.concatenate([jnp.where(strip % 2 == 0, x_tail, x_head), ones], 0),
    )
    nodes = jnp.pad(aux_node.reshape(peers, cap), ((0, 0), (0, LANES - cap)))
    table = (rows, LANES)
    group = (8, LANES)
    inner = (2, elem_count)
    moments = (8, elem_count)
    slots = (peers, 2, LANES)
    hots = ((3 * elem_count, LANES), jnp.bfloat16)
    lists = (2, 3 * elem_count + LANES)

    arguments = (
        x_edges, x_inner, elem_edges, live, elem_matrix, jnp.transpose(projection, (1, 0, 2)),
        b_edges, b_inner, w_edges, w_inner, aux_inverse,
    )
    *staged, by_moment, own, hot = local_call(
        functools.partial(stage_kernel, rim, len(arguments)),
        [(v.shape, v.dtype) for v in arguments] + [(elem_count // 2, LANES), moments, hots],
        in_place=True, scratch=[table], sems=len(arguments), name="stage",
    )(*[pltpu.with_memory_space_constraint(v, pltpu.HBM) for v in arguments])
    x_edges, x_inner, elem_edges, live, elem_matrix, nodal_first = staged[:6]
    b_edges, b_inner, w_edges, w_inner, aux_inverse = staged[6:]
    y, ends, odd_out, even_out = local_call(
        functools.partial(residual_kernel, rim), [moments, group, group, group], name="residual"
    )(
        even, via_odd, via_even, own, b_edges, w_edges, elem_edges, live, elem_matrix, hot
    )
    via_odd, via_even = swap(odd_out, even_out)
    size = 2 * agg
    r, r_inner, a, slots_hot, parts = local_call(
        functools.partial(partial_kernel, rim),
        [
            table, inner, moments, ((peers * LANES, agg), jnp.bfloat16),
            ((2 * size, aux_inverse.shape[0] * size), jnp.bfloat16),
        ],
        in_smem=(10,), name="partial",
    )(
        y, b_edges, b_inner, elem_edges, live, by_moment, hot, nodes, aux_inverse, owner_counts
    )
    r, s_rim, packed = local_call(
        functools.partial(restrict_kernel, rim, edge_count), [table, (2, LANES), slots],
        in_smem=(10,), scratch=[lists], name="restrict",
    )(
        even, via_odd, via_even, ends, exists, r, a, elem_edges, live, by_moment, owner_counts
    )
    arrived = lax.all_to_all(packed, "dom", split_axis=0, concat_axis=0, tiled=True)
    (outgoing,) = local_call(solve_kernel, [(2 * peers, LANES)], name="solve")(
        arrived.reshape(2 * peers, LANES), nodes, slots_hot, parts
    )
    outgoing = outgoing.reshape(slots)
    returned = lax.all_to_all(outgoing, "dom", split_axis=0, concat_axis=0, tiled=True)
    p, ends, odd_out, even_out = local_call(
        functools.partial(prolong_kernel, rim, edge_count),
        [moments, group, (4, LANES), (4, LANES)], in_smem=(5,), scratch=[lists], name="prolong",
    )(even, returned, elem_edges, live, nodal_first, owner_counts, hot)
    via_odd, via_even = swap(odd_out, even_out)
    z, x1_inner, az = local_call(
        functools.partial(smooth_kernel, rim), [table, inner, moments], name="smooth"
    )(p, r, r_inner, x_inner, w_edges, w_inner, elem_edges, live, elem_matrix, hot)
    az, change, odd_out, even_out = local_call(
        functools.partial(update_kernel, rim, edge_count),
        [moments, group, (2, LANES), (2, LANES)], name="update",
    )(
        even, via_odd, via_even, ends, exists, s_rim, az, elem_edges, live, elem_matrix, hot
    )
    via_odd, via_even = swap(odd_out, even_out)
    x1_edges, r1_part, r1_inner = local_call(
        functools.partial(output_kernel, rim), [x_edges.shape, x_edges.shape, inner],
        name="output",
    )(az, change, z, r, r_inner, x_edges, elem_edges, hot)
    (r1_edges,) = local_call(
        functools.partial(finish_kernel, rim), [x_edges.shape], name="finish"
    )(even, r1_part, via_odd, via_even)
    return x1_edges, x1_inner, r1_edges, r1_inner


def solution(mesh):
    edges = P(None, ("grp", "dom"))
    in_specs = (edges,) * 7 + (
        P(("grp", "dom")),
        P(None, None, ("grp", "dom")),
        P(None, None, ("grp", "dom")),
        P(("grp", "dom"), None),
        P(("grp", "dom")),
        P(("grp", "dom"), None, None),
    )
    return jax.shard_map(
        shards, mesh=mesh, in_specs=in_specs, out_specs=(edges,) * 4, check_vma=False
    )
```

```python
import functools

import jax
import jax.numpy as jnp
from jax import lax
from jax.experimental import pallas as pl
from jax.experimental.pallas import tpu as pltpu
from jax.sharding import PartitionSpec as P

LANES = 128
VMEM_LIMIT = 24 * 2**20


def iota(shape, dim):
    return lax.broadcasted_iota(jnp.int32, shape, dim)


def edge_places(edges_ref, rim, width):
    places = []
    for k in range(3):
        coded = edges_ref[k : k + 1, :]
        flip = (1 - 2 * (coded & 1)).astype(jnp.float32)
        place = (coded >> 1) - rim
        place = jnp.where(place < 0, place + width, place)
        places.append((place >> 7, place & (LANES - 1), flip))
    return places


def row_highs(blocks):
    row = iota((8, LANES), 0)
    return [4 * g + (row >> 1) for g in range(-(-(blocks + 1) // 4))]


def end_highs(blocks):
    row = iota((8, LANES), 0)
    rims = jnp.where(row < 6, blocks, -1)
    return [jnp.where(row < 2, 0, jnp.where(row < 4, blocks - 1, rims))]


def widen(mask_rows, count):
    return jnp.concatenate([mask_rows] * (count // LANES), 1)


def gather_moments(groups, highs, inner, places):
    count = inner.shape[1]
    wide = iota((8, count), 0)
    total = jnp.concatenate([jnp.zeros((6, count), jnp.float32), inner], 0)
    for k, (high, low, flip) in enumerate(places):
        columns = []
        for at in range(0, count, LANES):
            low_b = jnp.broadcast_to(low[:, at : at + LANES], (8, LANES))
            high_b = jnp.broadcast_to(high[:, at : at + LANES], (8, LANES))
            found = jnp.zeros((8, LANES), jnp.float32)
            for group, at_high in zip(groups, highs):
                picked = jnp.take_along_axis(group, low_b, axis=1)
                found = found + jnp.where(high_b == at_high, picked, 0.0)
            found = found + pltpu.roll(found, 4, 0)
            columns.append(found + pltpu.roll(found, 2, 0))
        found = jnp.concatenate(columns, 1)
        found = found * jnp.where(wide == 2 * k, flip, 1.0)
        total = jnp.where((wide >> 1) == k, found, total)
    return total


def scatter_moments(values, places, hot_ref, highs):
    count = values.shape[1]
    rows = 8 * len(highs)
    wide = iota((8, count), 0)
    total = jnp.zeros((2 * rows, LANES), jnp.float32)
    for k, (high, low, flip) in enumerate(places):
        part = jnp.where((wide >> 1) == k, values, 0.0)
        part = part * jnp.where(wide == 2 * k, flip, 1.0)
        part = part + pltpu.roll(part, 4, 0)
        part = part + pltpu.roll(part, 2, 0)
        coarse = part.astype(jnp.bfloat16).astype(jnp.float32)
        spread = []
        for piece in (coarse, part - coarse):
            for at_high in highs:
                spread.append(jnp.where(high == widen(at_high, count), piece, 0.0))
        spread = jnp.concatenate(spread, 0).astype(jnp.bfloat16)
        total = total + lax.dot_general(
            spread, hot_ref[k * count : (k + 1) * count, :], (((1,), (0,)), ((), ())),
            preferred_element_type=jnp.float32,
        )
    return total[:rows] + total[rows:]


def apply_matrix(matrix_ref, live_ref, u):
    y = matrix_ref[0] * u[0:1]
    for j in range(1, 8):
        y = y + matrix_ref[j] * u[j : j + 1]
    return y * live_ref[...].astype(jnp.float32)


def restrict(projection_ref, live_ref, u):
    columns = []
    for at in range(0, u.shape[1], LANES):
        first = at // 2
        a = projection_ref[first : first + 8, :] * u[0:1, at : at + LANES]
        for m in range(1, 8):
            rows = slice(first + 8 * m, first + 8 * m + 8)
            a = a + projection_ref[rows, :] * u[m : m + 1, at : at + LANES]
        columns.append(a)
    a = jnp.concatenate(columns, 1)
    return a * live_ref[...].astype(jnp.float32)


def rim_row(from_left, from_right, rim):
    lane = iota(from_left.shape, 1)
    low = jnp.where(lane < rim, from_right, 0.0)
    return jnp.where((lane >= rim) & (lane < 2 * rim), pltpu.roll(from_left, 64, 1), low)


def arrivals(left, right, rim):
    lane = iota((2, LANES), 1)
    head = jnp.where(lane < rim, left, 0.0)
    return head, jnp.where(lane >= LANES - rim, pltpu.roll(right, 64, 1), 0.0)


def by_side(even_ref, via_odd, via_even):
    even = even_ref[0 : via_odd.shape[0], :] > 0.5
    return jnp.where(even, via_odd, via_even), jnp.where(even, via_even, via_odd)


def load_table(table_ref, edges_ref):
    blocks = edges_ref.shape[1] // LANES
    for h in range(blocks):
        table_ref[2 * h : 2 * h + 2, :] = edges_ref[:, h * LANES : (h + 1) * LANES]
    rest = table_ref.shape[0] - 2 * blocks
    table_ref[2 * blocks :, :] = jnp.zeros((rest, LANES), jnp.float32)


def table_groups(table_ref):
    return [table_ref[8 * g : 8 * g + 8, :] for g in range(table_ref.shape[0] // 8)]


def stage_kernel(rim, count_in, *refs):
    sources, (staged, rest) = refs[:count_in], (refs[count_in : 2 * count_in], refs[2 * count_in :])
    by_moment_ref, y_ref, hot_ref, table_ref, sems = rest
    x_ref, inner_ref, edges_ref, live_ref, matrix_ref, projection_ref = staged[:6]
    copies = [
        pltpu.make_async_copy(source, target, sems.at[i])
        for i, (source, target) in enumerate(zip(sources, staged))
    ]
    for copy in copies:
        copy.start()
    for copy in copies[:4]:
        copy.wait()
    edge_count = x_ref.shape[1]
    count = inner_ref.shape[1]
    load_table(table_ref, x_ref)
    places = edge_places(edges_ref, rim, edge_count + 2 * rim)
    tall = iota((LANES, count), 0)
    for k, (_, low, _) in enumerate(places):
        hot = jnp.transpose(jnp.where(tall == low, 1.0, 0.0))
        hot_ref[k * count : (k + 1) * count, :] = hot.astype(jnp.bfloat16)
    highs = row_highs(edge_count // LANES)
    u = gather_moments(table_groups(table_ref), highs, inner_ref[...], places)
    for copy in copies[4:]:
        copy.wait()
    y_ref[...] = apply_matrix(matrix_ref, live_ref, u)
    by_moment_ref[...] = jnp.zeros(by_moment_ref.shape, jnp.float32)
    for n in range(projection_ref.shape[0]):
        for at in range(0, count, LANES):
            rows = pl.ds(at // 2 + n, 8, stride=8)
            by_moment_ref[rows, :] = projection_ref[n, :, at : at + LANES]


def residual_kernel(
    rim, even_ref, via_odd_ref, via_even_ref, own_ref, b_ref, w_ref, edges_ref, live_ref,
    matrix_ref, hot_ref, y_ref, ends_ref, odd_ref, even_out_ref,
):
    edge_count = b_ref.shape[1]
    blocks = edge_count // LANES
    count = own_ref.shape[1]
    tail = slice(edge_count - LANES, edge_count)
    heads, tails = via_odd_ref[:, :LANES], via_odd_ref[:, tail]
    even = even_ref[0:2, :] > 0.5
    left = jnp.where(even, tails, via_even_ref[...])
    right = jnp.where(even, via_even_ref[...], heads)
    none = jnp.zeros((2, LANES), jnp.float32)
    change = jnp.concatenate([none, none, rim_row(left, right, rim), none], 0)
    places = edge_places(edges_ref, rim, edge_count + 2 * rim)
    highs = end_highs(blocks)
    u = gather_moments([change], highs, jnp.zeros((2, count), jnp.float32), places)
    y = own_ref[...] + apply_matrix(matrix_ref, live_ref, u)
    y_ref[...] = y
    ends = scatter_moments(y, places, hot_ref, highs)
    ends_ref[...] = ends
    to_left = jnp.concatenate([ends[0:2], ends[4:6], b_ref[:, :LANES], w_ref[:, :LANES]], 0)
    to_right = jnp.concatenate([ends[2:4], ends[4:6], b_ref[:, tail], w_ref[:, tail]], 0)
    odd_ref[...], even_out_ref[...] = by_side(even_ref, to_left, to_right)


def partial_kernel(
    rim, y_ref, b_ref, b_inner_ref, edges_ref, live_ref, projection_ref, hot_ref, nodes_ref,
    inverse_ref, r_ref, r_inner_ref, a_ref, slots_ref, parts_ref,
):
    edge_count = b_ref.shape[1]
    blocks = edge_count // LANES
    places = edge_places(edges_ref, rim, edge_count + 2 * rim)
    highs = row_highs(blocks)
    load_table(r_ref, b_ref)
    total = scatter_moments(y_ref[...], places, hot_ref, highs)
    row = iota(total.shape, 0)
    r_ref[...] = r_ref[...] - jnp.where(row < 2 * blocks, total, 0.0)
    r_inner = b_inner_ref[...] - y_ref[6:8, :]
    r_inner_ref[...] = r_inner
    u = gather_moments(table_groups(r_ref), highs, r_inner, places)
    a_ref[...] = restrict(projection_ref, live_ref, u)
    place = nodes_ref[...] & (LANES - 1)
    tall = iota((LANES, LANES), 0)
    for d in range(nodes_ref.shape[0]):
        hot = jnp.transpose(jnp.where(tall == place[d : d + 1], 1.0, 0.0))
        slots_ref[d * LANES : (d + 1) * LANES, :] = hot.astype(jnp.bfloat16)
    size = inverse_ref.shape[1]
    for b in range(inverse_ref.shape[0]):
        coarse = inverse_ref[b].astype(jnp.bfloat16)
        fine = (inverse_ref[b] - coarse.astype(jnp.float32)).astype(jnp.bfloat16)
        parts_ref[:size, b * size : (b + 1) * size] = coarse
        parts_ref[size:, b * size : (b + 1) * size] = fine


def restrict_kernel(
    rim, edge_count, even_ref, via_odd_ref, via_even_ref, ends_ref, exists_ref, part_ref, a_ref,
    edges_ref, live_ref, projection_ref, counts_ref, r_ref, s_rim_ref, packed_ref, vals_ref,
):
    blocks = edge_count // LANES
    count = a_ref.shape[1]
    left, right = by_side(even_ref, via_odd_ref[...], via_even_ref[...])
    head, tail = arrivals(left[2:4], right[2:4], rim)
    exists = exists_ref[...]
    settled = ends_ref[4:6, :] + rim_row(left[0:2], right[0:2], rim)
    r_rim = exists * (rim_row(left[4:6], right[4:6], rim) - settled)
    change = jnp.concatenate([-head, -tail, r_rim, jnp.zeros((2, LANES), jnp.float32)], 0)
    s_rim_ref[...] = rim_row(left[6:8], right[6:8], rim) * r_rim
    places = edge_places(edges_ref, rim, edge_count + 2 * rim)
    u = gather_moments(
        [change], end_highs(blocks), jnp.zeros((2, count), jnp.float32), places
    )
    a = a_ref[...] + restrict(projection_ref, live_ref, u)
    for k in range(3):
        vals_ref[:, k * count : (k + 1) * count] = a[2 * k : 2 * k + 2]
    vals_ref[:, 3 * count :] = jnp.zeros((2, LANES), jnp.float32)
    lane = iota((2, LANES), 1)
    start = jnp.int32(0)
    for q in range(packed_ref.shape[0]):
        amount = counts_ref[0, q]
        shift = start & (LANES - 1)
        base = pl.multiple_of(start - shift, LANES)
        back = (LANES - shift) & (LANES - 1)
        first = pltpu.roll(vals_ref[:, pl.ds(base, LANES)], back, 1)
        second = pltpu.roll(vals_ref[:, pl.ds(base + LANES, LANES)], back, 1)
        chosen = jnp.where(lane < LANES - shift, first, second)
        packed_ref[q] = jnp.where(lane < amount, chosen, 0.0)
        start = start + amount
    r_ref[...] = part_ref[...]
    last = 2 * blocks - 2
    r_ref[0:2, :] = r_ref[0:2, :] - head
    r_ref[last : last + 2, :] = r_ref[last : last + 2, :] - tail


def solve_kernel(arrived_ref, nodes_ref, slots_ref, parts_ref, out_ref):
    peers, agg = nodes_ref.shape[0], parts_ref.shape[0] // 4
    groups = parts_ref.shape[1] // (2 * agg)
    row = iota((8, LANES), 0)
    half = nodes_ref[...] >> 7
    total = jnp.zeros((8, LANES), jnp.float32)
    span = 16
    for first in range(0, peers, span):
        spread = []
        for d in range(first, first + span):
            value = jnp.where(
                (row & 2) == 0,
                jnp.broadcast_to(arrived_ref[2 * d : 2 * d + 1, :], (8, LANES)),
                jnp.broadcast_to(arrived_ref[2 * d + 1 : 2 * d + 2, :], (8, LANES)),
            )
            value = jnp.where((row & 1) == half[d : d + 1], value, 0.0)
            coarse = value.astype(jnp.bfloat16).astype(jnp.float32)
            spread.append(jnp.where(row < 4, coarse, value - coarse))
        total = total + lax.dot_general(
            jnp.concatenate(spread, 1).astype(jnp.bfloat16),
            slots_ref[first * LANES : (first + span) * LANES, :],
            (((1,), (0,)), ((), ())), preferred_element_type=jnp.float32,
        )
    g = total + pltpu.roll(total, 4, 0)
    other = pltpu.roll(g, 2, 0)
    low = iota((8, LANES), 1) < agg
    evens = jnp.where(low, g, pltpu.roll(other, agg, 1))
    odds = jnp.where(low, pltpu.roll(g, agg, 1), other)
    vectors = jnp.where(row < 2, evens, pltpu.roll(odds, 2, 0))
    coarse = vectors.astype(jnp.bfloat16).astype(jnp.float32)
    fine = vectors - coarse
    sides = jnp.concatenate(
        [jnp.concatenate([coarse, coarse], 1), jnp.concatenate([fine, jnp.zeros_like(fine)], 1)], 0
    ).astype(jnp.bfloat16)
    solved = lax.dot_general(
        sides, parts_ref[...], (((1,), (0,)), ((), ())), preferred_element_type=jnp.float32
    )
    solved = solved[:8] + solved[8:]
    tables = [
        jnp.broadcast_to(solved[at : at + 1, b * LANES : (b + 1) * LANES], (8, LANES))
        for b, at in enumerate((0, 2, 1, 3)[:groups])
    ]
    for first in range(0, peers, 8):
        here = nodes_ref[first : first + 8, :]
        owner, place = here >> 6, here & (agg - 1)
        for c in range(2):
            found = jnp.zeros((8, LANES), jnp.float32)
            for b in range(groups):
                picked = jnp.take_along_axis(tables[b], place + c * agg, axis=1)
                found = jnp.where(owner == b, picked, found)
            out_ref[pl.ds(2 * first + c, 8, stride=2), :] = found


def prolong_kernel(
    rim, edge_count, even_ref, returned_ref, edges_ref, live_ref, projection_ref, counts_ref,
    hot_ref, p_ref, ends_ref, odd_ref, even_out_ref, vals_ref,
):
    count = live_ref.shape[1]
    lane = iota((2, LANES), 1)
    start = jnp.int32(0)
    for q in range(returned_ref.shape[0]):
        shift = start & (LANES - 1)
        base = pl.multiple_of(start - shift, LANES)
        moved = pltpu.roll(returned_ref[q], shift, 1)
        here = pl.ds(base, LANES)
        pltpu.store(vals_ref.at[:, here], moved, mask=lane >= shift)
        vals_ref[:, pl.ds(base + LANES, LANES)] = moved
        start = start + counts_ref[0, q]
    nodal = jnp.concatenate([vals_ref[:, k * count : (k + 1) * count] for k in range(3)], 0)
    p = projection_ref[0] * nodal[0:1]
    for n in range(1, 6):
        p = p + projection_ref[n] * nodal[n : n + 1]
    p = p * live_ref[...].astype(jnp.float32)
    p_ref[...] = p
    places = edge_places(edges_ref, rim, edge_count + 2 * rim)
    ends = scatter_moments(p, places, hot_ref, end_highs(edge_count // LANES))
    ends_ref[...] = ends
    to_left = jnp.concatenate([ends[0:2], ends[4:6]], 0)
    to_right = jnp.concatenate([ends[2:4], ends[4:6]], 0)
    odd_ref[...], even_out_ref[...] = by_side(even_ref, to_left, to_right)


def smooth_kernel(
    rim, p_ref, r_ref, r_inner_ref, inner_ref, w_ref, w_inner_ref, edges_ref, live_ref,
    matrix_ref, hot_ref, z_ref, x1_inner_ref, y_ref,
):
    edge_count = w_ref.shape[1]
    blocks = edge_count // LANES
    places = edge_places(edges_ref, rim, edge_count + 2 * rim)
    highs = row_highs(blocks)
    total = scatter_moments(p_ref[...], places, hot_ref, highs)
    row = iota(total.shape, 0)
    load_table(z_ref, w_ref)
    z_ref[...] = z_ref[...] * r_ref[...] + jnp.where(row < 2 * blocks, total, 0.0)
    z_inner = w_inner_ref[...] * r_inner_ref[...] + p_ref[6:8, :]
    x1_inner_ref[...] = inner_ref[...] + z_inner
    u = gather_moments(table_groups(z_ref), highs, z_inner, places)
    y_ref[...] = apply_matrix(matrix_ref, live_ref, u)


def update_kernel(
    rim, edge_count, even_ref, via_odd_ref, via_even_ref, ends_ref, exists_ref, s_rim_ref,
    part_ref, edges_ref, live_ref, matrix_ref, hot_ref, y_ref, change_ref, odd_ref, even_out_ref,
):
    count = part_ref.shape[1]
    left, right = by_side(even_ref, via_odd_ref[...], via_even_ref[...])
    head, tail = arrivals(left[2:4], right[2:4], rim)
    settled = ends_ref[4:6, :] + rim_row(left[0:2], right[0:2], rim)
    z_rim = s_rim_ref[...] + exists_ref[...] * settled
    change = jnp.concatenate([head, tail, z_rim, jnp.zeros((2, LANES), jnp.float32)], 0)
    change_ref[...] = change
    places = edge_places(edges_ref, rim, edge_count + 2 * rim)
    highs = end_highs(edge_count // LANES)
    u = gather_moments([change], highs, jnp.zeros((2, count), jnp.float32), places)
    y = part_ref[...] + apply_matrix(matrix_ref, live_ref, u)
    y_ref[...] = y
    rims = scatter_moments(y, places, hot_ref, highs)[4:6]
    odd_ref[...] = rims
    even_out_ref[...] = rims


def output_kernel(
    rim, y_ref, change_ref, z_ref, r_ref, r_inner_ref, x_ref, edges_ref, hot_ref,
    x1_ref, r1_ref, r1_inner_ref,
):
    edge_count = x_ref.shape[1]
    blocks = edge_count // LANES
    places = edge_places(edges_ref, rim, edge_count + 2 * rim)
    total = scatter_moments(y_ref[...], places, hot_ref, row_highs(blocks))
    r1_inner_ref[...] = r_inner_ref[...] - y_ref[6:8, :]
    for h in range(blocks):
        here = slice(h * LANES, (h + 1) * LANES)
        rows = slice(2 * h, 2 * h + 2)
        z = z_ref[rows, :]
        if h == 0:
            z = z + change_ref[0:2, :]
        if h == blocks - 1:
            z = z + change_ref[2:4, :]
        x1_ref[:, here] = x_ref[:, here] + z
        r1_ref[:, here] = r_ref[rows, :] - total[rows]


def finish_kernel(rim, even_ref, part_ref, via_odd_ref, via_even_ref, r1_ref):
    edge_count = part_ref.shape[1]
    left, right = by_side(even_ref, via_odd_ref[...], via_even_ref[...])
    head, tail = arrivals(left, right, rim)
    last = slice(edge_count - LANES, edge_count)
    r1_ref[...] = part_ref[...]
    r1_ref[:, :LANES] = part_ref[:, :LANES] - head
    r1_ref[:, last] = part_ref[:, last] - tail


def local_call(kernel, outs, in_place=False, scratch=(), sems=0, name=None):
    def call(*args):
        spaces = [pltpu.HBM if in_place else pltpu.VMEM] * len(args)
        shapes = [
            jax.ShapeDtypeStruct(*(o if isinstance(o[0], tuple) else (o, jnp.float32)))
            for o in outs
        ]
        extra = [pltpu.SemaphoreType.DMA((sems,))] if sems else []
        return pl.pallas_call(
            kernel,
            out_shape=shapes,
            in_specs=[pl.BlockSpec(memory_space=space) for space in spaces],
            out_specs=[pl.BlockSpec(memory_space=pltpu.VMEM)] * len(outs),
            scratch_shapes=[pltpu.VMEM(s, jnp.float32) for s in scratch] + extra,
            compiler_params=pltpu.CompilerParams(vmem_limit_bytes=VMEM_LIMIT),
            cost_estimate=pl.CostEstimate(
                flops=10**8, bytes_accessed=2 * 10**6, transcendentals=0
            ),
            name=name,
        )(*args)

    return call


def swap(odd, even):
    axis = ("grp", "dom")
    count = lax.axis_size(axis)

    def pairs(first):
        lows = range(first, count - 1, 2)
        return [(i, i + 1) for i in lows] + [(i + 1, i) for i in lows]

    return lax.ppermute(odd, axis, pairs(1)), lax.ppermute(even, axis, pairs(0))


def shards(
    x_edges,
    x_inner,
    b_edges,
    b_inner,
    w_edges,
    w_inner,
    elem_edges,
    element_live,
    elem_matrix,
    projection,
    owner_counts,
    aux_node,
    aux_inverse,
):
    edge_count = x_edges.shape[1]
    elem_count = x_inner.shape[1]
    rim = elem_count // 32
    peers = owner_counts.shape[1]
    cap = aux_node.shape[0] // peers
    rows = -(-2 * (edge_count // LANES + 1) // 8) * 8
    live = element_live.reshape(1, elem_count)
    strip = lax.axis_index(("grp", "dom"))
    even = jnp.where(strip % 2 == 0, jnp.ones((8, LANES), jnp.float32), 0.0)
    lane = iota((2, LANES), 1)
    is_last = strip == lax.axis_size(("grp", "dom")) - 1
    exists = jnp.where(lane < rim, jnp.where(is_last, 0.0, 1.0), jnp.where(strip == 0, 0.0, 1.0))
    exists = jnp.where(lane < 2 * rim, exists, 0.0)
    x_head, x_tail = x_edges[:, :LANES], x_edges[:, edge_count - LANES :]
    via_odd, via_even = swap(x_edges, jnp.where(strip % 2 == 0, x_tail, x_head))
    nodes = jnp.pad(aux_node.reshape(peers, cap), ((0, 0), (0, LANES - cap)))
    table = (rows, LANES)
    group = (8, LANES)
    inner = (2, elem_count)
    moments = (8, elem_count)
    slots = (peers, 2, LANES)
    hots = ((3 * elem_count, LANES), jnp.bfloat16)
    lists = (2, 3 * elem_count + LANES)

    arguments = (
        x_edges, x_inner, elem_edges, live, elem_matrix, jnp.transpose(projection, (1, 0, 2)),
        b_edges, b_inner, w_edges, w_inner, aux_inverse, owner_counts,
    )
    *staged, by_moment, own, hot = local_call(
        functools.partial(stage_kernel, rim, len(arguments)),
        [(v.shape, v.dtype) for v in arguments] + [(elem_count // 2, LANES), moments, hots],
        in_place=True, scratch=[table], sems=len(arguments), name="stage",
    )(*[pltpu.with_memory_space_constraint(v, pltpu.HBM) for v in arguments])
    x_edges, x_inner, elem_edges, live, elem_matrix, nodal_first = staged[:6]
    b_edges, b_inner, w_edges, w_inner, aux_inverse, owner_counts = staged[6:]
    y, ends, odd_out, even_out = local_call(
        functools.partial(residual_kernel, rim), [moments, group, group, group], name="residual"
    )(
        even, via_odd, via_even, own, b_edges, w_edges, elem_edges, live, elem_matrix, hot
    )
    via_odd, via_even = swap(odd_out, even_out)
    size = aux_inverse.shape[1]
    r, r_inner, a, slots_hot, parts = local_call(
        functools.partial(partial_kernel, rim),
        [
            table, inner, moments, ((peers * LANES, LANES), jnp.bfloat16),
            ((2 * size, aux_inverse.shape[0] * size), jnp.bfloat16),
        ],
        name="partial",
    )(
        y, b_edges, b_inner, elem_edges, live, by_moment, hot, nodes, aux_inverse
    )
    r, s_rim, packed = local_call(
        functools.partial(restrict_kernel, rim, edge_count), [table, (2, LANES), slots],
        scratch=[lists], name="restrict",
    )(
        even, via_odd, via_even, ends, exists, r, a, elem_edges, live, by_moment, owner_counts
    )
    arrived = lax.all_to_all(packed, "dom", split_axis=0, concat_axis=0, tiled=True)
    (outgoing,) = local_call(solve_kernel, [(2 * peers, LANES)], name="solve")(
        arrived.reshape(2 * peers, LANES), nodes, slots_hot, parts
    )
    outgoing = outgoing.reshape(slots)
    returned = lax.all_to_all(outgoing, "dom", split_axis=0, concat_axis=0, tiled=True)
    p, ends, odd_out, even_out = local_call(
        functools.partial(prolong_kernel, rim, edge_count),
        [moments, group, (4, LANES), (4, LANES)], scratch=[lists], name="prolong",
    )(even, returned, elem_edges, live, nodal_first, owner_counts, hot)
    via_odd, via_even = swap(odd_out, even_out)
    z, x1_inner, az = local_call(
        functools.partial(smooth_kernel, rim), [table, inner, moments], name="smooth"
    )(p, r, r_inner, x_inner, w_edges, w_inner, elem_edges, live, elem_matrix, hot)
    az, change, odd_out, even_out = local_call(
        functools.partial(update_kernel, rim, edge_count),
        [moments, group, (2, LANES), (2, LANES)], name="update",
    )(
        even, via_odd, via_even, ends, exists, s_rim, az, elem_edges, live, elem_matrix, hot
    )
    via_odd, via_even = swap(odd_out, even_out)
    x1_edges, r1_part, r1_inner = local_call(
        functools.partial(output_kernel, rim), [x_edges.shape, x_edges.shape, inner],
        name="output",
    )(az, change, z, r, r_inner, x_edges, elem_edges, hot)
    (r1_edges,) = local_call(
        functools.partial(finish_kernel, rim), [x_edges.shape], name="finish"
    )(even, r1_part, via_odd, via_even)
    return x1_edges, x1_inner, r1_edges, r1_inner


def solution(mesh):
    edges = P(None, ("grp", "dom"))
    in_specs = (edges,) * 7 + (
        P(("grp", "dom")),
        P(None, None, ("grp", "dom")),
        P(None, None, ("grp", "dom")),
        P(("grp", "dom"), None),
        P(("grp", "dom")),
        P(("grp", "dom"), None, None),
    )
    return jax.shard_map(
        shards, mesh=mesh, in_specs=in_specs, out_specs=(edges,) * 4, check_vma=False
    )
```

```python
import functools
import math

import jax
import jax.numpy as jnp
from jax import lax
from jax.experimental import pallas as pl
from jax.experimental.pallas import tpu as pltpu
from jax.sharding import PartitionSpec as P

LANES = 128
VMEM_LIMIT = 24 * 2**20


def iota(shape, dim):
    return lax.broadcasted_iota(jnp.int32, shape, dim)


def edge_places(edges_ref, rim, width):
    places = []
    for k in range(3):
        coded = edges_ref[k : k + 1, :]
        flip = (1 - 2 * (coded & 1)).astype(jnp.float32)
        place = (coded >> 1) - rim
        place = jnp.where(place < 0, place + width, place)
        places.append((place >> 7, place & (LANES - 1), flip))
    return places


def row_highs(blocks):
    row = iota((8, LANES), 0)
    return [4 * g + (row >> 1) for g in range(-(-(blocks + 1) // 4))]


def end_highs(blocks):
    row = iota((8, LANES), 0)
    rims = jnp.where(row < 6, blocks, -1)
    return [jnp.where(row < 2, 0, jnp.where(row < 4, blocks - 1, rims))]


def widen(mask_rows, count):
    return jnp.concatenate([mask_rows] * (count // LANES), 1)


def gather_moments(groups, highs, inner, places):
    count = inner.shape[1]
    wide = iota((8, count), 0)
    total = jnp.concatenate([jnp.zeros((6, count), jnp.float32), inner], 0)
    for k, (high, low, flip) in enumerate(places):
        columns = []
        for at in range(0, count, LANES):
            low_b = jnp.broadcast_to(low[:, at : at + LANES], (8, LANES))
            high_b = jnp.broadcast_to(high[:, at : at + LANES], (8, LANES))
            found = jnp.zeros((8, LANES), jnp.float32)
            for group, at_high in zip(groups, highs):
                picked = jnp.take_along_axis(group, low_b, axis=1)
                found = found + jnp.where(high_b == at_high, picked, 0.0)
            found = found + pltpu.roll(found, 4, 0)
            columns.append(found + pltpu.roll(found, 2, 0))
        found = jnp.concatenate(columns, 1)
        found = found * jnp.where(wide == 2 * k, flip, 1.0)
        total = jnp.where((wide >> 1) == k, found, total)
    return total


def scatter_moments(values, places, hot_ref, highs):
    count = values.shape[1]
    rows = 8 * len(highs)
    wide = iota((8, count), 0)
    total = jnp.zeros((2 * rows, LANES), jnp.float32)
    for k, (high, low, flip) in enumerate(places):
        part = jnp.where((wide >> 1) == k, values, 0.0)
        part = part * jnp.where(wide == 2 * k, flip, 1.0)
        part = part + pltpu.roll(part, 4, 0)
        part = part + pltpu.roll(part, 2, 0)
        coarse = part.astype(jnp.bfloat16).astype(jnp.float32)
        spread = []
        for piece in (coarse, part - coarse):
            for at_high in highs:
                spread.append(jnp.where(high == widen(at_high, count), piece, 0.0))
        spread = jnp.concatenate(spread, 0).astype(jnp.bfloat16)
        total = total + lax.dot_general(
            spread, hot_ref[k * count : (k + 1) * count, :], (((1,), (0,)), ((), ())),
            preferred_element_type=jnp.float32,
        )
    return total[:rows] + total[rows:]


def apply_matrix(matrix_ref, live_ref, u):
    y = matrix_ref[0] * u[0:1]
    for j in range(1, 8):
        y = y + matrix_ref[j] * u[j : j + 1]
    return y * live_ref[...].astype(jnp.float32)


def restrict(projection_ref, live_ref, u):
    columns = []
    for at in range(0, u.shape[1], LANES):
        first = at // 2
        a = projection_ref[first : first + 8, :] * u[0:1, at : at + LANES]
        for m in range(1, 8):
            rows = slice(first + 8 * m, first + 8 * m + 8)
            a = a + projection_ref[rows, :] * u[m : m + 1, at : at + LANES]
        columns.append(a)
    a = jnp.concatenate(columns, 1)
    return a * live_ref[...].astype(jnp.float32)


def rim_row(from_left, from_right, rim):
    lane = iota(from_left.shape, 1)
    low = jnp.where(lane < rim, from_right, 0.0)
    return jnp.where((lane >= rim) & (lane < 2 * rim), pltpu.roll(from_left, 64, 1), low)


def arrivals(left, right, rim):
    lane = iota((2, LANES), 1)
    head = jnp.where(lane < rim, left, 0.0)
    return head, jnp.where(lane >= LANES - rim, pltpu.roll(right, 64, 1), 0.0)


def by_side(even_ref, via_odd, via_even):
    even = even_ref[0 : via_odd.shape[0], :] > 0.5
    return jnp.where(even, via_odd, via_even), jnp.where(even, via_even, via_odd)


def load_table(table_ref, edges_ref):
    blocks = edges_ref.shape[1] // LANES
    for h in range(blocks):
        table_ref[2 * h : 2 * h + 2, :] = edges_ref[:, h * LANES : (h + 1) * LANES]
    rest = table_ref.shape[0] - 2 * blocks
    table_ref[2 * blocks :, :] = jnp.zeros((rest, LANES), jnp.float32)


def table_groups(table_ref):
    return [table_ref[8 * g : 8 * g + 8, :] for g in range(table_ref.shape[0] // 8)]


def stage_kernel(rim, count_in, *refs):
    sources, (staged, rest) = refs[:count_in], (refs[count_in : 2 * count_in], refs[2 * count_in :])
    by_moment_ref, y_ref, hot_ref, table_ref, sems = rest
    x_ref, inner_ref, edges_ref, live_ref, matrix_ref, projection_ref = staged[:6]
    copies = [
        pltpu.make_async_copy(source, target, sems.at[i])
        for i, (source, target) in enumerate(zip(sources, staged))
    ]
    for copy in copies:
        copy.start()
    for copy in copies[:4]:
        copy.wait()
    edge_count = x_ref.shape[1]
    count = inner_ref.shape[1]
    load_table(table_ref, x_ref)
    places = edge_places(edges_ref, rim, edge_count + 2 * rim)
    tall = iota((LANES, count), 0)
    for k, (_, low, _) in enumerate(places):
        hot = jnp.transpose(jnp.where(tall == low, 1.0, 0.0))
        hot_ref[k * count : (k + 1) * count, :] = hot.astype(jnp.bfloat16)
    highs = row_highs(edge_count // LANES)
    u = gather_moments(table_groups(table_ref), highs, inner_ref[...], places)
    for copy in copies[4:]:
        copy.wait()
    y_ref[...] = apply_matrix(matrix_ref, live_ref, u)
    by_moment_ref[...] = jnp.zeros(by_moment_ref.shape, jnp.float32)
    for n in range(projection_ref.shape[0]):
        for at in range(0, count, LANES):
            rows = pl.ds(at // 2 + n, 8, stride=8)
            by_moment_ref[rows, :] = projection_ref[n, :, at : at + LANES]


def residual_kernel(
    rim, even_ref, via_odd_ref, via_even_ref, own_ref, b_ref, w_ref, edges_ref, live_ref,
    matrix_ref, hot_ref, y_ref, ends_ref, odd_ref, even_out_ref,
):
    edge_count = b_ref.shape[1]
    blocks = edge_count // LANES
    count = own_ref.shape[1]
    tail = slice(edge_count - LANES, edge_count)
    left, _ = by_side(even_ref, via_odd_ref[:, tail], via_even_ref[:, tail])
    _, right = by_side(even_ref, via_odd_ref[:, :LANES], via_even_ref[:, :LANES])
    none = jnp.zeros((2, LANES), jnp.float32)
    change = jnp.concatenate([none, none, rim_row(left, right, rim), none], 0)
    places = edge_places(edges_ref, rim, edge_count + 2 * rim)
    highs = end_highs(blocks)
    u = gather_moments([change], highs, jnp.zeros((2, count), jnp.float32), places)
    y = own_ref[...] + apply_matrix(matrix_ref, live_ref, u)
    y_ref[...] = y
    ends = scatter_moments(y, places, hot_ref, highs)
    ends_ref[...] = ends
    to_left = jnp.concatenate([ends[0:2], ends[4:6], b_ref[:, :LANES], w_ref[:, :LANES]], 0)
    to_right = jnp.concatenate([ends[2:4], ends[4:6], b_ref[:, tail], w_ref[:, tail]], 0)
    odd_ref[...], even_out_ref[...] = by_side(even_ref, to_left, to_right)


def spread_lists(lists_ref, nodes_ref):
    peers = nodes_ref.shape[0]
    cap = lists_ref.shape[0] * LANES // peers
    period = math.lcm(cap, LANES) // cap
    rows = period * cap // LANES
    lane = iota((peers // period, LANES), 1)
    for d in range(period):
        row, shift = divmod(d * cap, LANES)
        back = (LANES - shift) % LANES
        found = lists_ref[pl.ds(row, peers // period, stride=rows), :]
        if shift:
            found = pltpu.roll(found, back, 1)
        if shift + cap > LANES:
            more = lists_ref[pl.ds(row + 1, peers // period, stride=rows), :]
            found = jnp.where(lane < back, found, pltpu.roll(more, back, 1))
        nodes_ref[pl.ds(d, peers // period, stride=period), :] = found


def partial_kernel(
    rim, y_ref, b_ref, b_inner_ref, edges_ref, live_ref, projection_ref, hot_ref, lists_ref,
    inverse_ref, r_ref, r_inner_ref, a_ref, slots_ref, parts_ref, nodes_ref,
):
    edge_count = b_ref.shape[1]
    blocks = edge_count // LANES
    places = edge_places(edges_ref, rim, edge_count + 2 * rim)
    highs = row_highs(blocks)
    load_table(r_ref, b_ref)
    total = scatter_moments(y_ref[...], places, hot_ref, highs)
    row = iota(total.shape, 0)
    r_ref[...] = r_ref[...] - jnp.where(row < 2 * blocks, total, 0.0)
    r_inner = b_inner_ref[...] - y_ref[6:8, :]
    r_inner_ref[...] = r_inner
    u = gather_moments(table_groups(r_ref), highs, r_inner, places)
    a_ref[...] = restrict(projection_ref, live_ref, u)
    spread_lists(lists_ref, nodes_ref)
    place = nodes_ref[...] & (LANES - 1)
    tall = iota((LANES, LANES), 0)
    for d in range(nodes_ref.shape[0]):
        hot = jnp.transpose(jnp.where(tall == place[d : d + 1], 1.0, 0.0))
        slots_ref[d * LANES : (d + 1) * LANES, :] = hot.astype(jnp.bfloat16)
    size = inverse_ref.shape[1]
    for b in range(inverse_ref.shape[0]):
        coarse = inverse_ref[b].astype(jnp.bfloat16)
        fine = (inverse_ref[b] - coarse.astype(jnp.float32)).astype(jnp.bfloat16)
        parts_ref[:size, b * size : (b + 1) * size] = coarse
        parts_ref[size:, b * size : (b + 1) * size] = fine


def restrict_kernel(
    rim, edge_count, even_ref, via_odd_ref, via_even_ref, ends_ref, exists_ref, part_ref, a_ref,
    edges_ref, live_ref, projection_ref, counts_ref, r_ref, s_rim_ref, packed_ref, vals_ref,
):
    blocks = edge_count // LANES
    count = a_ref.shape[1]
    left, right = by_side(even_ref, via_odd_ref[...], via_even_ref[...])
    head, tail = arrivals(left[2:4], right[2:4], rim)
    exists = exists_ref[...]
    settled = ends_ref[4:6, :] + rim_row(left[0:2], right[0:2], rim)
    r_rim = exists * (rim_row(left[4:6], right[4:6], rim) - settled)
    change = jnp.concatenate([-head, -tail, r_rim, jnp.zeros((2, LANES), jnp.float32)], 0)
    s_rim_ref[...] = rim_row(left[6:8], right[6:8], rim) * r_rim
    places = edge_places(edges_ref, rim, edge_count + 2 * rim)
    u = gather_moments(
        [change], end_highs(blocks), jnp.zeros((2, count), jnp.float32), places
    )
    a = a_ref[...] + restrict(projection_ref, live_ref, u)
    for k in range(3):
        vals_ref[:, k * count : (k + 1) * count] = a[2 * k : 2 * k + 2]
    vals_ref[:, 3 * count :] = jnp.zeros((2, LANES), jnp.float32)
    lane = iota((2, LANES), 1)
    start = jnp.int32(0)
    for q in range(packed_ref.shape[0]):
        amount = counts_ref[0, q]
        shift = start & (LANES - 1)
        base = pl.multiple_of(start - shift, LANES)
        back = (LANES - shift) & (LANES - 1)
        first = pltpu.roll(vals_ref[:, pl.ds(base, LANES)], back, 1)
        second = pltpu.roll(vals_ref[:, pl.ds(base + LANES, LANES)], back, 1)
        chosen = jnp.where(lane < LANES - shift, first, second)
        packed_ref[q] = jnp.where(lane < amount, chosen, 0.0)
        start = start + amount
    r_ref[...] = part_ref[...]
    last = 2 * blocks - 2
    r_ref[0:2, :] = r_ref[0:2, :] - head
    r_ref[last : last + 2, :] = r_ref[last : last + 2, :] - tail


def solve_kernel(arrived_ref, nodes_ref, slots_ref, parts_ref, out_ref):
    peers, agg = nodes_ref.shape[0], parts_ref.shape[0] // 4
    groups = parts_ref.shape[1] // (2 * agg)
    row = iota((8, LANES), 0)
    half = nodes_ref[...] >> 7
    total = jnp.zeros((8, LANES), jnp.float32)
    span = 16
    for first in range(0, peers, span):
        spread = []
        for d in range(first, first + span):
            value = jnp.where(
                (row & 2) == 0,
                jnp.broadcast_to(arrived_ref[2 * d : 2 * d + 1, :], (8, LANES)),
                jnp.broadcast_to(arrived_ref[2 * d + 1 : 2 * d + 2, :], (8, LANES)),
            )
            value = jnp.where((row & 1) == half[d : d + 1], value, 0.0)
            coarse = value.astype(jnp.bfloat16).astype(jnp.float32)
            spread.append(jnp.where(row < 4, coarse, value - coarse))
        total = total + lax.dot_general(
            jnp.concatenate(spread, 1).astype(jnp.bfloat16),
            slots_ref[first * LANES : (first + span) * LANES, :],
            (((1,), (0,)), ((), ())), preferred_element_type=jnp.float32,
        )
    g = total + pltpu.roll(total, 4, 0)
    other = pltpu.roll(g, 2, 0)
    low = iota((8, LANES), 1) < agg
    evens = jnp.where(low, g, pltpu.roll(other, agg, 1))
    odds = jnp.where(low, pltpu.roll(g, agg, 1), other)
    vectors = jnp.where(row < 2, evens, pltpu.roll(odds, 2, 0))
    coarse = vectors.astype(jnp.bfloat16).astype(jnp.float32)
    fine = vectors - coarse
    sides = jnp.concatenate(
        [jnp.concatenate([coarse, coarse], 1), jnp.concatenate([fine, jnp.zeros_like(fine)], 1)], 0
    ).astype(jnp.bfloat16)
    solved = lax.dot_general(
        sides, parts_ref[...], (((1,), (0,)), ((), ())), preferred_element_type=jnp.float32
    )
    solved = solved[:8] + solved[8:]
    tables = [
        jnp.broadcast_to(solved[at : at + 1, b * LANES : (b + 1) * LANES], (8, LANES))
        for b, at in enumerate((0, 2, 1, 3)[:groups])
    ]
    for first in range(0, peers, 8):
        here = nodes_ref[first : first + 8, :]
        owner, place = here >> 6, here & (agg - 1)
        for c in range(2):
            found = jnp.zeros((8, LANES), jnp.float32)
            for b in range(groups):
                picked = jnp.take_along_axis(tables[b], place + c * agg, axis=1)
                found = jnp.where(owner == b, picked, found)
            out_ref[pl.ds(2 * first + c, 8, stride=2), :] = found


def prolong_kernel(
    rim, edge_count, even_ref, returned_ref, edges_ref, live_ref, projection_ref, counts_ref,
    hot_ref, p_ref, ends_ref, odd_ref, even_out_ref, vals_ref,
):
    count = live_ref.shape[1]
    lane = iota((2, LANES), 1)
    start = jnp.int32(0)
    for q in range(returned_ref.shape[0]):
        shift = start & (LANES - 1)
        base = pl.multiple_of(start - shift, LANES)
        moved = pltpu.roll(returned_ref[q], shift, 1)
        here = pl.ds(base, LANES)
        pltpu.store(vals_ref.at[:, here], moved, mask=lane >= shift)
        vals_ref[:, pl.ds(base + LANES, LANES)] = moved
        start = start + counts_ref[0, q]
    nodal = jnp.concatenate([vals_ref[:, k * count : (k + 1) * count] for k in range(3)], 0)
    p = projection_ref[0] * nodal[0:1]
    for n in range(1, 6):
        p = p + projection_ref[n] * nodal[n : n + 1]
    p = p * live_ref[...].astype(jnp.float32)
    p_ref[...] = p
    places = edge_places(edges_ref, rim, edge_count + 2 * rim)
    ends = scatter_moments(p, places, hot_ref, end_highs(edge_count // LANES))
    ends_ref[...] = ends
    to_left = jnp.concatenate([ends[0:2], ends[4:6]], 0)
    to_right = jnp.concatenate([ends[2:4], ends[4:6]], 0)
    odd_ref[...], even_out_ref[...] = by_side(even_ref, to_left, to_right)


def smooth_kernel(
    rim, p_ref, r_ref, r_inner_ref, inner_ref, w_ref, w_inner_ref, edges_ref, live_ref,
    matrix_ref, hot_ref, z_ref, x1_inner_ref, y_ref,
):
    edge_count = w_ref.shape[1]
    blocks = edge_count // LANES
    places = edge_places(edges_ref, rim, edge_count + 2 * rim)
    highs = row_highs(blocks)
    total = scatter_moments(p_ref[...], places, hot_ref, highs)
    row = iota(total.shape, 0)
    load_table(z_ref, w_ref)
    z_ref[...] = z_ref[...] * r_ref[...] + jnp.where(row < 2 * blocks, total, 0.0)
    z_inner = w_inner_ref[...] * r_inner_ref[...] + p_ref[6:8, :]
    x1_inner_ref[...] = inner_ref[...] + z_inner
    u = gather_moments(table_groups(z_ref), highs, z_inner, places)
    y_ref[...] = apply_matrix(matrix_ref, live_ref, u)


def update_kernel(
    rim, edge_count, even_ref, via_odd_ref, via_even_ref, ends_ref, exists_ref, s_rim_ref,
    part_ref, edges_ref, live_ref, matrix_ref, hot_ref, y_ref, change_ref, odd_ref, even_out_ref,
):
    count = part_ref.shape[1]
    left, right = by_side(even_ref, via_odd_ref[...], via_even_ref[...])
    head, tail = arrivals(left[2:4], right[2:4], rim)
    settled = ends_ref[4:6, :] + rim_row(left[0:2], right[0:2], rim)
    z_rim = s_rim_ref[...] + exists_ref[...] * settled
    change = jnp.concatenate([head, tail, z_rim, jnp.zeros((2, LANES), jnp.float32)], 0)
    change_ref[...] = change
    places = edge_places(edges_ref, rim, edge_count + 2 * rim)
    highs = end_highs(edge_count // LANES)
    u = gather_moments([change], highs, jnp.zeros((2, count), jnp.float32), places)
    y = part_ref[...] + apply_matrix(matrix_ref, live_ref, u)
    y_ref[...] = y
    rims = scatter_moments(y, places, hot_ref, highs)[4:6]
    odd_ref[...] = rims
    even_out_ref[...] = rims


def output_kernel(
    rim, y_ref, change_ref, z_ref, r_ref, r_inner_ref, x_ref, edges_ref, hot_ref,
    x1_ref, r1_ref, r1_inner_ref,
):
    edge_count = x_ref.shape[1]
    blocks = edge_count // LANES
    places = edge_places(edges_ref, rim, edge_count + 2 * rim)
    total = scatter_moments(y_ref[...], places, hot_ref, row_highs(blocks))
    r1_inner_ref[...] = r_inner_ref[...] - y_ref[6:8, :]
    for h in range(blocks):
        here = slice(h * LANES, (h + 1) * LANES)
        rows = slice(2 * h, 2 * h + 2)
        z = z_ref[rows, :]
        if h == 0:
            z = z + change_ref[0:2, :]
        if h == blocks - 1:
            z = z + change_ref[2:4, :]
        x1_ref[:, here] = x_ref[:, here] + z
        r1_ref[:, here] = r_ref[rows, :] - total[rows]


def finish_kernel(rim, even_ref, part_ref, via_odd_ref, via_even_ref, r1_ref):
    edge_count = part_ref.shape[1]
    left, right = by_side(even_ref, via_odd_ref[...], via_even_ref[...])
    head, tail = arrivals(left, right, rim)
    last = slice(edge_count - LANES, edge_count)
    r1_ref[...] = part_ref[...]
    r1_ref[:, :LANES] = part_ref[:, :LANES] - head
    r1_ref[:, last] = part_ref[:, last] - tail


def local_call(kernel, outs, in_place=False, scratch=(), sems=0, name=None):
    def call(*args):
        spaces = [pltpu.HBM if in_place else pltpu.VMEM] * len(args)
        shapes = [
            jax.ShapeDtypeStruct(*(o if isinstance(o[0], tuple) else (o, jnp.float32)))
            for o in outs
        ]
        extra = [pltpu.SemaphoreType.DMA((sems,))] if sems else []
        return pl.pallas_call(
            kernel,
            out_shape=shapes,
            in_specs=[pl.BlockSpec(memory_space=space) for space in spaces],
            out_specs=[pl.BlockSpec(memory_space=pltpu.VMEM)] * len(outs),
            scratch_shapes=[pltpu.VMEM(s, jnp.float32) for s in scratch] + extra,
            compiler_params=pltpu.CompilerParams(vmem_limit_bytes=VMEM_LIMIT),
            cost_estimate=pl.CostEstimate(
                flops=10**8, bytes_accessed=2 * 10**6, transcendentals=0
            ),
            name=name,
        )(*args)

    return call


def swap(odd, even):
    axis = ("grp", "dom")
    count = lax.axis_size(axis)

    def pairs(first):
        lows = range(first, count - 1, 2)
        return [(i, i + 1) for i in lows] + [(i + 1, i) for i in lows]

    via_even = lax.ppermute(even, axis, pairs(0))
    return lax.ppermute(odd, axis, pairs(1)), via_even


def shards(
    x_edges,
    x_inner,
    b_edges,
    b_inner,
    w_edges,
    w_inner,
    elem_edges,
    element_live,
    elem_matrix,
    projection,
    owner_counts,
    aux_node,
    aux_inverse,
):
    edge_count = x_edges.shape[1]
    elem_count = x_inner.shape[1]
    rim = elem_count // 32
    peers = owner_counts.shape[1]
    rows = -(-2 * (edge_count // LANES + 1) // 8) * 8
    live = element_live.reshape(1, elem_count)
    strip = lax.axis_index(("grp", "dom"))
    even = jnp.where(strip % 2 == 0, jnp.ones((8, LANES), jnp.float32), 0.0)
    lane = iota((2, LANES), 1)
    is_last = strip == lax.axis_size(("grp", "dom")) - 1
    exists = jnp.where(lane < rim, jnp.where(is_last, 0.0, 1.0), jnp.where(strip == 0, 0.0, 1.0))
    exists = jnp.where(lane < 2 * rim, exists, 0.0)
    via_odd, via_even = swap(x_edges, x_edges)
    table = (rows, LANES)
    group = (8, LANES)
    inner = (2, elem_count)
    moments = (8, elem_count)
    slots = (peers, 2, LANES)
    hots = ((3 * elem_count, LANES), jnp.bfloat16)
    lists = (2, 3 * elem_count + LANES)

    arguments = (
        x_edges, x_inner, elem_edges, live, elem_matrix, jnp.transpose(projection, (1, 0, 2)),
        b_edges, b_inner, w_edges, w_inner, aux_inverse, owner_counts,
        aux_node.reshape(-1, LANES),
    )
    *staged, by_moment, own, hot = local_call(
        functools.partial(stage_kernel, rim, len(arguments)),
        [(v.shape, v.dtype) for v in arguments] + [(elem_count // 2, LANES), moments, hots],
        in_place=True, scratch=[table], sems=len(arguments), name="stage",
    )(*[pltpu.with_memory_space_constraint(v, pltpu.HBM) for v in arguments])
    x_edges, x_inner, elem_edges, live, elem_matrix, nodal_first = staged[:6]
    b_edges, b_inner, w_edges, w_inner, aux_inverse, owner_counts, aux_node = staged[6:]
    y, ends, odd_out, even_out = local_call(
        functools.partial(residual_kernel, rim), [moments, group, group, group], name="residual"
    )(
        even, via_odd, via_even, own, b_edges, w_edges, elem_edges, live, elem_matrix, hot
    )
    via_odd, via_even = swap(odd_out, even_out)
    size = aux_inverse.shape[1]
    r, r_inner, a, slots_hot, parts, nodes = local_call(
        functools.partial(partial_kernel, rim),
        [
            table, inner, moments, ((peers * LANES, LANES), jnp.bfloat16),
            ((2 * size, aux_inverse.shape[0] * size), jnp.bfloat16), ((peers, LANES), jnp.int32),
        ],
        name="partial",
    )(
        y, b_edges, b_inner, elem_edges, live, by_moment, hot, aux_node, aux_inverse
    )
    r, s_rim, packed = local_call(
        functools.partial(restrict_kernel, rim, edge_count), [table, (2, LANES), slots],
        scratch=[lists], name="restrict",
    )(
        even, via_odd, via_even, ends, exists, r, a, elem_edges, live, by_moment, owner_counts
    )
    arrived = lax.all_to_all(packed, "dom", split_axis=0, concat_axis=0, tiled=True)
    (outgoing,) = local_call(solve_kernel, [(2 * peers, LANES)], name="solve")(
        arrived.reshape(2 * peers, LANES), nodes, slots_hot, parts
    )
    outgoing = outgoing.reshape(slots)
    returned = lax.all_to_all(outgoing, "dom", split_axis=0, concat_axis=0, tiled=True)
    p, ends, odd_out, even_out = local_call(
        functools.partial(prolong_kernel, rim, edge_count),
        [moments, group, (4, LANES), (4, LANES)], scratch=[lists], name="prolong",
    )(even, returned, elem_edges, live, nodal_first, owner_counts, hot)
    via_odd, via_even = swap(odd_out, even_out)
    z, x1_inner, az = local_call(
        functools.partial(smooth_kernel, rim), [table, inner, moments], name="smooth"
    )(p, r, r_inner, x_inner, w_edges, w_inner, elem_edges, live, elem_matrix, hot)
    az, change, odd_out, even_out = local_call(
        functools.partial(update_kernel, rim, edge_count),
        [moments, group, (2, LANES), (2, LANES)], name="update",
    )(
        even, via_odd, via_even, ends, exists, s_rim, az, elem_edges, live, elem_matrix, hot
    )
    via_odd, via_even = swap(odd_out, even_out)
    x1_edges, r1_part, r1_inner = local_call(
        functools.partial(output_kernel, rim), [x_edges.shape, x_edges.shape, inner],
        name="output",
    )(az, change, z, r, r_inner, x_edges, elem_edges, hot)
    (r1_edges,) = local_call(
        functools.partial(finish_kernel, rim), [x_edges.shape], name="finish"
    )(even, r1_part, via_odd, via_even)
    return x1_edges, x1_inner, r1_edges, r1_inner


def solution(mesh):
    edges = P(None, ("grp", "dom"))
    in_specs = (edges,) * 7 + (
        P(("grp", "dom")),
        P(None, None, ("grp", "dom")),
        P(None, None, ("grp", "dom")),
        P(("grp", "dom"), None),
        P(("grp", "dom")),
        P(("grp", "dom"), None, None),
    )
    return jax.shard_map(
        shards, mesh=mesh, in_specs=in_specs, out_specs=(edges,) * 4, check_vma=False
    )
```

```python
import functools
import math

import jax
import jax.numpy as jnp
from jax import lax
from jax.experimental import pallas as pl
from jax.experimental.pallas import tpu as pltpu
from jax.sharding import PartitionSpec as P

LANES = 128
VMEM_LIMIT = 24 * 2**20


def iota(shape, dim):
    return lax.broadcasted_iota(jnp.int32, shape, dim)


def edge_places(edges_ref, rim, width):
    places = []
    for k in range(3):
        coded = edges_ref[k : k + 1, :]
        flip = (1 - 2 * (coded & 1)).astype(jnp.float32)
        place = (coded >> 1) - rim
        place = jnp.where(place < 0, place + width, place)
        places.append((place >> 7, place & (LANES - 1), flip))
    return places


def row_highs(blocks):
    row = iota((8, LANES), 0)
    return [4 * g + (row >> 1) for g in range(-(-(blocks + 1) // 4))]


def end_highs(blocks):
    row = iota((8, LANES), 0)
    rims = jnp.where(row < 6, blocks, -1)
    return [jnp.where(row < 2, 0, jnp.where(row < 4, blocks - 1, rims))]


def widen(mask_rows, count):
    return jnp.concatenate([mask_rows] * (count // LANES), 1)


def gather_moments(groups, highs, inner, places):
    count = inner.shape[1]
    wide = iota((8, count), 0)
    total = jnp.concatenate([jnp.zeros((6, count), jnp.float32), inner], 0)
    for k, (high, low, flip) in enumerate(places):
        columns = []
        for at in range(0, count, LANES):
            low_b = jnp.broadcast_to(low[:, at : at + LANES], (8, LANES))
            high_b = jnp.broadcast_to(high[:, at : at + LANES], (8, LANES))
            found = jnp.zeros((8, LANES), jnp.float32)
            for group, at_high in zip(groups, highs):
                picked = jnp.take_along_axis(group, low_b, axis=1)
                found = found + jnp.where(high_b == at_high, picked, 0.0)
            found = found + pltpu.roll(found, 4, 0)
            columns.append(found + pltpu.roll(found, 2, 0))
        found = jnp.concatenate(columns, 1)
        found = found * jnp.where(wide == 2 * k, flip, 1.0)
        total = jnp.where((wide >> 1) == k, found, total)
    return total


def scatter_moments(values, places, hot_ref, highs):
    count = values.shape[1]
    rows = 8 * len(highs)
    wide = iota((8, count), 0)
    total = jnp.zeros((2 * rows, LANES), jnp.float32)
    for k, (high, low, flip) in enumerate(places):
        part = jnp.where((wide >> 1) == k, values, 0.0)
        part = part * jnp.where(wide == 2 * k, flip, 1.0)
        part = part + pltpu.roll(part, 4, 0)
        part = part + pltpu.roll(part, 2, 0)
        coarse = part.astype(jnp.bfloat16).astype(jnp.float32)
        spread = []
        for piece in (coarse, part - coarse):
            for at_high in highs:
                spread.append(jnp.where(high == widen(at_high, count), piece, 0.0))
        spread = jnp.concatenate(spread, 0).astype(jnp.bfloat16)
        total = total + lax.dot_general(
            spread, hot_ref[k * count : (k + 1) * count, :], (((1,), (0,)), ((), ())),
            preferred_element_type=jnp.float32,
        )
    return total[:rows] + total[rows:]


def apply_matrix(matrix_ref, live_ref, u):
    y = matrix_ref[0] * u[0:1]
    for j in range(1, 8):
        y = y + matrix_ref[j] * u[j : j + 1]
    return y * live_ref[...].astype(jnp.float32)


def restrict(projection_ref, live_ref, u):
    columns = []
    for at in range(0, u.shape[1], LANES):
        first = at // 2
        a = projection_ref[first : first + 8, :] * u[0:1, at : at + LANES]
        for m in range(1, 8):
            rows = slice(first + 8 * m, first + 8 * m + 8)
            a = a + projection_ref[rows, :] * u[m : m + 1, at : at + LANES]
        columns.append(a)
    a = jnp.concatenate(columns, 1)
    return a * live_ref[...].astype(jnp.float32)


def rim_row(from_left, from_right, rim):
    lane = iota(from_left.shape, 1)
    low = jnp.where(lane < rim, from_right, 0.0)
    return jnp.where((lane >= rim) & (lane < 2 * rim), pltpu.roll(from_left, 64, 1), low)


def arrivals(left, right, rim):
    lane = iota((2, LANES), 1)
    head = jnp.where(lane < rim, left, 0.0)
    return head, jnp.where(lane >= LANES - rim, pltpu.roll(right, 64, 1), 0.0)


def by_side(even_ref, via_odd, via_even):
    even = even_ref[0 : via_odd.shape[0], :] > 0.5
    return jnp.where(even, via_odd, via_even), jnp.where(even, via_even, via_odd)


def load_table(table_ref, edges_ref):
    blocks = edges_ref.shape[1] // LANES
    for h in range(blocks):
        table_ref[2 * h : 2 * h + 2, :] = edges_ref[:, h * LANES : (h + 1) * LANES]
    rest = table_ref.shape[0] - 2 * blocks
    table_ref[2 * blocks :, :] = jnp.zeros((rest, LANES), jnp.float32)


def table_groups(table_ref):
    return [table_ref[8 * g : 8 * g + 8, :] for g in range(table_ref.shape[0] // 8)]


def stage_kernel(rim, count_in, *refs):
    sources, (staged, rest) = refs[:count_in], (refs[count_in : 2 * count_in], refs[2 * count_in :])
    by_moment_ref, y_ref, hot_ref, table_ref, sems = rest
    x_ref, inner_ref, edges_ref, live_ref, matrix_ref, projection_ref = staged[:6]
    copies = [
        pltpu.make_async_copy(source, target, sems.at[i])
        for i, (source, target) in enumerate(zip(sources, staged))
    ]
    for copy in copies:
        copy.start()
    for copy in copies[:4]:
        copy.wait()
    edge_count = x_ref.shape[1]
    count = inner_ref.shape[1]
    load_table(table_ref, x_ref)
    places = edge_places(edges_ref, rim, edge_count + 2 * rim)
    tall = iota((LANES, count), 0)
    for k, (_, low, _) in enumerate(places):
        hot = jnp.transpose(jnp.where(tall == low, 1.0, 0.0))
        hot_ref[k * count : (k + 1) * count, :] = hot.astype(jnp.bfloat16)
    highs = row_highs(edge_count // LANES)
    u = gather_moments(table_groups(table_ref), highs, inner_ref[...], places)
    for copy in copies[4:]:
        copy.wait()
    y_ref[...] = apply_matrix(matrix_ref, live_ref, u)
    by_moment_ref[...] = jnp.zeros(by_moment_ref.shape, jnp.float32)
    for n in range(projection_ref.shape[0]):
        for at in range(0, count, LANES):
            rows = pl.ds(at // 2 + n, 8, stride=8)
            by_moment_ref[rows, :] = projection_ref[n, :, at : at + LANES]


def end_columns(place, blocks, rim):
    high, low, _ = place
    owned = jnp.where((high == blocks - 1) & (low >= LANES - rim), low, -1)
    owned = jnp.where((high == 0) & (low < rim), low + 2 * rim, owned)
    return jnp.where(high == blocks, low, owned)


def couple_kernel(rim, edge_count, edges_ref, live_ref, matrix_ref, right_ref, left_ref):
    blocks = edge_count // LANES
    count = live_ref.shape[1]
    places = edge_places(edges_ref, rim, edge_count + 2 * rim)
    columns = [end_columns(place, blocks, rim) for place in places]
    live = live_ref[...].astype(jnp.float32)
    wide = iota((8, count), 0)
    signs = jnp.ones((8, count), jnp.float32)
    for k, (_, _, flip) in enumerate(places):
        signs = jnp.where(wide == 2 * k, flip, signs)
    tall = iota((LANES, count), 0)
    total = jnp.zeros((LANES, 2 * LANES), jnp.float32)
    for k in range(3):
        blocks_of = {}
        for c in range(2):
            j = 2 * k + c
            weights = matrix_ref[j] * signs * (signs[j : j + 1] * live)
            for d in range(2):
                for side in range(2):
                    row = iota((rim, count), 0) + side * rim
                    block = jnp.zeros((rim, count), jnp.float32)
                    for m in range(3):
                        weight = weights[2 * m + d : 2 * m + d + 1]
                        block = block + jnp.where(row == columns[m], weight, 0.0)
                    blocks_of[side, c, d] = block
        rows = jnp.concatenate([blocks_of[key] for key in sorted(blocks_of)], 0)
        coarse = rows.astype(jnp.bfloat16)
        fine = (rows - coarse.astype(jnp.float32)).astype(jnp.bfloat16)
        hot = jnp.where(tall == columns[k], 1.0, 0.0).astype(jnp.bfloat16)
        for piece in (coarse, fine):
            total = total + lax.dot_general(
                hot, piece, (((1,), (1,)), ((), ())), preferred_element_type=jnp.float32
            )
    right_ref[...] = total[:, :LANES]
    left_ref[...] = total[:, LANES:]


def residual_kernel(
    rim, even_ref, via_odd_ref, via_even_ref, own_ref, b_ref, w_ref, edges_ref, live_ref,
    matrix_ref, hot_ref, to_right_ref, to_left_ref, y_ref, ends_ref, odd_ref, even_out_ref,
):
    edge_count = b_ref.shape[1]
    blocks = edge_count // LANES
    count = own_ref.shape[1]
    tail = slice(edge_count - LANES, edge_count)
    left, _ = by_side(even_ref, via_odd_ref[:, tail], via_even_ref[:, tail])
    _, right = by_side(even_ref, via_odd_ref[:, :LANES], via_even_ref[:, :LANES])
    none = jnp.zeros((2, LANES), jnp.float32)
    change = jnp.concatenate([none, none, rim_row(left, right, rim), none], 0)
    places = edge_places(edges_ref, rim, edge_count + 2 * rim)
    highs = end_highs(blocks)
    u = gather_moments([change], highs, jnp.zeros((2, count), jnp.float32), places)
    y = own_ref[...] + apply_matrix(matrix_ref, live_ref, u)
    y_ref[...] = y
    ends = scatter_moments(y, places, hot_ref, highs)
    ends_ref[...] = ends
    to_left = jnp.concatenate([ends[0:2], ends[4:6], b_ref[:, :LANES], w_ref[:, :LANES]], 0)
    to_right = jnp.concatenate([ends[2:4], ends[4:6], b_ref[:, tail], w_ref[:, tail]], 0)
    odd_ref[0:8, :], even_out_ref[0:8, :] = by_side(even_ref, to_left, to_right)
    for at in range(0, LANES, 8):
        rows, there = slice(at, at + 8), slice(at + 8, at + 16)
        odd_ref[there, :], even_out_ref[there, :] = by_side(
            even_ref, to_left_ref[rows, :], to_right_ref[rows, :]
        )


def spread_lists(lists_ref, nodes_ref):
    peers = nodes_ref.shape[0]
    cap = lists_ref.shape[0] * LANES // peers
    period = math.lcm(cap, LANES) // cap
    rows = period * cap // LANES
    lane = iota((peers // period, LANES), 1)
    for d in range(period):
        row, shift = divmod(d * cap, LANES)
        back = (LANES - shift) % LANES
        found = lists_ref[pl.ds(row, peers // period, stride=rows), :]
        if shift:
            found = pltpu.roll(found, back, 1)
        if shift + cap > LANES:
            more = lists_ref[pl.ds(row + 1, peers // period, stride=rows), :]
            found = jnp.where(lane < back, found, pltpu.roll(more, back, 1))
        nodes_ref[pl.ds(d, peers // period, stride=period), :] = found


def partial_kernel(
    rim, y_ref, b_ref, b_inner_ref, edges_ref, live_ref, projection_ref, hot_ref, lists_ref,
    inverse_ref, r_ref, r_inner_ref, a_ref, slots_ref, parts_ref, nodes_ref,
):
    edge_count = b_ref.shape[1]
    blocks = edge_count // LANES
    places = edge_places(edges_ref, rim, edge_count + 2 * rim)
    highs = row_highs(blocks)
    load_table(r_ref, b_ref)
    total = scatter_moments(y_ref[...], places, hot_ref, highs)
    row = iota(total.shape, 0)
    r_ref[...] = r_ref[...] - jnp.where(row < 2 * blocks, total, 0.0)
    r_inner = b_inner_ref[...] - y_ref[6:8, :]
    r_inner_ref[...] = r_inner
    u = gather_moments(table_groups(r_ref), highs, r_inner, places)
    a_ref[...] = restrict(projection_ref, live_ref, u)
    spread_lists(lists_ref, nodes_ref)
    place = nodes_ref[...] & (LANES - 1)
    tall = iota((LANES, LANES), 0)
    for d in range(nodes_ref.shape[0]):
        hot = jnp.transpose(jnp.where(tall == place[d : d + 1], 1.0, 0.0))
        slots_ref[d * LANES : (d + 1) * LANES, :] = hot.astype(jnp.bfloat16)
    size = inverse_ref.shape[1]
    for b in range(inverse_ref.shape[0]):
        coarse = inverse_ref[b].astype(jnp.bfloat16)
        fine = (inverse_ref[b] - coarse.astype(jnp.float32)).astype(jnp.bfloat16)
        parts_ref[:size, b * size : (b + 1) * size] = coarse
        parts_ref[size:, b * size : (b + 1) * size] = fine


def restrict_kernel(
    rim, edge_count, even_ref, via_odd_ref, via_even_ref, ends_ref, exists_ref, part_ref, a_ref,
    edges_ref, live_ref, projection_ref, counts_ref, r_ref, s_rim_ref, packed_ref, vals_ref,
):
    blocks = edge_count // LANES
    count = a_ref.shape[1]
    left, right = by_side(even_ref, via_odd_ref[0:8, :], via_even_ref[0:8, :])
    head, tail = arrivals(left[2:4], right[2:4], rim)
    exists = exists_ref[...]
    settled = ends_ref[4:6, :] + rim_row(left[0:2], right[0:2], rim)
    r_rim = exists * (rim_row(left[4:6], right[4:6], rim) - settled)
    change = jnp.concatenate([-head, -tail, r_rim, jnp.zeros((2, LANES), jnp.float32)], 0)
    s_rim_ref[...] = rim_row(left[6:8], right[6:8], rim) * r_rim
    places = edge_places(edges_ref, rim, edge_count + 2 * rim)
    u = gather_moments(
        [change], end_highs(blocks), jnp.zeros((2, count), jnp.float32), places
    )
    a = a_ref[...] + restrict(projection_ref, live_ref, u)
    for k in range(3):
        vals_ref[:, k * count : (k + 1) * count] = a[2 * k : 2 * k + 2]
    vals_ref[:, 3 * count :] = jnp.zeros((2, LANES), jnp.float32)
    lane = iota((2, LANES), 1)
    start = jnp.int32(0)
    for q in range(packed_ref.shape[0]):
        amount = counts_ref[0, q]
        shift = start & (LANES - 1)
        base = pl.multiple_of(start - shift, LANES)
        back = (LANES - shift) & (LANES - 1)
        first = pltpu.roll(vals_ref[:, pl.ds(base, LANES)], back, 1)
        second = pltpu.roll(vals_ref[:, pl.ds(base + LANES, LANES)], back, 1)
        chosen = jnp.where(lane < LANES - shift, first, second)
        packed_ref[q] = jnp.where(lane < amount, chosen, 0.0)
        start = start + amount
    r_ref[...] = part_ref[...]
    last = 2 * blocks - 2
    r_ref[0:2, :] = r_ref[0:2, :] - head
    r_ref[last : last + 2, :] = r_ref[last : last + 2, :] - tail


def solve_kernel(arrived_ref, nodes_ref, slots_ref, parts_ref, out_ref):
    peers, agg = nodes_ref.shape[0], parts_ref.shape[0] // 4
    groups = parts_ref.shape[1] // (2 * agg)
    row = iota((8, LANES), 0)
    half = nodes_ref[...] >> 7
    total = jnp.zeros((8, LANES), jnp.float32)
    span = 16
    for first in range(0, peers, span):
        spread = []
        for d in range(first, first + span):
            value = jnp.where(
                (row & 2) == 0,
                jnp.broadcast_to(arrived_ref[2 * d : 2 * d + 1, :], (8, LANES)),
                jnp.broadcast_to(arrived_ref[2 * d + 1 : 2 * d + 2, :], (8, LANES)),
            )
            value = jnp.where((row & 1) == half[d : d + 1], value, 0.0)
            coarse = value.astype(jnp.bfloat16).astype(jnp.float32)
            spread.append(jnp.where(row < 4, coarse, value - coarse))
        total = total + lax.dot_general(
            jnp.concatenate(spread, 1).astype(jnp.bfloat16),
            slots_ref[first * LANES : (first + span) * LANES, :],
            (((1,), (0,)), ((), ())), preferred_element_type=jnp.float32,
        )
    g = total + pltpu.roll(total, 4, 0)
    other = pltpu.roll(g, 2, 0)
    low = iota((8, LANES), 1) < agg
    evens = jnp.where(low, g, pltpu.roll(other, agg, 1))
    odds = jnp.where(low, pltpu.roll(g, agg, 1), other)
    vectors = jnp.where(row < 2, evens, pltpu.roll(odds, 2, 0))
    coarse = vectors.astype(jnp.bfloat16).astype(jnp.float32)
    fine = vectors - coarse
    sides = jnp.concatenate(
        [jnp.concatenate([coarse, coarse], 1), jnp.concatenate([fine, jnp.zeros_like(fine)], 1)], 0
    ).astype(jnp.bfloat16)
    solved = lax.dot_general(
        sides, parts_ref[...], (((1,), (0,)), ((), ())), preferred_element_type=jnp.float32
    )
    solved = solved[:8] + solved[8:]
    tables = [
        jnp.broadcast_to(solved[at : at + 1, b * LANES : (b + 1) * LANES], (8, LANES))
        for b, at in enumerate((0, 2, 1, 3)[:groups])
    ]
    for first in range(0, peers, 8):
        here = nodes_ref[first : first + 8, :]
        owner, place = here >> 6, here & (agg - 1)
        for c in range(2):
            found = jnp.zeros((8, LANES), jnp.float32)
            for b in range(groups):
                picked = jnp.take_along_axis(tables[b], place + c * agg, axis=1)
                found = jnp.where(owner == b, picked, found)
            out_ref[pl.ds(2 * first + c, 8, stride=2), :] = found


def prolong_kernel(
    rim, even_ref, low_ref, returned_ref, edges_ref, live_ref, projection_ref, counts_ref,
    hot_ref, exists_ref, s_rim_ref, r_ref, r_inner_ref, w_ref, w_inner_ref, matrix_ref,
    z_ref, z_inner_ref, y_ref, ends_ref, two_high_ref, odd_ref, two_low_ref, even_out_ref,
    vals_ref,
):
    count = live_ref.shape[1]
    edge_count = w_ref.shape[1]
    blocks = edge_count // LANES
    last = 2 * blocks - 2
    lane = iota((2, LANES), 1)
    start = jnp.int32(0)
    for q in range(returned_ref.shape[0]):
        shift = start & (LANES - 1)
        base = pl.multiple_of(start - shift, LANES)
        moved = pltpu.roll(returned_ref[q], shift, 1)
        here = pl.ds(base, LANES)
        pltpu.store(vals_ref.at[:, here], moved, mask=lane >= shift)
        vals_ref[:, pl.ds(base + LANES, LANES)] = moved
        start = start + counts_ref[0, q]
    nodal = jnp.concatenate([vals_ref[:, k * count : (k + 1) * count] for k in range(3)], 0)
    p = projection_ref[0] * nodal[0:1]
    for n in range(1, 6):
        p = p + projection_ref[n] * nodal[n : n + 1]
    p = p * live_ref[...].astype(jnp.float32)
    places = edge_places(edges_ref, rim, edge_count + 2 * rim)
    highs = row_highs(blocks)
    total = scatter_moments(p, places, hot_ref, highs)
    none = jnp.zeros((2, LANES), jnp.float32)
    ends = jnp.concatenate([total[0:2], total[last : last + 4], none], 0)
    ends_ref[...] = ends
    load_table(z_ref, w_ref)
    row = iota(total.shape, 0)
    z_ref[...] = z_ref[...] * r_ref[...] + jnp.where(row < 2 * blocks, total, 0.0)
    z_ref[last + 2 : last + 4, :] = s_rim_ref[...] + exists_ref[...] * ends[4:6]
    z_inner = w_inner_ref[...] * r_inner_ref[...] + p[6:8]
    z_inner_ref[...] = z_inner
    u = gather_moments(table_groups(z_ref), highs, z_inner, places)
    y = apply_matrix(matrix_ref, live_ref, u)
    y_ref[...] = y
    rims = scatter_moments(y, places, hot_ref, end_highs(blocks))[4:6]
    to_left = jnp.concatenate([ends[0:2], ends[4:6], rims, none], 0)
    to_right = jnp.concatenate([ends[2:4], ends[4:6], rims, none], 0)
    odd_ref[...], even_out_ref[...] = by_side(even_ref, to_left, to_right)
    two_high_ref[...], two_low_ref[...] = by_side(low_ref, to_left, to_right)


def output_kernel(
    rim, y_ref, z_inner_ref, r_ref, inner_ref, w_ref, edges_ref, hot_ref, x1_inner_ref, part_ref
):
    edge_count = w_ref.shape[1]
    x1_inner_ref[...] = inner_ref[...] + z_inner_ref[...]
    places = edge_places(edges_ref, rim, edge_count + 2 * rim)
    total = scatter_moments(y_ref[...], places, hot_ref, row_highs(edge_count // LANES))
    part_ref[...] = r_ref[...] - total


def coupled(change, coupling, rim):
    rows = jnp.concatenate([change, jnp.zeros((6, LANES), jnp.float32)], 0)
    found = lax.dot_general(
        rows, coupling, (((1,), (0,)), ((), ())),
        precision=lax.Precision.HIGHEST, preferred_element_type=jnp.float32,
    )
    return found[0:1] + pltpu.roll(found[1:2], 64, 1)


def finish_kernel(
    rim, via_two_low_ref, via_two_high_ref, via_odd_ref, via_even_ref, even_ref, low_ref,
    odd_before_ref, even_before_ref, ends_ref, exists_ref, z_ref, y_ref, part_ref, x_ref,
    r_inner_ref, edges_ref, live_ref, matrix_ref, hot_ref, x1_ref, r1_ref, r1_inner_ref,
):
    edge_count = x_ref.shape[1]
    count = y_ref.shape[1]
    blocks = edge_count // LANES
    left, right = by_side(even_ref, via_odd_ref[...], via_even_ref[...])
    left_two, right_two = by_side(low_ref, via_two_high_ref[...], via_two_low_ref[...])
    head, tail = arrivals(left[2:4], right[2:4], rim)
    z_rim = exists_ref[...] * rim_row(left[0:2], right[0:2], rim)
    change = jnp.concatenate([head, tail, z_rim, jnp.zeros((2, LANES), jnp.float32)], 0)
    places = edge_places(edges_ref, rim, edge_count + 2 * rim)
    u = gather_moments(
        [change], end_highs(blocks), jnp.zeros((2, count), jnp.float32), places
    )
    more = apply_matrix(matrix_ref, live_ref, u)
    r1_inner_ref[...] = r_inner_ref[...] - (y_ref[6:8, :] + more[6:8])
    total = scatter_moments(more, places, hot_ref, row_highs(blocks))

    ends = ends_ref[...]
    lane = iota((2, LANES), 1)

    def columns(first, second, third, fourth):
        turned = [pltpu.roll(v, 64, 1) for v in (second, third, fourth)]
        latter = jnp.where(lane < 3 * rim, turned[1], turned[2])
        return jnp.where(lane < rim, first, jnp.where(lane < 2 * rim, turned[0], latter))

    unknown_left = columns(ends[0:2], left_two[0:2], left_two[2:4], ends[4:6])
    unknown_right = columns(right_two[0:2], ends[2:4], ends[4:6], right_two[2:4])
    is_even = even_ref[0:1, :] > 0.5
    odd_before, even_before = odd_before_ref[8:, :], even_before_ref[8:, :]
    from_left = coupled(unknown_left, jnp.where(is_even, odd_before, even_before), rim)
    from_right = coupled(unknown_right, jnp.where(is_even, even_before, odd_before), rim)
    head_sum, tail_sum = arrivals(left[4:6], right[4:6], rim)
    add_head = jnp.concatenate([from_left, pltpu.roll(from_left, LANES - rim, 1)], 0)
    add_tail = jnp.concatenate(
        [pltpu.roll(from_right, LANES - rim, 1), pltpu.roll(from_right, LANES - 2 * rim, 1)], 0
    )
    head_sum = head_sum + jnp.where(lane < rim, add_head, 0.0)
    tail_sum = tail_sum + jnp.where(lane >= LANES - rim, add_tail, 0.0)
    for h in range(blocks):
        here = slice(h * LANES, (h + 1) * LANES)
        rows = slice(2 * h, 2 * h + 2)
        z = z_ref[rows, :]
        r1 = part_ref[rows, :] - total[rows]
        if h == 0:
            z, r1 = z + head, r1 - head_sum
        if h == blocks - 1:
            z, r1 = z + tail, r1 - tail_sum
        x1_ref[:, here] = x_ref[:, here] + z
        r1_ref[:, here] = r1


def local_call(kernel, outs, in_place=False, scratch=(), sems=0, name=None):
    def call(*args):
        spaces = [pltpu.HBM if in_place else pltpu.VMEM] * len(args)
        shapes = [
            jax.ShapeDtypeStruct(*(o if isinstance(o[0], tuple) else (o, jnp.float32)))
            for o in outs
        ]
        extra = [pltpu.SemaphoreType.DMA((sems,))] if sems else []
        return pl.pallas_call(
            kernel,
            out_shape=shapes,
            in_specs=[pl.BlockSpec(memory_space=space) for space in spaces],
            out_specs=[pl.BlockSpec(memory_space=pltpu.VMEM)] * len(outs),
            scratch_shapes=[pltpu.VMEM(s, jnp.float32) for s in scratch] + extra,
            compiler_params=pltpu.CompilerParams(vmem_limit_bytes=VMEM_LIMIT),
            cost_estimate=pl.CostEstimate(
                flops=10**8, bytes_accessed=2 * 10**6, transcendentals=0
            ),
            name=name,
        )(*args)

    return call


def swap(message, lows):
    pairs = [pair for low, high in lows for pair in ((low, high), (high, low))]
    return lax.ppermute(message, ("grp", "dom"), pairs)


def strip_pairs(gap, first):
    count = lax.axis_size(("grp", "dom"))
    lows = [i for i in range(count - gap) if (i - first) % (2 * gap) < gap]
    return [(i, i + gap) for i in lows]


def shards(
    x_edges,
    x_inner,
    b_edges,
    b_inner,
    w_edges,
    w_inner,
    elem_edges,
    element_live,
    elem_matrix,
    projection,
    owner_counts,
    aux_node,
    aux_inverse,
):
    edge_count = x_edges.shape[1]
    elem_count = x_inner.shape[1]
    rim = elem_count // 32
    peers = owner_counts.shape[1]
    rows = -(-2 * (edge_count // LANES + 1) // 8) * 8
    live = element_live.reshape(1, elem_count)
    strip = lax.axis_index(("grp", "dom"))
    even = jnp.where(strip % 2 == 0, jnp.ones((8, LANES), jnp.float32), 0.0)
    lane = iota((2, LANES), 1)
    is_last = strip == lax.axis_size(("grp", "dom")) - 1
    exists = jnp.where(lane < rim, jnp.where(is_last, 0.0, 1.0), jnp.where(strip == 0, 0.0, 1.0))
    exists = jnp.where(lane < 2 * rim, exists, 0.0)
    odd, evens = strip_pairs(1, 1), strip_pairs(1, 0)
    low = jnp.where(strip % 4 < 2, jnp.ones((8, LANES), jnp.float32), 0.0)
    via_even = swap(x_edges, evens)
    via_odd = swap(x_edges, odd)
    table = (rows, LANES)
    group = (8, LANES)
    inner = (2, elem_count)
    moments = (8, elem_count)
    slots = (peers, 2, LANES)
    hots = ((3 * elem_count, LANES), jnp.bfloat16)
    lists = (2, 3 * elem_count + LANES)

    arguments = (
        x_edges, x_inner, elem_edges, live, elem_matrix, jnp.transpose(projection, (1, 0, 2)),
        b_edges, b_inner, w_edges, w_inner, aux_inverse, owner_counts,
        aux_node.reshape(-1, LANES),
    )
    *staged, by_moment, own, hot = local_call(
        functools.partial(stage_kernel, rim, len(arguments)),
        [(v.shape, v.dtype) for v in arguments] + [(elem_count // 2, LANES), moments, hots],
        in_place=True, scratch=[table], sems=len(arguments), name="stage",
    )(*[pltpu.with_memory_space_constraint(v, pltpu.HBM) for v in arguments])
    x_edges, x_inner, elem_edges, live, elem_matrix, nodal_first = staged[:6]
    b_edges, b_inner, w_edges, w_inner, aux_inverse, owner_counts, aux_node = staged[6:]
    square = (LANES, LANES)
    to_right, to_left = local_call(
        functools.partial(couple_kernel, rim, edge_count), [square, square], name="couple"
    )(elem_edges, live, elem_matrix)
    message = (8 + LANES, LANES)
    y, ends, odd_out, even_out = local_call(
        functools.partial(residual_kernel, rim), [moments, group, message, message],
        name="residual",
    )(
        even, via_odd, via_even, own, b_edges, w_edges, elem_edges, live, elem_matrix, hot,
        to_right, to_left,
    )
    even_before = swap(even_out, evens)
    odd_before = swap(odd_out, odd)
    size = aux_inverse.shape[1]
    r, r_inner, a, slots_hot, parts, nodes = local_call(
        functools.partial(partial_kernel, rim),
        [
            table, inner, moments, ((peers * LANES, LANES), jnp.bfloat16),
            ((2 * size, aux_inverse.shape[0] * size), jnp.bfloat16), ((peers, LANES), jnp.int32),
        ],
        name="partial",
    )(
        y, b_edges, b_inner, elem_edges, live, by_moment, hot, aux_node, aux_inverse
    )
    r, s_rim, packed = local_call(
        functools.partial(restrict_kernel, rim, edge_count), [table, (2, LANES), slots],
        scratch=[lists], name="restrict",
    )(
        even, odd_before, even_before, ends, exists, r, a, elem_edges, live, by_moment, owner_counts
    )
    arrived = lax.all_to_all(packed, "dom", split_axis=0, concat_axis=0, tiled=True)
    (outgoing,) = local_call(solve_kernel, [(2 * peers, LANES)], name="solve")(
        arrived.reshape(2 * peers, LANES), nodes, slots_hot, parts
    )
    outgoing = outgoing.reshape(slots)
    returned = lax.all_to_all(outgoing, "dom", split_axis=0, concat_axis=0, tiled=True)
    z, z_inner, az, ends, two_high, odd_out, two_low, even_out = local_call(
        functools.partial(prolong_kernel, rim),
        [table, inner, moments, group, group, group, group, group],
        scratch=[lists], name="prolong",
    )(
        even, low, returned, elem_edges, live, nodal_first, owner_counts, hot, exists, s_rim, r,
        r_inner, w_edges, w_inner, elem_matrix,
    )
    via_even = swap(even_out, evens)
    via_two_low = swap(two_low, strip_pairs(2, 0))
    via_odd = swap(odd_out, odd)
    via_two_high = swap(two_high, strip_pairs(2, 2))
    x1_inner, part = local_call(
        functools.partial(output_kernel, rim), [inner, table], name="output"
    )(az, z_inner, r, x_inner, w_edges, elem_edges, hot)
    x1_edges, r1_edges, r1_inner = local_call(
        functools.partial(finish_kernel, rim), [x_edges.shape, x_edges.shape, inner], name="finish"
    )(
        via_two_low, via_two_high, via_odd, via_even, even, low, odd_before, even_before, ends,
        exists, z, az, part, x_edges, r_inner, elem_edges, live, elem_matrix, hot,
    )
    return x1_edges, x1_inner, r1_edges, r1_inner


def solution(mesh):
    edges = P(None, ("grp", "dom"))
    in_specs = (edges,) * 7 + (
        P(("grp", "dom")),
        P(None, None, ("grp", "dom")),
        P(None, None, ("grp", "dom")),
        P(("grp", "dom"), None),
        P(("grp", "dom")),
        P(("grp", "dom"), None, None),
    )
    return jax.shard_map(
        shards, mesh=mesh, in_specs=in_specs, out_specs=(edges,) * 4, check_vma=False
    )
```

```python
import functools
import math

import jax
import jax.numpy as jnp
from jax import lax
from jax.experimental import pallas as pl
from jax.experimental.pallas import tpu as pltpu
from jax.sharding import PartitionSpec as P

LANES = 128
VMEM_LIMIT = 24 * 2**20


def iota(shape, dim):
    return lax.broadcasted_iota(jnp.int32, shape, dim)


def edge_places(edges_ref, rim, width):
    places = []
    for k in range(3):
        coded = edges_ref[k : k + 1, :]
        flip = (1 - 2 * (coded & 1)).astype(jnp.float32)
        place = (coded >> 1) - rim
        place = jnp.where(place < 0, place + width, place)
        places.append((place >> 7, place & (LANES - 1), flip))
    return places


def row_highs(blocks):
    row = iota((8, LANES), 0)
    return [4 * g + (row >> 1) for g in range(-(-(blocks + 1) // 4))]


def end_highs(blocks):
    row = iota((8, LANES), 0)
    rims = jnp.where(row < 6, blocks, -1)
    return [jnp.where(row < 2, 0, jnp.where(row < 4, blocks - 1, rims))]


def widen(mask_rows, count):
    return jnp.concatenate([mask_rows] * (count // LANES), 1)


def gather_moments(groups, highs, inner, places):
    count = inner.shape[1]
    wide = iota((8, count), 0)
    total = jnp.concatenate([jnp.zeros((6, count), jnp.float32), inner], 0)
    for k, (high, low, flip) in enumerate(places):
        columns = []
        for at in range(0, count, LANES):
            low_b = jnp.broadcast_to(low[:, at : at + LANES], (8, LANES))
            high_b = jnp.broadcast_to(high[:, at : at + LANES], (8, LANES))
            found = jnp.zeros((8, LANES), jnp.float32)
            for group, at_high in zip(groups, highs):
                picked = jnp.take_along_axis(group, low_b, axis=1)
                found = found + jnp.where(high_b == at_high, picked, 0.0)
            found = found + pltpu.roll(found, 4, 0)
            columns.append(found + pltpu.roll(found, 2, 0))
        found = jnp.concatenate(columns, 1)
        found = found * jnp.where(wide == 2 * k, flip, 1.0)
        total = jnp.where((wide >> 1) == k, found, total)
    return total


def scatter_moments(values, places, hot_ref, highs):
    count = values.shape[1]
    rows = 8 * len(highs)
    wide = iota((8, count), 0)
    total = jnp.zeros((2 * rows, LANES), jnp.float32)
    for k, (high, low, flip) in enumerate(places):
        part = jnp.where((wide >> 1) == k, values, 0.0)
        part = part * jnp.where(wide == 2 * k, flip, 1.0)
        part = part + pltpu.roll(part, 4, 0)
        part = part + pltpu.roll(part, 2, 0)
        coarse = part.astype(jnp.bfloat16).astype(jnp.float32)
        spread = []
        for piece in (coarse, part - coarse):
            for at_high in highs:
                spread.append(jnp.where(high == widen(at_high, count), piece, 0.0))
        spread = jnp.concatenate(spread, 0).astype(jnp.bfloat16)
        total = total + lax.dot_general(
            spread, hot_ref[k * count : (k + 1) * count, :], (((1,), (0,)), ((), ())),
            preferred_element_type=jnp.float32,
        )
    return total[:rows] + total[rows:]


def apply_matrix(matrix_ref, live_ref, u):
    y = matrix_ref[0] * u[0:1]
    for j in range(1, 8):
        y = y + matrix_ref[j] * u[j : j + 1]
    return y * live_ref[...].astype(jnp.float32)


def restrict(projection_ref, live_ref, u):
    columns = []
    for at in range(0, u.shape[1], LANES):
        first = at // 2
        a = projection_ref[first : first + 8, :] * u[0:1, at : at + LANES]
        for m in range(1, 8):
            rows = slice(first + 8 * m, first + 8 * m + 8)
            a = a + projection_ref[rows, :] * u[m : m + 1, at : at + LANES]
        columns.append(a)
    a = jnp.concatenate(columns, 1)
    return a * live_ref[...].astype(jnp.float32)


def rim_row(from_left, from_right, rim):
    lane = iota(from_left.shape, 1)
    low = jnp.where(lane < rim, from_right, 0.0)
    return jnp.where((lane >= rim) & (lane < 2 * rim), pltpu.roll(from_left, 64, 1), low)


def arrivals(left, right, rim):
    lane = iota((2, LANES), 1)
    head = jnp.where(lane < rim, left, 0.0)
    return head, jnp.where(lane >= LANES - rim, pltpu.roll(right, 64, 1), 0.0)


def by_side(even_ref, via_odd, via_even):
    even = even_ref[0 : via_odd.shape[0], :] > 0.5
    return jnp.where(even, via_odd, via_even), jnp.where(even, via_even, via_odd)


def load_table(table_ref, edges_ref):
    blocks = edges_ref.shape[1] // LANES
    for h in range(blocks):
        table_ref[2 * h : 2 * h + 2, :] = edges_ref[:, h * LANES : (h + 1) * LANES]
    rest = table_ref.shape[0] - 2 * blocks
    table_ref[2 * blocks :, :] = jnp.zeros((rest, LANES), jnp.float32)


def table_groups(table_ref):
    return [table_ref[8 * g : 8 * g + 8, :] for g in range(table_ref.shape[0] // 8)]


def stage_kernel(rim, count_in, *refs):
    sources, (staged, rest) = refs[:count_in], (refs[count_in : 2 * count_in], refs[2 * count_in :])
    by_moment_ref, y_ref, hot_ref, table_ref, sems = rest
    x_ref, inner_ref, edges_ref, live_ref, matrix_ref, projection_ref = staged[:6]
    copies = [
        pltpu.make_async_copy(source, target, sems.at[i])
        for i, (source, target) in enumerate(zip(sources, staged))
    ]
    for copy in copies:
        copy.start()
    for copy in copies[:4]:
        copy.wait()
    edge_count = x_ref.shape[1]
    count = inner_ref.shape[1]
    load_table(table_ref, x_ref)
    places = edge_places(edges_ref, rim, edge_count + 2 * rim)
    tall = iota((LANES, count), 0)
    for k, (_, low, _) in enumerate(places):
        hot = jnp.transpose(jnp.where(tall == low, 1.0, 0.0))
        hot_ref[k * count : (k + 1) * count, :] = hot.astype(jnp.bfloat16)
    highs = row_highs(edge_count // LANES)
    u = gather_moments(table_groups(table_ref), highs, inner_ref[...], places)
    for copy in copies[4:]:
        copy.wait()
    y_ref[...] = apply_matrix(matrix_ref, live_ref, u)
    by_moment_ref[...] = jnp.zeros(by_moment_ref.shape, jnp.float32)
    for n in range(projection_ref.shape[0]):
        for at in range(0, count, LANES):
            rows = pl.ds(at // 2 + n, 8, stride=8)
            by_moment_ref[rows, :] = projection_ref[n, :, at : at + LANES]


def end_columns(place, blocks, rim):
    high, low, _ = place
    owned = jnp.where((high == blocks - 1) & (low >= LANES - rim), low, -1)
    owned = jnp.where((high == 0) & (low < rim), low + 2 * rim, owned)
    return jnp.where(high == blocks, low, owned)


def couple_kernel(rim, edge_count, even_ref, edges_ref, live_ref, matrix_ref, out_ref):
    blocks = edge_count // LANES
    count = live_ref.shape[1]
    places = edge_places(edges_ref, rim, edge_count + 2 * rim)
    columns = [end_columns(place, blocks, rim) for place in places]
    live = live_ref[...].astype(jnp.float32)
    wide = iota((8, count), 0)
    signs = jnp.ones((8, count), jnp.float32)
    for k, (_, _, flip) in enumerate(places):
        signs = jnp.where(wide == 2 * k, flip, signs)
    tall = iota((LANES, count), 0)
    row = iota((rim, count), 0)
    shift = jnp.where(even_ref[0:1, :] > 0.5, rim, 0)
    shift = jnp.concatenate([shift] * (count // LANES), 1)
    total = jnp.zeros((LANES, LANES), jnp.float32)
    for k in range(3):
        rows = []
        for c in range(2):
            j = 2 * k + c
            weights = matrix_ref[j] * signs * (signs[j : j + 1] * live)
            for d in range(2):
                block = jnp.zeros((rim, count), jnp.float32)
                for m in range(3):
                    weight = weights[2 * m + d : 2 * m + d + 1]
                    block = block + jnp.where(row == columns[m] - shift, weight, 0.0)
                rows.append(block)
        rows = jnp.concatenate(rows, 0)
        coarse = rows.astype(jnp.bfloat16)
        fine = (rows - coarse.astype(jnp.float32)).astype(jnp.bfloat16)
        hot = jnp.where(tall == columns[k], 1.0, 0.0).astype(jnp.bfloat16)
        for piece in (coarse, fine):
            total = total + lax.dot_general(
                hot, piece, (((1,), (1,)), ((), ())), preferred_element_type=jnp.float32
            )
    out_ref[...] = total


def residual_kernel(
    rim, even_ref, via_odd_ref, via_even_ref, own_ref, b_ref, w_ref, edges_ref, live_ref,
    matrix_ref, hot_ref, coupling_ref, y_ref, ends_ref, odd_ref, even_out_ref,
):
    edge_count = b_ref.shape[1]
    blocks = edge_count // LANES
    count = own_ref.shape[1]
    tail = slice(edge_count - LANES, edge_count)
    left, _ = by_side(even_ref, via_odd_ref[:, tail], via_even_ref[:, tail])
    _, right = by_side(even_ref, via_odd_ref[:, :LANES], via_even_ref[:, :LANES])
    none = jnp.zeros((2, LANES), jnp.float32)
    change = jnp.concatenate([none, none, rim_row(left, right, rim), none], 0)
    places = edge_places(edges_ref, rim, edge_count + 2 * rim)
    highs = end_highs(blocks)
    u = gather_moments([change], highs, jnp.zeros((2, count), jnp.float32), places)
    y = own_ref[...] + apply_matrix(matrix_ref, live_ref, u)
    y_ref[...] = y
    ends = scatter_moments(y, places, hot_ref, highs)
    ends_ref[...] = ends
    to_left = jnp.concatenate([ends[0:2], ends[4:6], b_ref[:, :LANES], w_ref[:, :LANES]], 0)
    to_right = jnp.concatenate([ends[2:4], ends[4:6], b_ref[:, tail], w_ref[:, tail]], 0)
    odd_ref[0:8, :], even_out_ref[...] = by_side(even_ref, to_left, to_right)
    odd_ref[8:, :] = coupling_ref[...]


def spread_lists(lists_ref, nodes_ref):
    peers = nodes_ref.shape[0]
    cap = lists_ref.shape[0] * LANES // peers
    period = math.lcm(cap, LANES) // cap
    rows = period * cap // LANES
    lane = iota((peers // period, LANES), 1)
    for d in range(period):
        row, shift = divmod(d * cap, LANES)
        back = (LANES - shift) % LANES
        found = lists_ref[pl.ds(row, peers // period, stride=rows), :]
        if shift:
            found = pltpu.roll(found, back, 1)
        if shift + cap > LANES:
            more = lists_ref[pl.ds(row + 1, peers // period, stride=rows), :]
            found = jnp.where(lane < back, found, pltpu.roll(more, back, 1))
        nodes_ref[pl.ds(d, peers // period, stride=period), :] = found


def partial_kernel(
    rim, y_ref, b_ref, b_inner_ref, edges_ref, live_ref, projection_ref, hot_ref, lists_ref,
    inverse_ref, r_ref, r_inner_ref, a_ref, slots_ref, parts_ref, nodes_ref,
):
    edge_count = b_ref.shape[1]
    blocks = edge_count // LANES
    places = edge_places(edges_ref, rim, edge_count + 2 * rim)
    highs = row_highs(blocks)
    load_table(r_ref, b_ref)
    total = scatter_moments(y_ref[...], places, hot_ref, highs)
    row = iota(total.shape, 0)
    r_ref[...] = r_ref[...] - jnp.where(row < 2 * blocks, total, 0.0)
    r_inner = b_inner_ref[...] - y_ref[6:8, :]
    r_inner_ref[...] = r_inner
    u = gather_moments(table_groups(r_ref), highs, r_inner, places)
    a_ref[...] = restrict(projection_ref, live_ref, u)
    spread_lists(lists_ref, nodes_ref)
    place = nodes_ref[...] & (LANES - 1)
    tall = iota((LANES, LANES), 0)
    for d in range(nodes_ref.shape[0]):
        hot = jnp.transpose(jnp.where(tall == place[d : d + 1], 1.0, 0.0))
        slots_ref[d * LANES : (d + 1) * LANES, :] = hot.astype(jnp.bfloat16)
    size = inverse_ref.shape[1]
    for b in range(inverse_ref.shape[0]):
        coarse = inverse_ref[b].astype(jnp.bfloat16)
        fine = (inverse_ref[b] - coarse.astype(jnp.float32)).astype(jnp.bfloat16)
        parts_ref[:size, b * size : (b + 1) * size] = coarse
        parts_ref[size:, b * size : (b + 1) * size] = fine


def restrict_kernel(
    rim, edge_count, even_ref, via_odd_ref, via_even_ref, ends_ref, exists_ref, part_ref, a_ref,
    edges_ref, live_ref, projection_ref, counts_ref, r_ref, s_rim_ref, packed_ref, vals_ref,
):
    blocks = edge_count // LANES
    count = a_ref.shape[1]
    left, right = by_side(even_ref, via_odd_ref[0:8, :], via_even_ref[...])
    head, tail = arrivals(left[2:4], right[2:4], rim)
    exists = exists_ref[...]
    settled = ends_ref[4:6, :] + rim_row(left[0:2], right[0:2], rim)
    r_rim = exists * (rim_row(left[4:6], right[4:6], rim) - settled)
    change = jnp.concatenate([-head, -tail, r_rim, jnp.zeros((2, LANES), jnp.float32)], 0)
    s_rim_ref[...] = rim_row(left[6:8], right[6:8], rim) * r_rim
    places = edge_places(edges_ref, rim, edge_count + 2 * rim)
    u = gather_moments(
        [change], end_highs(blocks), jnp.zeros((2, count), jnp.float32), places
    )
    a = a_ref[...] + restrict(projection_ref, live_ref, u)
    for k in range(3):
        vals_ref[:, k * count : (k + 1) * count] = a[2 * k : 2 * k + 2]
    vals_ref[:, 3 * count :] = jnp.zeros((2, LANES), jnp.float32)
    lane = iota((2, LANES), 1)
    start = jnp.int32(0)
    for q in range(packed_ref.shape[0]):
        amount = counts_ref[0, q]
        shift = start & (LANES - 1)
        base = pl.multiple_of(start - shift, LANES)
        back = (LANES - shift) & (LANES - 1)
        first = pltpu.roll(vals_ref[:, pl.ds(base, LANES)], back, 1)
        second = pltpu.roll(vals_ref[:, pl.ds(base + LANES, LANES)], back, 1)
        chosen = jnp.where(lane < LANES - shift, first, second)
        packed_ref[q] = jnp.where(lane < amount, chosen, 0.0)
        start = start + amount
    r_ref[...] = part_ref[...]
    last = 2 * blocks - 2
    r_ref[0:2, :] = r_ref[0:2, :] - head
    r_ref[last : last + 2, :] = r_ref[last : last + 2, :] - tail


def solve_kernel(arrived_ref, nodes_ref, slots_ref, parts_ref, out_ref):
    peers, agg = nodes_ref.shape[0], parts_ref.shape[0] // 4
    groups = parts_ref.shape[1] // (2 * agg)
    row = iota((8, LANES), 0)
    half = nodes_ref[...] >> 7
    total = jnp.zeros((8, LANES), jnp.float32)
    span = 16
    for first in range(0, peers, span):
        spread = []
        for d in range(first, first + span):
            value = jnp.where(
                (row & 2) == 0,
                jnp.broadcast_to(arrived_ref[2 * d : 2 * d + 1, :], (8, LANES)),
                jnp.broadcast_to(arrived_ref[2 * d + 1 : 2 * d + 2, :], (8, LANES)),
            )
            value = jnp.where((row & 1) == half[d : d + 1], value, 0.0)
            coarse = value.astype(jnp.bfloat16).astype(jnp.float32)
            spread.append(jnp.where(row < 4, coarse, value - coarse))
        total = total + lax.dot_general(
            jnp.concatenate(spread, 1).astype(jnp.bfloat16),
            slots_ref[first * LANES : (first + span) * LANES, :],
            (((1,), (0,)), ((), ())), preferred_element_type=jnp.float32,
        )
    g = total + pltpu.roll(total, 4, 0)
    other = pltpu.roll(g, 2, 0)
    low = iota((8, LANES), 1) < agg
    evens = jnp.where(low, g, pltpu.roll(other, agg, 1))
    odds = jnp.where(low, pltpu.roll(g, agg, 1), other)
    vectors = jnp.where(row < 2, evens, pltpu.roll(odds, 2, 0))
    coarse = vectors.astype(jnp.bfloat16).astype(jnp.float32)
    fine = vectors - coarse
    sides = jnp.concatenate(
        [jnp.concatenate([coarse, coarse], 1), jnp.concatenate([fine, jnp.zeros_like(fine)], 1)], 0
    ).astype(jnp.bfloat16)
    solved = lax.dot_general(
        sides, parts_ref[...], (((1,), (0,)), ((), ())), preferred_element_type=jnp.float32
    )
    solved = solved[:8] + solved[8:]
    tables = [
        jnp.broadcast_to(solved[at : at + 1, b * LANES : (b + 1) * LANES], (8, LANES))
        for b, at in enumerate((0, 2, 1, 3)[:groups])
    ]
    for first in range(0, peers, 8):
        here = nodes_ref[first : first + 8, :]
        owner, place = here >> 6, here & (agg - 1)
        for c in range(2):
            found = jnp.zeros((8, LANES), jnp.float32)
            for b in range(groups):
                picked = jnp.take_along_axis(tables[b], place + c * agg, axis=1)
                found = jnp.where(owner == b, picked, found)
            out_ref[pl.ds(2 * first + c, 8, stride=2), :] = found


def prolong_kernel(
    rim, edge_count, even_ref, returned_ref, edges_ref, live_ref, projection_ref, counts_ref,
    hot_ref, p_ref, ends_ref, odd_ref, even_out_ref, vals_ref,
):
    count = live_ref.shape[1]
    lane = iota((2, LANES), 1)
    start = jnp.int32(0)
    for q in range(returned_ref.shape[0]):
        shift = start & (LANES - 1)
        base = pl.multiple_of(start - shift, LANES)
        moved = pltpu.roll(returned_ref[q], shift, 1)
        here = pl.ds(base, LANES)
        pltpu.store(vals_ref.at[:, here], moved, mask=lane >= shift)
        vals_ref[:, pl.ds(base + LANES, LANES)] = moved
        start = start + counts_ref[0, q]
    nodal = jnp.concatenate([vals_ref[:, k * count : (k + 1) * count] for k in range(3)], 0)
    p = projection_ref[0] * nodal[0:1]
    for n in range(1, 6):
        p = p + projection_ref[n] * nodal[n : n + 1]
    p = p * live_ref[...].astype(jnp.float32)
    p_ref[...] = p
    places = edge_places(edges_ref, rim, edge_count + 2 * rim)
    ends = scatter_moments(p, places, hot_ref, end_highs(edge_count // LANES))
    ends_ref[...] = ends
    to_left = jnp.concatenate([ends[0:2], ends[4:6]], 0)
    to_right = jnp.concatenate([ends[2:4], ends[4:6]], 0)
    odd_ref[...], even_out_ref[...] = by_side(even_ref, to_left, to_right)


def smooth_kernel(
    rim, p_ref, r_ref, r_inner_ref, inner_ref, w_ref, w_inner_ref, edges_ref, live_ref,
    matrix_ref, hot_ref, ends_ref, exists_ref, s_rim_ref, z_ref, x1_inner_ref, y_ref,
):
    edge_count = w_ref.shape[1]
    blocks = edge_count // LANES
    places = edge_places(edges_ref, rim, edge_count + 2 * rim)
    highs = row_highs(blocks)
    total = scatter_moments(p_ref[...], places, hot_ref, highs)
    row = iota(total.shape, 0)
    load_table(z_ref, w_ref)
    z_ref[...] = z_ref[...] * r_ref[...] + jnp.where(row < 2 * blocks, total, 0.0)
    rims = slice(2 * blocks, 2 * blocks + 2)
    z_ref[rims, :] = s_rim_ref[...] + exists_ref[...] * ends_ref[4:6, :]
    z_inner = w_inner_ref[...] * r_inner_ref[...] + p_ref[6:8, :]
    x1_inner_ref[...] = inner_ref[...] + z_inner
    u = gather_moments(table_groups(z_ref), highs, z_inner, places)
    y_ref[...] = apply_matrix(matrix_ref, live_ref, u)


def update_kernel(
    rim, edge_count, from_odd, via_ref, even_ref, exists_ref, part_ref, edges_ref, live_ref,
    matrix_ref, hot_ref, before_ref, y_ref, change_ref, rims_ref,
):
    count = part_ref.shape[1]
    via = via_ref[...]
    none = jnp.zeros_like(via)
    sides = (via, none) if from_odd else (none, via)
    left, right = by_side(even_ref, *sides)
    head, tail = arrivals(left[2:4], right[2:4], rim)
    z_rim = exists_ref[...] * rim_row(left[0:2], right[0:2], rim)
    change = jnp.concatenate([head, tail, z_rim, jnp.zeros((2, LANES), jnp.float32)], 0)
    change_ref[...] = before_ref[...] + change
    places = edge_places(edges_ref, rim, edge_count + 2 * rim)
    highs = end_highs(edge_count // LANES)
    u = gather_moments([change], highs, jnp.zeros((2, count), jnp.float32), places)
    y = part_ref[...] + apply_matrix(matrix_ref, live_ref, u)
    y_ref[...] = y
    rims = scatter_moments(y, places, hot_ref, highs)[4:6]
    rims_ref[0:2, :] = rims
    if rims_ref.shape[0] > 2:
        rims_ref[2:, :] = jnp.zeros((rims_ref.shape[0] - 2, LANES), jnp.float32)


def partner_part(rim, even_ref, ends_ref, coupling):
    ends = ends_ref[...]
    lane = iota((2, LANES), 1)
    even = even_ref[0:2, :] > 0.5
    turned = pltpu.roll(ends[4:6], 64, 1)
    for_low = jnp.where(lane < rim, ends[0:2], jnp.where(lane >= 3 * rim, turned, 0.0))
    for_high = jnp.where(lane < 2 * rim, pltpu.roll(ends[2:4], 64, 1), turned)
    for_high = jnp.where((lane >= rim) & (lane < 3 * rim), for_high, 0.0)
    change = jnp.where(even, for_low, for_high)
    rows = jnp.concatenate([change, jnp.zeros((6, LANES), jnp.float32)], 0)
    found = lax.dot_general(
        rows, coupling, (((1,), (0,)), ((), ())),
        precision=lax.Precision.HIGHEST, preferred_element_type=jnp.float32,
    )
    found = found[0:1] + pltpu.roll(found[1:2], 64, 1)
    head = jnp.concatenate([found, pltpu.roll(found, LANES - rim, 1)], 0)
    tail = pltpu.roll(head, LANES - rim, 1)
    head = jnp.where(even & (lane < rim), head, 0.0)
    return head, jnp.where(even | (lane < LANES - rim), 0.0, tail)


def output_kernel(
    rim, y_ref, change_ref, z_ref, r_ref, r_inner_ref, x_ref, edges_ref, hot_ref, even_ref,
    ends_ref, odd_before_ref, x1_ref, r1_ref, r1_inner_ref,
):
    edge_count = x_ref.shape[1]
    blocks = edge_count // LANES
    places = edge_places(edges_ref, rim, edge_count + 2 * rim)
    total = scatter_moments(y_ref[...], places, hot_ref, row_highs(blocks))
    r1_inner_ref[...] = r_inner_ref[...] - y_ref[6:8, :]
    head, tail = partner_part(rim, even_ref, ends_ref, odd_before_ref[8:, :])
    for h in range(blocks):
        here = slice(h * LANES, (h + 1) * LANES)
        rows = slice(2 * h, 2 * h + 2)
        z = z_ref[rows, :]
        r1 = r_ref[rows, :] - total[rows]
        if h == 0:
            z, r1 = z + change_ref[0:2, :], r1 - head
        if h == blocks - 1:
            z, r1 = z + change_ref[2:4, :], r1 - tail
        x1_ref[:, here] = x_ref[:, here] + z
        r1_ref[:, here] = r1


def finish_kernel(rim, even_ref, part_ref, via_odd_ref, via_even_ref, r1_ref):
    edge_count = part_ref.shape[1]
    left, right = by_side(even_ref, via_odd_ref[0:2, :], via_even_ref[...])
    head, tail = arrivals(left, right, rim)
    last = slice(edge_count - LANES, edge_count)
    r1_ref[...] = part_ref[...]
    r1_ref[:, :LANES] = part_ref[:, :LANES] - head
    r1_ref[:, last] = part_ref[:, last] - tail


def local_call(kernel, outs, in_place=False, scratch=(), sems=0, flops=10**8, name=None):
    def call(*args):
        spaces = [pltpu.HBM if in_place else pltpu.VMEM] * len(args)
        shapes = [
            jax.ShapeDtypeStruct(*(o if isinstance(o[0], tuple) else (o, jnp.float32)))
            for o in outs
        ]
        extra = [pltpu.SemaphoreType.DMA((sems,))] if sems else []
        return pl.pallas_call(
            kernel,
            out_shape=shapes,
            in_specs=[pl.BlockSpec(memory_space=space) for space in spaces],
            out_specs=[pl.BlockSpec(memory_space=pltpu.VMEM)] * len(outs),
            scratch_shapes=[pltpu.VMEM(s, jnp.float32) for s in scratch] + extra,
            compiler_params=pltpu.CompilerParams(vmem_limit_bytes=VMEM_LIMIT),
            cost_estimate=pl.CostEstimate(
                flops=flops, bytes_accessed=flops // 50, transcendentals=0
            ),
            name=name,
        )(*args)

    return call


def swap(message, first):
    axis = ("grp", "dom")
    lows = range(first, lax.axis_size(axis) - 1, 2)
    pairs = [(i, i + 1) for i in lows] + [(i + 1, i) for i in lows]
    return lax.ppermute(message, axis, pairs)


def shards(
    x_edges,
    x_inner,
    b_edges,
    b_inner,
    w_edges,
    w_inner,
    elem_edges,
    element_live,
    elem_matrix,
    projection,
    owner_counts,
    aux_node,
    aux_inverse,
):
    edge_count = x_edges.shape[1]
    elem_count = x_inner.shape[1]
    rim = elem_count // 32
    peers = owner_counts.shape[1]
    rows = -(-2 * (edge_count // LANES + 1) // 8) * 8
    live = element_live.reshape(1, elem_count)
    strip = lax.axis_index(("grp", "dom"))
    even = jnp.where(strip % 2 == 0, jnp.ones((8, LANES), jnp.float32), 0.0)
    lane = iota((2, LANES), 1)
    is_last = strip == lax.axis_size(("grp", "dom")) - 1
    exists = jnp.where(lane < rim, jnp.where(is_last, 0.0, 1.0), jnp.where(strip == 0, 0.0, 1.0))
    exists = jnp.where(lane < 2 * rim, exists, 0.0)
    via_even = swap(x_edges, 0)
    via_odd = swap(x_edges, 1)
    table = (rows, LANES)
    group = (8, LANES)
    inner = (2, elem_count)
    moments = (8, elem_count)
    slots = (peers, 2, LANES)
    hots = ((3 * elem_count, LANES), jnp.bfloat16)
    lists = (2, 3 * elem_count + LANES)

    arguments = (
        x_edges, x_inner, elem_edges, live, elem_matrix, jnp.transpose(projection, (1, 0, 2)),
        b_edges, b_inner, w_edges, w_inner, aux_inverse, owner_counts,
        aux_node.reshape(-1, LANES),
    )
    *staged, by_moment, own, hot = local_call(
        functools.partial(stage_kernel, rim, len(arguments)),
        [(v.shape, v.dtype) for v in arguments] + [(elem_count // 2, LANES), moments, hots],
        in_place=True, scratch=[table], sems=len(arguments), name="stage",
    )(*[pltpu.with_memory_space_constraint(v, pltpu.HBM) for v in arguments])
    x_edges, x_inner, elem_edges, live, elem_matrix, nodal_first = staged[:6]
    b_edges, b_inner, w_edges, w_inner, aux_inverse, owner_counts, aux_node = staged[6:]
    (coupling,) = local_call(
        functools.partial(couple_kernel, rim, edge_count), [(LANES, LANES)], name="couple"
    )(even, elem_edges, live, elem_matrix)
    y, ends, odd_out, even_out = local_call(
        functools.partial(residual_kernel, rim), [moments, group, (8 + LANES, LANES), group],
        name="residual",
    )(
        even, via_odd, via_even, own, b_edges, w_edges, elem_edges, live, elem_matrix, hot, coupling
    )
    via_even = swap(even_out, 0)
    odd_before = swap(odd_out, 1)
    size = aux_inverse.shape[1]
    r, r_inner, a, slots_hot, parts, nodes = local_call(
        functools.partial(partial_kernel, rim),
        [
            table, inner, moments, ((peers * LANES, LANES), jnp.bfloat16),
            ((2 * size, aux_inverse.shape[0] * size), jnp.bfloat16), ((peers, LANES), jnp.int32),
        ],
        name="partial",
    )(
        y, b_edges, b_inner, elem_edges, live, by_moment, hot, aux_node, aux_inverse
    )
    r, s_rim, packed = local_call(
        functools.partial(restrict_kernel, rim, edge_count), [table, (2, LANES), slots],
        scratch=[lists], name="restrict",
    )(
        even, odd_before, via_even, ends, exists, r, a, elem_edges, live, by_moment, owner_counts
    )
    arrived = lax.all_to_all(packed, "dom", split_axis=0, concat_axis=0, tiled=True)
    (outgoing,) = local_call(solve_kernel, [(2 * peers, LANES)], name="solve")(
        arrived.reshape(2 * peers, LANES), nodes, slots_hot, parts
    )
    outgoing = outgoing.reshape(slots)
    returned = lax.all_to_all(outgoing, "dom", split_axis=0, concat_axis=0, tiled=True)
    p, ends, odd_out, even_out = local_call(
        functools.partial(prolong_kernel, rim, edge_count),
        [moments, group, (4, LANES), (4, LANES)], scratch=[lists], name="prolong",
    )(even, returned, elem_edges, live, nodal_first, owner_counts, hot)
    via_even = swap(even_out, 0)
    via_odd = swap(odd_out, 1)
    z, x1_inner, az = local_call(
        functools.partial(smooth_kernel, rim), [table, inner, moments], name="smooth"
    )(
        p, r, r_inner, x_inner, w_edges, w_inner, elem_edges, live, elem_matrix, hot, ends, exists,
        s_rim,
    )
    shared = (even, exists)
    element = (elem_edges, live, elem_matrix, hot)
    az, change, rims = local_call(
        functools.partial(update_kernel, rim, edge_count, False),
        [moments, group, (8, LANES)], name="update_even",
    )(via_even, *shared, az, *element, jnp.zeros(group, jnp.float32))
    rims_odd = swap(rims, 1)
    az, change, rims = local_call(
        functools.partial(update_kernel, rim, edge_count, True),
        [moments, group, (2, LANES)], flops=10**10, name="update_odd",
    )(via_odd, *shared, az, *element, change)
    rims_even = swap(rims, 0)
    x1_edges, r1_part, r1_inner = local_call(
        functools.partial(output_kernel, rim), [x_edges.shape, x_edges.shape, inner],
        flops=10**4, name="output",
    )(az, change, z, r, r_inner, x_edges, elem_edges, hot, even, ends, odd_before)
    (r1_edges,) = local_call(
        functools.partial(finish_kernel, rim), [x_edges.shape], name="finish"
    )(even, r1_part, rims_odd, rims_even)
    return x1_edges, x1_inner, r1_edges, r1_inner


def solution(mesh):
    edges = P(None, ("grp", "dom"))
    in_specs = (edges,) * 7 + (
        P(("grp", "dom")),
        P(None, None, ("grp", "dom")),
        P(None, None, ("grp", "dom")),
        P(("grp", "dom"), None),
        P(("grp", "dom")),
        P(("grp", "dom"), None, None),
    )
    return jax.shard_map(
        shards, mesh=mesh, in_specs=in_specs, out_specs=(edges,) * 4, check_vma=False
    )
```

```python
import functools
import math

import jax
import jax.numpy as jnp
from jax import lax
from jax.experimental import pallas as pl
from jax.experimental.pallas import tpu as pltpu
from jax.sharding import PartitionSpec as P

LANES = 128
VMEM_LIMIT = 24 * 2**20


def iota(shape, dim):
    return lax.broadcasted_iota(jnp.int32, shape, dim)


def edge_places(edges_ref, rim, width):
    places = []
    for k in range(3):
        coded = edges_ref[k : k + 1, :]
        flip = (1 - 2 * (coded & 1)).astype(jnp.float32)
        place = (coded >> 1) - rim
        place = jnp.where(place < 0, place + width, place)
        places.append((place >> 7, place & (LANES - 1), flip))
    return places


def row_highs(blocks):
    row = iota((8, LANES), 0)
    return [4 * g + (row >> 1) for g in range(-(-(blocks + 1) // 4))]


def end_highs(blocks):
    row = iota((8, LANES), 0)
    rims = jnp.where(row < 6, blocks, -1)
    return [jnp.where(row < 2, 0, jnp.where(row < 4, blocks - 1, rims))]


def widen(mask_rows, count):
    return jnp.concatenate([mask_rows] * (count // LANES), 1)


def gather_moments(groups, highs, inner, places):
    count = inner.shape[1]
    wide = iota((8, count), 0)
    total = jnp.concatenate([jnp.zeros((6, count), jnp.float32), inner], 0)
    for k, (high, low, flip) in enumerate(places):
        columns = []
        for at in range(0, count, LANES):
            low_b = jnp.broadcast_to(low[:, at : at + LANES], (8, LANES))
            high_b = jnp.broadcast_to(high[:, at : at + LANES], (8, LANES))
            found = jnp.zeros((8, LANES), jnp.float32)
            for group, at_high in zip(groups, highs):
                picked = jnp.take_along_axis(group, low_b, axis=1)
                found = found + jnp.where(high_b == at_high, picked, 0.0)
            found = found + pltpu.roll(found, 4, 0)
            columns.append(found + pltpu.roll(found, 2, 0))
        found = jnp.concatenate(columns, 1)
        found = found * jnp.where(wide == 2 * k, flip, 1.0)
        total = jnp.where((wide >> 1) == k, found, total)
    return total


def scatter_moments(values, places, hot_ref, highs):
    count = values.shape[1]
    rows = 8 * len(highs)
    wide = iota((8, count), 0)
    total = jnp.zeros((2 * rows, LANES), jnp.float32)
    for k, (high, low, flip) in enumerate(places):
        part = jnp.where((wide >> 1) == k, values, 0.0)
        part = part * jnp.where(wide == 2 * k, flip, 1.0)
        part = part + pltpu.roll(part, 4, 0)
        part = part + pltpu.roll(part, 2, 0)
        coarse = part.astype(jnp.bfloat16).astype(jnp.float32)
        spread = []
        for piece in (coarse, part - coarse):
            for at_high in highs:
                spread.append(jnp.where(high == widen(at_high, count), piece, 0.0))
        spread = jnp.concatenate(spread, 0).astype(jnp.bfloat16)
        total = total + lax.dot_general(
            spread, hot_ref[k * count : (k + 1) * count, :], (((1,), (0,)), ((), ())),
            preferred_element_type=jnp.float32,
        )
    return total[:rows] + total[rows:]


def apply_matrix(matrix_ref, live_ref, u):
    y = matrix_ref[0] * u[0:1]
    for j in range(1, 8):
        y = y + matrix_ref[j] * u[j : j + 1]
    return y * live_ref[...].astype(jnp.float32)


def restrict(projection_ref, live_ref, u):
    columns = []
    for at in range(0, u.shape[1], LANES):
        first = at // 2
        a = projection_ref[first : first + 8, :] * u[0:1, at : at + LANES]
        for m in range(1, 8):
            rows = slice(first + 8 * m, first + 8 * m + 8)
            a = a + projection_ref[rows, :] * u[m : m + 1, at : at + LANES]
        columns.append(a)
    a = jnp.concatenate(columns, 1)
    return a * live_ref[...].astype(jnp.float32)


def rim_row(from_left, from_right, rim):
    lane = iota(from_left.shape, 1)
    low = jnp.where(lane < rim, from_right, 0.0)
    return jnp.where((lane >= rim) & (lane < 2 * rim), pltpu.roll(from_left, 64, 1), low)


def arrivals(left, right, rim):
    lane = iota((2, LANES), 1)
    head = jnp.where(lane < rim, left, 0.0)
    return head, jnp.where(lane >= LANES - rim, pltpu.roll(right, 64, 1), 0.0)


def by_side(even_ref, via_odd, via_even):
    even = even_ref[0 : via_odd.shape[0], :] > 0.5
    return jnp.where(even, via_odd, via_even), jnp.where(even, via_even, via_odd)


def load_table(table_ref, edges_ref):
    blocks = edges_ref.shape[1] // LANES
    for h in range(blocks):
        table_ref[2 * h : 2 * h + 2, :] = edges_ref[:, h * LANES : (h + 1) * LANES]
    rest = table_ref.shape[0] - 2 * blocks
    table_ref[2 * blocks :, :] = jnp.zeros((rest, LANES), jnp.float32)


def table_groups(table_ref):
    return [table_ref[8 * g : 8 * g + 8, :] for g in range(table_ref.shape[0] // 8)]


def stage_kernel(rim, count_in, *refs):
    sources, (staged, rest) = refs[:count_in], (refs[count_in : 2 * count_in], refs[2 * count_in :])
    by_moment_ref, y_ref, hot_ref, table_ref, sems = rest
    x_ref, inner_ref, edges_ref, live_ref, matrix_ref, projection_ref = staged[:6]
    copies = [
        pltpu.make_async_copy(source, target, sems.at[i])
        for i, (source, target) in enumerate(zip(sources, staged))
    ]
    for copy in copies:
        copy.start()
    for copy in copies[:4]:
        copy.wait()
    edge_count = x_ref.shape[1]
    count = inner_ref.shape[1]
    load_table(table_ref, x_ref)
    places = edge_places(edges_ref, rim, edge_count + 2 * rim)
    tall = iota((LANES, count), 0)
    for k, (_, low, _) in enumerate(places):
        hot = jnp.transpose(jnp.where(tall == low, 1.0, 0.0))
        hot_ref[k * count : (k + 1) * count, :] = hot.astype(jnp.bfloat16)
    highs = row_highs(edge_count // LANES)
    u = gather_moments(table_groups(table_ref), highs, inner_ref[...], places)
    for copy in copies[4:]:
        copy.wait()
    y_ref[...] = apply_matrix(matrix_ref, live_ref, u)
    by_moment_ref[...] = jnp.zeros(by_moment_ref.shape, jnp.float32)
    for n in range(projection_ref.shape[0]):
        for at in range(0, count, LANES):
            rows = pl.ds(at // 2 + n, 8, stride=8)
            by_moment_ref[rows, :] = projection_ref[n, :, at : at + LANES]


def residual_kernel(
    rim, via_first_ref, via_odd_ref, via_even_ref, even_ref, own_ref, b_ref, w_ref, edges_ref, live_ref,
    matrix_ref, hot_ref, y_ref, ends_ref, first_ref, odd_ref, even_out_ref,
):
    edge_count = b_ref.shape[1]
    blocks = edge_count // LANES
    count = own_ref.shape[1]
    tail = slice(edge_count - LANES, edge_count)
    head = slice(0, LANES)
    near_tail = via_first_ref[:, tail] + via_even_ref[:, tail]
    near_head = via_first_ref[:, head] + via_even_ref[:, head]
    left, _ = by_side(even_ref, via_odd_ref[:, tail], near_tail)
    _, right = by_side(even_ref, via_odd_ref[:, head], near_head)
    none = jnp.zeros((2, LANES), jnp.float32)
    change = jnp.concatenate([none, none, rim_row(left, right, rim), none], 0)
    places = edge_places(edges_ref, rim, edge_count + 2 * rim)
    highs = end_highs(blocks)
    u = gather_moments([change], highs, jnp.zeros((2, count), jnp.float32), places)
    y = own_ref[...] + apply_matrix(matrix_ref, live_ref, u)
    y_ref[...] = y
    ends = scatter_moments(y, places, hot_ref, highs)
    ends_ref[...] = ends
    to_left = jnp.concatenate([ends[0:2], ends[4:6], b_ref[:, :LANES], w_ref[:, :LANES]], 0)
    to_right = jnp.concatenate([ends[2:4], ends[4:6], b_ref[:, tail], w_ref[:, tail]], 0)
    odd_ref[...], even_out_ref[...] = by_side(even_ref, to_left, to_right)
    first_ref[...] = even_out_ref[...]


def spread_lists(lists_ref, nodes_ref):
    peers = nodes_ref.shape[0]
    cap = lists_ref.shape[0] * LANES // peers
    period = math.lcm(cap, LANES) // cap
    rows = period * cap // LANES
    lane = iota((peers // period, LANES), 1)
    for d in range(period):
        row, shift = divmod(d * cap, LANES)
        back = (LANES - shift) % LANES
        found = lists_ref[pl.ds(row, peers // period, stride=rows), :]
        if shift:
            found = pltpu.roll(found, back, 1)
        if shift + cap > LANES:
            more = lists_ref[pl.ds(row + 1, peers // period, stride=rows), :]
            found = jnp.where(lane < back, found, pltpu.roll(more, back, 1))
        nodes_ref[pl.ds(d, peers // period, stride=period), :] = found


def partial_kernel(
    rim, y_ref, b_ref, b_inner_ref, edges_ref, live_ref, projection_ref, hot_ref, lists_ref,
    inverse_ref, r_ref, r_inner_ref, a_ref, slots_ref, parts_ref, nodes_ref,
):
    edge_count = b_ref.shape[1]
    blocks = edge_count // LANES
    places = edge_places(edges_ref, rim, edge_count + 2 * rim)
    highs = row_highs(blocks)
    load_table(r_ref, b_ref)
    total = scatter_moments(y_ref[...], places, hot_ref, highs)
    row = iota(total.shape, 0)
    r_ref[...] = r_ref[...] - jnp.where(row < 2 * blocks, total, 0.0)
    r_inner = b_inner_ref[...] - y_ref[6:8, :]
    r_inner_ref[...] = r_inner
    u = gather_moments(table_groups(r_ref), highs, r_inner, places)
    a_ref[...] = restrict(projection_ref, live_ref, u)
    spread_lists(lists_ref, nodes_ref)
    place = nodes_ref[...] & (LANES - 1)
    tall = iota((LANES, LANES), 0)
    for d in range(nodes_ref.shape[0]):
        hot = jnp.transpose(jnp.where(tall == place[d : d + 1], 1.0, 0.0))
        slots_ref[d * LANES : (d + 1) * LANES, :] = hot.astype(jnp.bfloat16)
    size = inverse_ref.shape[1]
    for b in range(inverse_ref.shape[0]):
        coarse = inverse_ref[b].astype(jnp.bfloat16)
        fine = (inverse_ref[b] - coarse.astype(jnp.float32)).astype(jnp.bfloat16)
        parts_ref[:size, b * size : (b + 1) * size] = coarse
        parts_ref[size:, b * size : (b + 1) * size] = fine


def restrict_kernel(
    rim, edge_count, via_first_ref, via_odd_ref, via_even_ref, even_ref, ends_ref, exists_ref,
    part_ref, a_ref,
    edges_ref, live_ref, projection_ref, counts_ref, r_ref, s_rim_ref, packed_ref, vals_ref,
):
    blocks = edge_count // LANES
    count = a_ref.shape[1]
    via_near = via_first_ref[...] + via_even_ref[...]
    left, right = by_side(even_ref, via_odd_ref[...], via_near)
    head, tail = arrivals(left[2:4], right[2:4], rim)
    exists = exists_ref[...]
    settled = ends_ref[4:6, :] + rim_row(left[0:2], right[0:2], rim)
    r_rim = exists * (rim_row(left[4:6], right[4:6], rim) - settled)
    change = jnp.concatenate([-head, -tail, r_rim, jnp.zeros((2, LANES), jnp.float32)], 0)
    s_rim_ref[...] = rim_row(left[6:8], right[6:8], rim) * r_rim
    places = edge_places(edges_ref, rim, edge_count + 2 * rim)
    u = gather_moments(
        [change], end_highs(blocks), jnp.zeros((2, count), jnp.float32), places
    )
    a = a_ref[...] + restrict(projection_ref, live_ref, u)
    for k in range(3):
        vals_ref[:, k * count : (k + 1) * count] = a[2 * k : 2 * k + 2]
    vals_ref[:, 3 * count :] = jnp.zeros((2, LANES), jnp.float32)
    lane = iota((2, LANES), 1)
    start = jnp.int32(0)
    for q in range(packed_ref.shape[0]):
        amount = counts_ref[0, q]
        shift = start & (LANES - 1)
        base = pl.multiple_of(start - shift, LANES)
        back = (LANES - shift) & (LANES - 1)
        first = pltpu.roll(vals_ref[:, pl.ds(base, LANES)], back, 1)
        second = pltpu.roll(vals_ref[:, pl.ds(base + LANES, LANES)], back, 1)
        chosen = jnp.where(lane < LANES - shift, first, second)
        packed_ref[q] = jnp.where(lane < amount, chosen, 0.0)
        start = start + amount
    r_ref[...] = part_ref[...]
    last = 2 * blocks - 2
    r_ref[0:2, :] = r_ref[0:2, :] - head
    r_ref[last : last + 2, :] = r_ref[last : last + 2, :] - tail


def solve_kernel(arrived_ref, nodes_ref, slots_ref, parts_ref, out_ref):
    peers, agg = nodes_ref.shape[0], parts_ref.shape[0] // 4
    groups = parts_ref.shape[1] // (2 * agg)
    row = iota((8, LANES), 0)
    half = nodes_ref[...] >> 7
    total = jnp.zeros((8, LANES), jnp.float32)
    span = 16
    for first in range(0, peers, span):
        spread = []
        for d in range(first, first + span):
            value = jnp.where(
                (row & 2) == 0,
                jnp.broadcast_to(arrived_ref[2 * d : 2 * d + 1, :], (8, LANES)),
                jnp.broadcast_to(arrived_ref[2 * d + 1 : 2 * d + 2, :], (8, LANES)),
            )
            value = jnp.where((row & 1) == half[d : d + 1], value, 0.0)
            coarse = value.astype(jnp.bfloat16).astype(jnp.float32)
            spread.append(jnp.where(row < 4, coarse, value - coarse))
        total = total + lax.dot_general(
            jnp.concatenate(spread, 1).astype(jnp.bfloat16),
            slots_ref[first * LANES : (first + span) * LANES, :],
            (((1,), (0,)), ((), ())), preferred_element_type=jnp.float32,
        )
    g = total + pltpu.roll(total, 4, 0)
    other = pltpu.roll(g, 2, 0)
    low = iota((8, LANES), 1) < agg
    evens = jnp.where(low, g, pltpu.roll(other, agg, 1))
    odds = jnp.where(low, pltpu.roll(g, agg, 1), other)
    vectors = jnp.where(row < 2, evens, pltpu.roll(odds, 2, 0))
    coarse = vectors.astype(jnp.bfloat16).astype(jnp.float32)
    fine = vectors - coarse
    sides = jnp.concatenate(
        [jnp.concatenate([coarse, coarse], 1), jnp.concatenate([fine, jnp.zeros_like(fine)], 1)], 0
    ).astype(jnp.bfloat16)
    solved = lax.dot_general(
        sides, parts_ref[...], (((1,), (0,)), ((), ())), preferred_element_type=jnp.float32
    )
    solved = solved[:8] + solved[8:]
    tables = [
        jnp.broadcast_to(solved[at : at + 1, b * LANES : (b + 1) * LANES], (8, LANES))
        for b, at in enumerate((0, 2, 1, 3)[:groups])
    ]
    for first in range(0, peers, 8):
        here = nodes_ref[first : first + 8, :]
        owner, place = here >> 6, here & (agg - 1)
        for c in range(2):
            found = jnp.zeros((8, LANES), jnp.float32)
            for b in range(groups):
                picked = jnp.take_along_axis(tables[b], place + c * agg, axis=1)
                found = jnp.where(owner == b, picked, found)
            out_ref[pl.ds(2 * first + c, 8, stride=2), :] = found


def prolong_kernel(
    rim, edge_count, even_ref, returned_ref, edges_ref, live_ref, projection_ref, counts_ref,
    hot_ref, p_ref, ends_ref, odd_ref, even_out_ref, vals_ref,
):
    count = live_ref.shape[1]
    lane = iota((2, LANES), 1)
    start = jnp.int32(0)
    for q in range(returned_ref.shape[0]):
        shift = start & (LANES - 1)
        base = pl.multiple_of(start - shift, LANES)
        moved = pltpu.roll(returned_ref[q], shift, 1)
        here = pl.ds(base, LANES)
        pltpu.store(vals_ref.at[:, here], moved, mask=lane >= shift)
        vals_ref[:, pl.ds(base + LANES, LANES)] = moved
        start = start + counts_ref[0, q]
    nodal = jnp.concatenate([vals_ref[:, k * count : (k + 1) * count] for k in range(3)], 0)
    p = projection_ref[0] * nodal[0:1]
    for n in range(1, 6):
        p = p + projection_ref[n] * nodal[n : n + 1]
    p = p * live_ref[...].astype(jnp.float32)
    p_ref[...] = p
    places = edge_places(edges_ref, rim, edge_count + 2 * rim)
    ends = scatter_moments(p, places, hot_ref, end_highs(edge_count // LANES))
    ends_ref[...] = ends
    to_left = jnp.concatenate([ends[0:2], ends[4:6]], 0)
    to_right = jnp.concatenate([ends[2:4], ends[4:6]], 0)
    odd_ref[...], even_out_ref[...] = by_side(even_ref, to_left, to_right)


def smooth_kernel(
    rim, p_ref, r_ref, r_inner_ref, inner_ref, w_ref, w_inner_ref, edges_ref, live_ref,
    matrix_ref, hot_ref, z_ref, x1_inner_ref, y_ref,
):
    edge_count = w_ref.shape[1]
    blocks = edge_count // LANES
    places = edge_places(edges_ref, rim, edge_count + 2 * rim)
    highs = row_highs(blocks)
    total = scatter_moments(p_ref[...], places, hot_ref, highs)
    row = iota(total.shape, 0)
    load_table(z_ref, w_ref)
    z_ref[...] = z_ref[...] * r_ref[...] + jnp.where(row < 2 * blocks, total, 0.0)
    z_inner = w_inner_ref[...] * r_inner_ref[...] + p_ref[6:8, :]
    x1_inner_ref[...] = inner_ref[...] + z_inner
    u = gather_moments(table_groups(z_ref), highs, z_inner, places)
    y_ref[...] = apply_matrix(matrix_ref, live_ref, u)


def update_kernel(
    rim, edge_count, even_ref, via_odd_ref, via_even_ref, ends_ref, exists_ref, s_rim_ref,
    part_ref, edges_ref, live_ref, matrix_ref, hot_ref, y_ref, change_ref, odd_ref, even_out_ref,
):
    count = part_ref.shape[1]
    left, right = by_side(even_ref, via_odd_ref[...], via_even_ref[...])
    head, tail = arrivals(left[2:4], right[2:4], rim)
    settled = ends_ref[4:6, :] + rim_row(left[0:2], right[0:2], rim)
    z_rim = s_rim_ref[...] + exists_ref[...] * settled
    change = jnp.concatenate([head, tail, z_rim, jnp.zeros((2, LANES), jnp.float32)], 0)
    change_ref[...] = change
    places = edge_places(edges_ref, rim, edge_count + 2 * rim)
    highs = end_highs(edge_count // LANES)
    u = gather_moments([change], highs, jnp.zeros((2, count), jnp.float32), places)
    y = part_ref[...] + apply_matrix(matrix_ref, live_ref, u)
    y_ref[...] = y
    rims = scatter_moments(y, places, hot_ref, highs)[4:6]
    odd_ref[...] = rims
    even_out_ref[...] = rims


def output_kernel(
    rim, y_ref, change_ref, z_ref, r_ref, r_inner_ref, x_ref, edges_ref, hot_ref,
    x1_ref, r1_ref, r1_inner_ref,
):
    edge_count = x_ref.shape[1]
    blocks = edge_count // LANES
    places = edge_places(edges_ref, rim, edge_count + 2 * rim)
    total = scatter_moments(y_ref[...], places, hot_ref, row_highs(blocks))
    r1_inner_ref[...] = r_inner_ref[...] - y_ref[6:8, :]
    for h in range(blocks):
        here = slice(h * LANES, (h + 1) * LANES)
        rows = slice(2 * h, 2 * h + 2)
        z = z_ref[rows, :]
        if h == 0:
            z = z + change_ref[0:2, :]
        if h == blocks - 1:
            z = z + change_ref[2:4, :]
        x1_ref[:, here] = x_ref[:, here] + z
        r1_ref[:, here] = r_ref[rows, :] - total[rows]


def finish_kernel(rim, even_ref, part_ref, via_odd_ref, via_even_ref, r1_ref):
    edge_count = part_ref.shape[1]
    left, right = by_side(even_ref, via_odd_ref[...], via_even_ref[...])
    head, tail = arrivals(left, right, rim)
    last = slice(edge_count - LANES, edge_count)
    r1_ref[...] = part_ref[...]
    r1_ref[:, :LANES] = part_ref[:, :LANES] - head
    r1_ref[:, last] = part_ref[:, last] - tail


def local_call(kernel, outs, in_place=False, scratch=(), sems=0, name=None):
    def call(*args):
        spaces = [pltpu.HBM if in_place else pltpu.VMEM] * len(args)
        shapes = [
            jax.ShapeDtypeStruct(*(o if isinstance(o[0], tuple) else (o, jnp.float32)))
            for o in outs
        ]
        extra = [pltpu.SemaphoreType.DMA((sems,))] if sems else []
        return pl.pallas_call(
            kernel,
            out_shape=shapes,
            in_specs=[pl.BlockSpec(memory_space=space) for space in spaces],
            out_specs=[pl.BlockSpec(memory_space=pltpu.VMEM)] * len(outs),
            scratch_shapes=[pltpu.VMEM(s, jnp.float32) for s in scratch] + extra,
            compiler_params=pltpu.CompilerParams(vmem_limit_bytes=VMEM_LIMIT),
            cost_estimate=pl.CostEstimate(
                flops=10**8, bytes_accessed=2 * 10**6, transcendentals=0
            ),
            name=name,
        )(*args)

    return call


def swap(message, lows):
    pairs = [(i, i + 1) for i in lows] + [(i + 1, i) for i in lows]
    return lax.ppermute(message, ("grp", "dom"), pairs)


def shards(
    x_edges,
    x_inner,
    b_edges,
    b_inner,
    w_edges,
    w_inner,
    elem_edges,
    element_live,
    elem_matrix,
    projection,
    owner_counts,
    aux_node,
    aux_inverse,
):
    edge_count = x_edges.shape[1]
    elem_count = x_inner.shape[1]
    rim = elem_count // 32
    peers = owner_counts.shape[1]
    rows = -(-2 * (edge_count // LANES + 1) // 8) * 8
    live = element_live.reshape(1, elem_count)
    strip = lax.axis_index(("grp", "dom"))
    even = jnp.where(strip % 2 == 0, jnp.ones((8, LANES), jnp.float32), 0.0)
    lane = iota((2, LANES), 1)
    is_last = strip == lax.axis_size(("grp", "dom")) - 1
    exists = jnp.where(lane < rim, jnp.where(is_last, 0.0, 1.0), jnp.where(strip == 0, 0.0, 1.0))
    exists = jnp.where(lane < 2 * rim, exists, 0.0)
    strips, group_size = lax.axis_size(("grp", "dom")), lax.axis_size("dom")
    odd, evens = range(1, strips - 1, 2), range(0, strips - 1, 2)
    firsts = [i for i in evens if i % group_size == 0]
    others = [i for i in evens if i % group_size != 0]
    via_first = swap(x_edges, firsts)
    via_odd = swap(x_edges, odd)
    via_even = swap(x_edges, others)
    table = (rows, LANES)
    group = (8, LANES)
    inner = (2, elem_count)
    moments = (8, elem_count)
    slots = (peers, 2, LANES)
    hots = ((3 * elem_count, LANES), jnp.bfloat16)
    lists = (2, 3 * elem_count + LANES)

    arguments = (
        x_edges, x_inner, elem_edges, live, elem_matrix, jnp.transpose(projection, (1, 0, 2)),
        b_edges, b_inner, w_edges, w_inner, aux_inverse, owner_counts,
        aux_node.reshape(-1, LANES),
    )
    *staged, by_moment, own, hot = local_call(
        functools.partial(stage_kernel, rim, len(arguments)),
        [(v.shape, v.dtype) for v in arguments] + [(elem_count // 2, LANES), moments, hots],
        in_place=True, scratch=[table], sems=len(arguments), name="stage",
    )(*[pltpu.with_memory_space_constraint(v, pltpu.HBM) for v in arguments])
    x_edges, x_inner, elem_edges, live, elem_matrix, nodal_first = staged[:6]
    b_edges, b_inner, w_edges, w_inner, aux_inverse, owner_counts, aux_node = staged[6:]
    y, ends, first_out, odd_out, even_out = local_call(
        functools.partial(residual_kernel, rim), [moments, group, group, group, group],
        name="residual",
    )(
        via_first, via_odd, via_even, even, own, b_edges, w_edges, elem_edges, live, elem_matrix, hot
    )
    via_first = swap(first_out, firsts)
    via_odd = swap(odd_out, odd)
    via_even = swap(even_out, others)
    size = aux_inverse.shape[1]
    r, r_inner, a, slots_hot, parts, nodes = local_call(
        functools.partial(partial_kernel, rim),
        [
            table, inner, moments, ((peers * LANES, LANES), jnp.bfloat16),
            ((2 * size, aux_inverse.shape[0] * size), jnp.bfloat16), ((peers, LANES), jnp.int32),
        ],
        name="partial",
    )(
        y, b_edges, b_inner, elem_edges, live, by_moment, hot, aux_node, aux_inverse
    )
    r, s_rim, packed = local_call(
        functools.partial(restrict_kernel, rim, edge_count), [table, (2, LANES), slots],
        scratch=[lists], name="restrict",
    )(
        via_first, via_odd, via_even, even, ends, exists, r, a, elem_edges, live, by_moment, owner_counts
    )
    arrived = lax.all_to_all(packed, "dom", split_axis=0, concat_axis=0, tiled=True)
    (outgoing,) = local_call(solve_kernel, [(2 * peers, LANES)], name="solve")(
        arrived.reshape(2 * peers, LANES), nodes, slots_hot, parts
    )
    outgoing = outgoing.reshape(slots)
    returned = lax.all_to_all(outgoing, "dom", split_axis=0, concat_axis=0, tiled=True)
    p, ends, odd_out, even_out = local_call(
        functools.partial(prolong_kernel, rim, edge_count),
        [moments, group, (4, LANES), (4, LANES)], scratch=[lists], name="prolong",
    )(even, returned, elem_edges, live, nodal_first, owner_counts, hot)
    via_odd, via_even = swap(odd_out, odd), swap(even_out, evens)
    z, x1_inner, az = local_call(
        functools.partial(smooth_kernel, rim), [table, inner, moments], name="smooth"
    )(p, r, r_inner, x_inner, w_edges, w_inner, elem_edges, live, elem_matrix, hot)
    az, change, odd_out, even_out = local_call(
        functools.partial(update_kernel, rim, edge_count),
        [moments, group, (2, LANES), (2, LANES)], name="update",
    )(
        even, via_odd, via_even, ends, exists, s_rim, az, elem_edges, live, elem_matrix, hot
    )
    via_odd, via_even = swap(odd_out, odd), swap(even_out, evens)
    x1_edges, r1_part, r1_inner = local_call(
        functools.partial(output_kernel, rim), [x_edges.shape, x_edges.shape, inner],
        name="output",
    )(az, change, z, r, r_inner, x_edges, elem_edges, hot)
    (r1_edges,) = local_call(
        functools.partial(finish_kernel, rim), [x_edges.shape], name="finish"
    )(even, r1_part, via_odd, via_even)
    return x1_edges, x1_inner, r1_edges, r1_inner


def solution(mesh):
    edges = P(None, ("grp", "dom"))
    in_specs = (edges,) * 7 + (
        P(("grp", "dom")),
        P(None, None, ("grp", "dom")),
        P(None, None, ("grp", "dom")),
        P(("grp", "dom"), None),
        P(("grp", "dom")),
        P(("grp", "dom"), None, None),
    )
    return jax.shard_map(
        shards, mesh=mesh, in_specs=in_specs, out_specs=(edges,) * 4, check_vma=False
    )
```

```python
import functools
import math

import jax
import jax.numpy as jnp
from jax import lax
from jax.experimental import pallas as pl
from jax.experimental.pallas import tpu as pltpu
from jax.sharding import PartitionSpec as P

LANES = 128
VMEM_LIMIT = 24 * 2**20


def iota(shape, dim):
    return lax.broadcasted_iota(jnp.int32, shape, dim)


def edge_places(edges_ref, rim, width):
    places = []
    for k in range(3):
        coded = edges_ref[k : k + 1, :]
        flip = (1 - 2 * (coded & 1)).astype(jnp.float32)
        place = (coded >> 1) - rim
        place = jnp.where(place < 0, place + width, place)
        places.append((place >> 7, place & (LANES - 1), flip))
    return places


def row_highs(blocks):
    row = iota((8, LANES), 0)
    return [4 * g + (row >> 1) for g in range(-(-(blocks + 1) // 4))]


def end_highs(blocks):
    row = iota((8, LANES), 0)
    rims = jnp.where(row < 6, blocks, -1)
    return [jnp.where(row < 2, 0, jnp.where(row < 4, blocks - 1, rims))]


def widen(mask_rows, count):
    return jnp.concatenate([mask_rows] * (count // LANES), 1)


def gather_moments(groups, highs, inner, places):
    count = inner.shape[1]
    wide = iota((8, count), 0)
    total = jnp.concatenate([jnp.zeros((6, count), jnp.float32), inner], 0)
    for k, (high, low, flip) in enumerate(places):
        columns = []
        for at in range(0, count, LANES):
            low_b = jnp.broadcast_to(low[:, at : at + LANES], (8, LANES))
            high_b = jnp.broadcast_to(high[:, at : at + LANES], (8, LANES))
            found = jnp.zeros((8, LANES), jnp.float32)
            for group, at_high in zip(groups, highs):
                picked = jnp.take_along_axis(group, low_b, axis=1)
                found = found + jnp.where(high_b == at_high, picked, 0.0)
            found = found + pltpu.roll(found, 4, 0)
            columns.append(found + pltpu.roll(found, 2, 0))
        found = jnp.concatenate(columns, 1)
        found = found * jnp.where(wide == 2 * k, flip, 1.0)
        total = jnp.where((wide >> 1) == k, found, total)
    return total


def scatter_moments(values, places, hot_ref, highs):
    count = values.shape[1]
    rows = 8 * len(highs)
    wide = iota((8, count), 0)
    total = jnp.zeros((2 * rows, LANES), jnp.float32)
    for k, (high, low, flip) in enumerate(places):
        part = jnp.where((wide >> 1) == k, values, 0.0)
        part = part * jnp.where(wide == 2 * k, flip, 1.0)
        part = part + pltpu.roll(part, 4, 0)
        part = part + pltpu.roll(part, 2, 0)
        coarse = part.astype(jnp.bfloat16).astype(jnp.float32)
        spread = []
        for piece in (coarse, part - coarse):
            for at_high in highs:
                spread.append(jnp.where(high == widen(at_high, count), piece, 0.0))
        spread = jnp.concatenate(spread, 0).astype(jnp.bfloat16)
        total = total + lax.dot_general(
            spread, hot_ref[k * count : (k + 1) * count, :], (((1,), (0,)), ((), ())),
            preferred_element_type=jnp.float32,
        )
    return total[:rows] + total[rows:]


def apply_matrix(matrix_ref, live_ref, u):
    y = matrix_ref[0] * u[0:1]
    for j in range(1, 8):
        y = y + matrix_ref[j] * u[j : j + 1]
    return y * live_ref[...].astype(jnp.float32)


def restrict(projection_ref, live_ref, u):
    columns = []
    for at in range(0, u.shape[1], LANES):
        first = at // 2
        a = projection_ref[first : first + 8, :] * u[0:1, at : at + LANES]
        for m in range(1, 8):
            rows = slice(first + 8 * m, first + 8 * m + 8)
            a = a + projection_ref[rows, :] * u[m : m + 1, at : at + LANES]
        columns.append(a)
    a = jnp.concatenate(columns, 1)
    return a * live_ref[...].astype(jnp.float32)


def rim_row(from_left, from_right, rim):
    lane = iota(from_left.shape, 1)
    low = jnp.where(lane < rim, from_right, 0.0)
    return jnp.where((lane >= rim) & (lane < 2 * rim), pltpu.roll(from_left, 64, 1), low)


def arrivals(left, right, rim):
    lane = iota((2, LANES), 1)
    head = jnp.where(lane < rim, left, 0.0)
    return head, jnp.where(lane >= LANES - rim, pltpu.roll(right, 64, 1), 0.0)


def by_side(even_ref, via_odd, via_even):
    even = even_ref[0 : via_odd.shape[0], :] > 0.5
    return jnp.where(even, via_odd, via_even), jnp.where(even, via_even, via_odd)


def load_table(table_ref, edges_ref):
    blocks = edges_ref.shape[1] // LANES
    for h in range(blocks):
        table_ref[2 * h : 2 * h + 2, :] = edges_ref[:, h * LANES : (h + 1) * LANES]
    rest = table_ref.shape[0] - 2 * blocks
    table_ref[2 * blocks :, :] = jnp.zeros((rest, LANES), jnp.float32)


def table_groups(table_ref):
    return [table_ref[8 * g : 8 * g + 8, :] for g in range(table_ref.shape[0] // 8)]


def stage_kernel(rim, count_in, *refs):
    sources, (staged, rest) = refs[:count_in], (refs[count_in : 2 * count_in], refs[2 * count_in :])
    by_moment_ref, y_ref, hot_ref, table_ref, sems = rest
    x_ref, inner_ref, edges_ref, live_ref, matrix_ref, projection_ref = staged[:6]
    copies = [
        pltpu.make_async_copy(source, target, sems.at[i])
        for i, (source, target) in enumerate(zip(sources, staged))
    ]
    for copy in copies:
        copy.start()
    for copy in copies[:4]:
        copy.wait()
    edge_count = x_ref.shape[1]
    count = inner_ref.shape[1]
    load_table(table_ref, x_ref)
    places = edge_places(edges_ref, rim, edge_count + 2 * rim)
    tall = iota((LANES, count), 0)
    for k, (_, low, _) in enumerate(places):
        hot = jnp.transpose(jnp.where(tall == low, 1.0, 0.0))
        hot_ref[k * count : (k + 1) * count, :] = hot.astype(jnp.bfloat16)
    highs = row_highs(edge_count // LANES)
    u = gather_moments(table_groups(table_ref), highs, inner_ref[...], places)
    for copy in copies[4:]:
        copy.wait()
    y_ref[...] = apply_matrix(matrix_ref, live_ref, u)
    by_moment_ref[...] = jnp.zeros(by_moment_ref.shape, jnp.float32)
    for n in range(projection_ref.shape[0]):
        for at in range(0, count, LANES):
            rows = pl.ds(at // 2 + n, 8, stride=8)
            by_moment_ref[rows, :] = projection_ref[n, :, at : at + LANES]


def residual_kernel(
    rim, even_ref, via_odd_ref, via_even_ref, own_ref, b_ref, w_ref, edges_ref, live_ref,
    matrix_ref, hot_ref, y_ref, ends_ref, odd_ref, even_out_ref,
):
    edge_count = b_ref.shape[1]
    blocks = edge_count // LANES
    count = own_ref.shape[1]
    tail = slice(edge_count - LANES, edge_count)
    left, _ = by_side(even_ref, via_odd_ref[:, tail], via_even_ref[:, tail])
    _, right = by_side(even_ref, via_odd_ref[:, :LANES], via_even_ref[:, :LANES])
    none = jnp.zeros((2, LANES), jnp.float32)
    change = jnp.concatenate([none, none, rim_row(left, right, rim), none], 0)
    places = edge_places(edges_ref, rim, edge_count + 2 * rim)
    highs = end_highs(blocks)
    u = gather_moments([change], highs, jnp.zeros((2, count), jnp.float32), places)
    y = own_ref[...] + apply_matrix(matrix_ref, live_ref, u)
    y_ref[...] = y
    ends = scatter_moments(y, places, hot_ref, highs)
    ends_ref[...] = ends
    to_left = jnp.concatenate([ends[0:2], ends[4:6], b_ref[:, :LANES], w_ref[:, :LANES]], 0)
    to_right = jnp.concatenate([ends[2:4], ends[4:6], b_ref[:, tail], w_ref[:, tail]], 0)
    odd_ref[...], even_out_ref[...] = by_side(even_ref, to_left, to_right)


def spread_lists(lists_ref, nodes_ref):
    peers = nodes_ref.shape[0]
    cap = lists_ref.shape[0] * LANES // peers
    period = math.lcm(cap, LANES) // cap
    rows = period * cap // LANES
    lane = iota((peers // period, LANES), 1)
    for d in range(period):
        row, shift = divmod(d * cap, LANES)
        back = (LANES - shift) % LANES
        found = lists_ref[pl.ds(row, peers // period, stride=rows), :]
        if shift:
            found = pltpu.roll(found, back, 1)
        if shift + cap > LANES:
            more = lists_ref[pl.ds(row + 1, peers // period, stride=rows), :]
            found = jnp.where(lane < back, found, pltpu.roll(more, back, 1))
        nodes_ref[pl.ds(d, peers // period, stride=period), :] = found


def partial_kernel(
    rim, y_ref, b_ref, b_inner_ref, edges_ref, live_ref, projection_ref, hot_ref, lists_ref,
    inverse_ref, r_ref, r_inner_ref, a_ref, slots_ref, parts_ref, nodes_ref,
):
    edge_count = b_ref.shape[1]
    blocks = edge_count // LANES
    places = edge_places(edges_ref, rim, edge_count + 2 * rim)
    highs = row_highs(blocks)
    load_table(r_ref, b_ref)
    total = scatter_moments(y_ref[...], places, hot_ref, highs)
    row = iota(total.shape, 0)
    r_ref[...] = r_ref[...] - jnp.where(row < 2 * blocks, total, 0.0)
    r_inner = b_inner_ref[...] - y_ref[6:8, :]
    r_inner_ref[...] = r_inner
    u = gather_moments(table_groups(r_ref), highs, r_inner, places)
    a_ref[...] = restrict(projection_ref, live_ref, u)
    spread_lists(lists_ref, nodes_ref)
    place = nodes_ref[...] & (LANES - 1)
    tall = iota((LANES, LANES), 0)
    for d in range(nodes_ref.shape[0]):
        hot = jnp.transpose(jnp.where(tall == place[d : d + 1], 1.0, 0.0))
        slots_ref[d * LANES : (d + 1) * LANES, :] = hot.astype(jnp.bfloat16)
    size = inverse_ref.shape[1]
    for b in range(inverse_ref.shape[0]):
        coarse = inverse_ref[b].astype(jnp.bfloat16)
        fine = (inverse_ref[b] - coarse.astype(jnp.float32)).astype(jnp.bfloat16)
        parts_ref[:size, b * size : (b + 1) * size] = coarse
        parts_ref[size:, b * size : (b + 1) * size] = fine


def restrict_kernel(
    rim, edge_count, even_ref, via_odd_ref, via_even_ref, ends_ref, exists_ref, part_ref, a_ref,
    edges_ref, live_ref, projection_ref, counts_ref, r_ref, s_rim_ref, packed_ref, vals_ref,
):
    blocks = edge_count // LANES
    count = a_ref.shape[1]
    left, right = by_side(even_ref, via_odd_ref[...], via_even_ref[...])
    head, tail = arrivals(left[2:4], right[2:4], rim)
    exists = exists_ref[...]
    settled = ends_ref[4:6, :] + rim_row(left[0:2], right[0:2], rim)
    r_rim = exists * (rim_row(left[4:6], right[4:6], rim) - settled)
    change = jnp.concatenate([-head, -tail, r_rim, jnp.zeros((2, LANES), jnp.float32)], 0)
    s_rim_ref[...] = rim_row(left[6:8], right[6:8], rim) * r_rim
    places = edge_places(edges_ref, rim, edge_count + 2 * rim)
    u = gather_moments(
        [change], end_highs(blocks), jnp.zeros((2, count), jnp.float32), places
    )
    a = a_ref[...] + restrict(projection_ref, live_ref, u)
    for k in range(3):
        vals_ref[:, k * count : (k + 1) * count] = a[2 * k : 2 * k + 2]
    vals_ref[:, 3 * count :] = jnp.zeros((2, LANES), jnp.float32)
    lane = iota((2, LANES), 1)
    start = jnp.int32(0)
    for q in range(packed_ref.shape[0]):
        amount = counts_ref[0, q]
        shift = start & (LANES - 1)
        base = pl.multiple_of(start - shift, LANES)
        back = (LANES - shift) & (LANES - 1)
        first = pltpu.roll(vals_ref[:, pl.ds(base, LANES)], back, 1)
        second = pltpu.roll(vals_ref[:, pl.ds(base + LANES, LANES)], back, 1)
        chosen = jnp.where(lane < LANES - shift, first, second)
        packed_ref[q] = jnp.where(lane < amount, chosen, 0.0)
        start = start + amount
    r_ref[...] = part_ref[...]
    last = 2 * blocks - 2
    r_ref[0:2, :] = r_ref[0:2, :] - head
    r_ref[last : last + 2, :] = r_ref[last : last + 2, :] - tail


def solve_kernel(arrived_ref, nodes_ref, slots_ref, parts_ref, out_ref):
    peers, agg = nodes_ref.shape[0], parts_ref.shape[0] // 4
    groups = parts_ref.shape[1] // (2 * agg)
    row = iota((8, LANES), 0)
    half = nodes_ref[...] >> 7
    total = jnp.zeros((8, LANES), jnp.float32)
    span = 16
    for first in range(0, peers, span):
        spread = []
        for d in range(first, first + span):
            value = jnp.where(
                (row & 2) == 0,
                jnp.broadcast_to(arrived_ref[2 * d : 2 * d + 1, :], (8, LANES)),
                jnp.broadcast_to(arrived_ref[2 * d + 1 : 2 * d + 2, :], (8, LANES)),
            )
            value = jnp.where((row & 1) == half[d : d + 1], value, 0.0)
            coarse = value.astype(jnp.bfloat16).astype(jnp.float32)
            spread.append(jnp.where(row < 4, coarse, value - coarse))
        total = total + lax.dot_general(
            jnp.concatenate(spread, 1).astype(jnp.bfloat16),
            slots_ref[first * LANES : (first + span) * LANES, :],
            (((1,), (0,)), ((), ())), preferred_element_type=jnp.float32,
        )
    g = total + pltpu.roll(total, 4, 0)
    other = pltpu.roll(g, 2, 0)
    low = iota((8, LANES), 1) < agg
    evens = jnp.where(low, g, pltpu.roll(other, agg, 1))
    odds = jnp.where(low, pltpu.roll(g, agg, 1), other)
    vectors = jnp.where(row < 2, evens, pltpu.roll(odds, 2, 0))
    coarse = vectors.astype(jnp.bfloat16).astype(jnp.float32)
    fine = vectors - coarse
    sides = jnp.concatenate(
        [jnp.concatenate([coarse, coarse], 1), jnp.concatenate([fine, jnp.zeros_like(fine)], 1)], 0
    ).astype(jnp.bfloat16)
    solved = lax.dot_general(
        sides, parts_ref[...], (((1,), (0,)), ((), ())), preferred_element_type=jnp.float32
    )
    solved = solved[:8] + solved[8:]
    tables = [
        jnp.broadcast_to(solved[at : at + 1, b * LANES : (b + 1) * LANES], (8, LANES))
        for b, at in enumerate((0, 2, 1, 3)[:groups])
    ]
    for first in range(0, peers, 8):
        here = nodes_ref[first : first + 8, :]
        owner, place = here >> 6, here & (agg - 1)
        for c in range(2):
            found = jnp.zeros((8, LANES), jnp.float32)
            for b in range(groups):
                picked = jnp.take_along_axis(tables[b], place + c * agg, axis=1)
                found = jnp.where(owner == b, picked, found)
            out_ref[pl.ds(2 * first + c, 8, stride=2), :] = found


def prolong_kernel(
    rim, edge_count, even_ref, returned_ref, edges_ref, live_ref, projection_ref, counts_ref,
    hot_ref, p_ref, ends_ref, odd_ref, even_out_ref, vals_ref,
):
    count = live_ref.shape[1]
    lane = iota((2, LANES), 1)
    start = jnp.int32(0)
    for q in range(returned_ref.shape[0]):
        shift = start & (LANES - 1)
        base = pl.multiple_of(start - shift, LANES)
        moved = pltpu.roll(returned_ref[q], shift, 1)
        here = pl.ds(base, LANES)
        pltpu.store(vals_ref.at[:, here], moved, mask=lane >= shift)
        vals_ref[:, pl.ds(base + LANES, LANES)] = moved
        start = start + counts_ref[0, q]
    nodal = jnp.concatenate([vals_ref[:, k * count : (k + 1) * count] for k in range(3)], 0)
    p = projection_ref[0] * nodal[0:1]
    for n in range(1, 6):
        p = p + projection_ref[n] * nodal[n : n + 1]
    p = p * live_ref[...].astype(jnp.float32)
    p_ref[...] = p
    places = edge_places(edges_ref, rim, edge_count + 2 * rim)
    ends = scatter_moments(p, places, hot_ref, end_highs(edge_count // LANES))
    ends_ref[...] = ends
    to_left = jnp.concatenate([ends[0:2], ends[4:6]], 0)
    to_right = jnp.concatenate([ends[2:4], ends[4:6]], 0)
    odd_ref[...], even_out_ref[...] = by_side(even_ref, to_left, to_right)


def smooth_kernel(
    rim, p_ref, r_ref, r_inner_ref, w_ref, w_inner_ref, edges_ref, live_ref, matrix_ref, hot_ref,
    z_ref, z_inner_ref, y_ref,
):
    edge_count = w_ref.shape[1]
    blocks = edge_count // LANES
    places = edge_places(edges_ref, rim, edge_count + 2 * rim)
    highs = row_highs(blocks)
    total = scatter_moments(p_ref[...], places, hot_ref, highs)
    row = iota(total.shape, 0)
    load_table(z_ref, w_ref)
    z_ref[...] = z_ref[...] * r_ref[...] + jnp.where(row < 2 * blocks, total, 0.0)
    z_inner = w_inner_ref[...] * r_inner_ref[...] + p_ref[6:8, :]
    z_inner_ref[...] = z_inner
    u = gather_moments(table_groups(z_ref), highs, z_inner, places)
    y_ref[...] = apply_matrix(matrix_ref, live_ref, u)


def update_kernel(
    rim, edge_count, even_ref, via_odd_ref, via_even_ref, ends_ref, exists_ref, s_rim_ref,
    part_ref, edges_ref, live_ref, matrix_ref, hot_ref, y_ref, change_ref, odd_ref, even_out_ref,
):
    count = part_ref.shape[1]
    left, right = by_side(even_ref, via_odd_ref[...], via_even_ref[...])
    head, tail = arrivals(left[2:4], right[2:4], rim)
    settled = ends_ref[4:6, :] + rim_row(left[0:2], right[0:2], rim)
    z_rim = s_rim_ref[...] + exists_ref[...] * settled
    change = jnp.concatenate([head, tail, z_rim, jnp.zeros((2, LANES), jnp.float32)], 0)
    change_ref[...] = change
    places = edge_places(edges_ref, rim, edge_count + 2 * rim)
    highs = end_highs(edge_count // LANES)
    u = gather_moments([change], highs, jnp.zeros((2, count), jnp.float32), places)
    y = part_ref[...] + apply_matrix(matrix_ref, live_ref, u)
    y_ref[...] = y
    rims = scatter_moments(y, places, hot_ref, highs)[4:6]
    odd_ref[...] = rims
    even_out_ref[...] = rims


def output_kernel(
    rim, y_ref, change_ref, z_ref, z_inner_ref, r_ref, r_inner_ref, x_ref, inner_ref, edges_ref,
    hot_ref, x1_ref, x1_inner_ref, r1_ref, r1_inner_ref,
):
    edge_count = x_ref.shape[1]
    blocks = edge_count // LANES
    places = edge_places(edges_ref, rim, edge_count + 2 * rim)
    total = scatter_moments(y_ref[...], places, hot_ref, row_highs(blocks))
    x1_inner_ref[...] = inner_ref[...] + z_inner_ref[...]
    r1_inner_ref[...] = r_inner_ref[...] - y_ref[6:8, :]
    for h in range(blocks):
        here = slice(h * LANES, (h + 1) * LANES)
        rows = slice(2 * h, 2 * h + 2)
        z = z_ref[rows, :]
        if h == 0:
            z = z + change_ref[0:2, :]
        if h == blocks - 1:
            z = z + change_ref[2:4, :]
        x1_ref[:, here] = x_ref[:, here] + z
        r1_ref[:, here] = r_ref[rows, :] - total[rows]


def finish_kernel(rim, even_ref, part_ref, via_odd_ref, via_even_ref, r1_ref):
    edge_count = part_ref.shape[1]
    left, right = by_side(even_ref, via_odd_ref[...], via_even_ref[...])
    head, tail = arrivals(left, right, rim)
    last = slice(edge_count - LANES, edge_count)
    r1_ref[...] = part_ref[...]
    r1_ref[:, :LANES] = part_ref[:, :LANES] - head
    r1_ref[:, last] = part_ref[:, last] - tail


def local_call(kernel, outs, in_place=False, scratch=(), sems=0, name=None):
    def call(*args):
        spaces = [pltpu.HBM if in_place else pltpu.VMEM] * len(args)
        shapes = [
            jax.ShapeDtypeStruct(*(o if isinstance(o[0], tuple) else (o, jnp.float32)))
            for o in outs
        ]
        extra = [pltpu.SemaphoreType.DMA((sems,))] if sems else []
        return pl.pallas_call(
            kernel,
            out_shape=shapes,
            in_specs=[pl.BlockSpec(memory_space=space) for space in spaces],
            out_specs=[pl.BlockSpec(memory_space=pltpu.VMEM)] * len(outs),
            scratch_shapes=[pltpu.VMEM(s, jnp.float32) for s in scratch] + extra,
            compiler_params=pltpu.CompilerParams(vmem_limit_bytes=VMEM_LIMIT),
            cost_estimate=pl.CostEstimate(
                flops=10**8, bytes_accessed=2 * 10**6, transcendentals=0
            ),
            name=name,
        )(*args)

    return call


def swap(odd, even):
    axis = ("grp", "dom")
    count = lax.axis_size(axis)

    def pairs(first):
        lows = range(first, count - 1, 2)
        return [(i, i + 1) for i in lows] + [(i + 1, i) for i in lows]

    via_even = lax.ppermute(even, axis, pairs(0))
    return lax.ppermute(odd, axis, pairs(1)), via_even


def shards(
    x_edges,
    x_inner,
    b_edges,
    b_inner,
    w_edges,
    w_inner,
    elem_edges,
    element_live,
    elem_matrix,
    projection,
    owner_counts,
    aux_node,
    aux_inverse,
):
    edge_count = x_edges.shape[1]
    elem_count = x_inner.shape[1]
    rim = elem_count // 32
    peers = owner_counts.shape[1]
    rows = -(-2 * (edge_count // LANES + 1) // 8) * 8
    live = element_live.reshape(1, elem_count)
    strip = lax.axis_index(("grp", "dom"))
    even = jnp.where(strip % 2 == 0, jnp.ones((8, LANES), jnp.float32), 0.0)
    lane = iota((2, LANES), 1)
    is_last = strip == lax.axis_size(("grp", "dom")) - 1
    exists = jnp.where(lane < rim, jnp.where(is_last, 0.0, 1.0), jnp.where(strip == 0, 0.0, 1.0))
    exists = jnp.where(lane < 2 * rim, exists, 0.0)
    via_odd, via_even = swap(x_edges, x_edges)
    table = (rows, LANES)
    group = (8, LANES)
    inner = (2, elem_count)
    moments = (8, elem_count)
    slots = (peers, 2, LANES)
    hots = ((3 * elem_count, LANES), jnp.bfloat16)
    lists = (2, 3 * elem_count + LANES)

    arguments = (
        x_edges, x_inner, elem_edges, live, elem_matrix, jnp.transpose(projection, (1, 0, 2)),
        b_edges, b_inner, w_edges, w_inner, aux_inverse, owner_counts,
        aux_node.reshape(-1, LANES),
    )
    *staged, by_moment, own, hot = local_call(
        functools.partial(stage_kernel, rim, len(arguments)),
        [(v.shape, v.dtype) for v in arguments] + [(elem_count // 2, LANES), moments, hots],
        in_place=True, scratch=[table], sems=len(arguments), name="stage",
    )(*[pltpu.with_memory_space_constraint(v, pltpu.HBM) for v in arguments])
    x_edges, x_inner, elem_edges, live, elem_matrix, nodal_first = staged[:6]
    b_edges, b_inner, w_edges, w_inner, aux_inverse, owner_counts, aux_node = staged[6:]
    y, ends, odd_out, even_out = local_call(
        functools.partial(residual_kernel, rim), [moments, group, group, group], name="residual"
    )(
        even, via_odd, via_even, own, b_edges, w_edges, elem_edges, live, elem_matrix, hot
    )
    via_odd, via_even = swap(odd_out, even_out)
    size = aux_inverse.shape[1]
    r, r_inner, a, slots_hot, parts, nodes = local_call(
        functools.partial(partial_kernel, rim),
        [
            table, inner, moments, ((peers * LANES, LANES), jnp.bfloat16),
            ((2 * size, aux_inverse.shape[0] * size), jnp.bfloat16), ((peers, LANES), jnp.int32),
        ],
        name="partial",
    )(
        y, b_edges, b_inner, elem_edges, live, by_moment, hot, aux_node, aux_inverse
    )
    r, s_rim, packed = local_call(
        functools.partial(restrict_kernel, rim, edge_count), [table, (2, LANES), slots],
        scratch=[lists], name="restrict",
    )(
        even, via_odd, via_even, ends, exists, r, a, elem_edges, live, by_moment, owner_counts
    )
    arrived = lax.all_to_all(packed, "dom", split_axis=0, concat_axis=0, tiled=True)
    (outgoing,) = local_call(solve_kernel, [(2 * peers, LANES)], name="solve")(
        arrived.reshape(2 * peers, LANES), nodes, slots_hot, parts
    )
    outgoing = outgoing.reshape(slots)
    returned = lax.all_to_all(outgoing, "dom", split_axis=0, concat_axis=0, tiled=True)
    p, ends, odd_out, even_out = local_call(
        functools.partial(prolong_kernel, rim, edge_count),
        [moments, group, (4, LANES), (4, LANES)], scratch=[lists], name="prolong",
    )(even, returned, elem_edges, live, nodal_first, owner_counts, hot)
    via_odd, via_even = swap(odd_out, even_out)
    z, z_inner, az = local_call(
        functools.partial(smooth_kernel, rim), [table, inner, moments], name="smooth"
    )(p, r, r_inner, w_edges, w_inner, elem_edges, live, elem_matrix, hot)
    az, change, odd_out, even_out = local_call(
        functools.partial(update_kernel, rim, edge_count),
        [moments, group, (2, LANES), (2, LANES)], name="update",
    )(
        even, via_odd, via_even, ends, exists, s_rim, az, elem_edges, live, elem_matrix, hot
    )
    via_odd, via_even = swap(odd_out, even_out)
    x1_edges, x1_inner, r1_part, r1_inner = local_call(
        functools.partial(output_kernel, rim), [x_edges.shape, inner, x_edges.shape, inner],
        name="output",
    )(az, change, z, z_inner, r, r_inner, x_edges, x_inner, elem_edges, hot)
    (r1_edges,) = local_call(
        functools.partial(finish_kernel, rim), [x_edges.shape], name="finish"
    )(even, r1_part, via_odd, via_even)
    return x1_edges, x1_inner, r1_edges, r1_inner


def solution(mesh):
    edges = P(None, ("grp", "dom"))
    in_specs = (edges,) * 7 + (
        P(("grp", "dom")),
        P(None, None, ("grp", "dom")),
        P(None, None, ("grp", "dom")),
        P(("grp", "dom"), None),
        P(("grp", "dom")),
        P(("grp", "dom"), None, None),
    )
    return jax.shard_map(
        shards, mesh=mesh, in_specs=in_specs, out_specs=(edges,) * 4, check_vma=False
    )
```
